32 devices in a mesh: dp: 8 (over z, x), ctx: 4 (over y, core).
Axes of the slice: x: 2, y: 2, z: 4, core: 2. Of those that a mesh axis runs over, the one named last changes fastest.
Arguments:
- tokens: bfloat16 [16, 1024, 1024], P('dp', 'ctx'), may hold values from -6 to 6
- cotangent: bfloat16 [16, 1024, 1024], P('dp', 'ctx'), may hold values from -6 to 6
- adapter_ids: int32 [16], replicated, may hold values from 0 to 7
- attend_weight: bfloat16 [2, 1024, 3072], P(None, ('dp', 'ctx')), may hold values from -0.1875 to 0.1875
- output_weight: bfloat16 [2, 1024, 1024], P(None, ('dp', 'ctx')), may hold values from -4 to 4
- expand_weight: bfloat16 [2, 1024, 4096], P(None, ('dp', 'ctx')), may hold values from -0.1875 to 0.1875
- reduce_weight: bfloat16 [2, 4096, 1024], P(None, ('dp', 'ctx')), may hold values from -0.09375 to 0.09375
- attend_bias: float32 [2, 2048], replicated, may hold values from -3 to 3
- output_bias: float32 [2, 1024], replicated, may hold values from -3 to 3
- expand_bias: float32 [2, 4096], replicated, may hold values from -3 to 3
- reduce_bias: float32 [2, 1024], replicated, may hold values from -3 to 3
- first_gain: float32 [2, 1024], replicated, may hold values from 0.1 to 1.9
- first_shift: float32 [2, 1024], replicated, may hold values from -3 to 3
- second_gain: float32 [2, 1024], replicated, may hold values from 0.1 to 1.9
- second_shift: float32 [2, 1024], replicated, may hold values from -3 to 3
- attend_left: bfloat16 [2, 8, 1024, 16], P(None, None, ('dp', 'ctx')), may hold values from -0.1875 to 0.1875
- attend_right: bfloat16 [2, 8, 3072, 16], P(None, None, ('dp', 'ctx')), may hold values from -0.75 to 0.75
- output_left: bfloat16 [2, 8, 1024, 16], P(None, None, ('dp', 'ctx')), may hold values from -4 to 4
- output_right: bfloat16 [2, 8, 1024, 16], P(None, None, ('dp', 'ctx')), may hold values from -0.75 to 0.75
- expand_left: bfloat16 [2, 8, 1024, 16], P(None, None, ('dp', 'ctx')), may hold values from -0.1875 to 0.1875
- expand_right: bfloat16 [2, 8, 4096, 16], P(None, None, ('dp', 'ctx')), may hold values from -0.75 to 0.75
- reduce_left: bfloat16 [2, 8, 4096, 16], P(None, None, ('dp', 'ctx')), may hold values from -0.09375 to 0.09375
- reduce_right: bfloat16 [2, 8, 1024, 16], P(None, None, ('dp', 'ctx')), may hold values from -0.75 to 0.75
Outputs:
- output: bfloat16 [16, 1024, 1024], P('dp', 'ctx')
- input_grad: float32 [16, 1024, 1024], P('dp', 'ctx')
- attend_left_grad: float32 [2, 8, 1024, 16], P(None, None, ('dp', 'ctx'))
- attend_right_grad: float32 [2, 8, 3072, 16], P(None, None, ('dp', 'ctx'))
- output_left_grad: float32 [2, 8, 1024, 16], P(None, None, ('dp', 'ctx'))
- output_right_grad: float32 [2, 8, 1024, 16], P(None, None, ('dp', 'ctx'))
- expand_left_grad: float32 [2, 8, 1024, 16], P(None, None, ('dp', 'ctx'))
- expand_right_grad: float32 [2, 8, 4096, 16], P(None, None, ('dp', 'ctx'))
- reduce_left_grad: float32 [2, 8, 4096, 16], P(None, None, ('dp', 'ctx'))
- reduce_right_grad: float32 [2, 8, 1024, 16], P(None, None, ('dp', 'ctx'))
The draws below stay inside these ranges and needn't reach their ends.
Inputs may be any that keep to these rules, and one draw needn't show every extreme that they name: adapter_ids[s] is the adapter that sequence s uses in every layer.
All inputs are finite; a program needn't handle non-finite values.
Results may differ from the reference program's by a relative error of at most 0.018.
Values may be sent and summed in bfloat16 or wider, within the bound.
No kernel may reach another device: no remote copies, remote signals or barrier semaphores. Data moves between devices by JAX's collectives and lax.ppermute only.
A program may use at most 384 MiB of HBM per device.

```python
import jax
import jax.numpy as jnp
from jax import lax

D = 1024
HEADS = 16
HEAD_DIM = 64
FF = 4096
RANK = 16
ADAPTERS = 8
LAYERS = 2
BLK = 256
SEQ = 1024
NSEQ = 16


def with_ends(array, rng, least, top_value):
    longest = array.shape.index(max(array.shape))
    spots = []
    for shift in (0, 1):
        where = [jax.random.randint(jax.random.fold_in(rng, axis), (), 0, length) for axis, length in enumerate(array.shape)]
        where[longest] = (where[longest] + shift) % array.shape[longest]
        spots.append(tuple(where))
    return array.at[spots[0]].set(least).at[spots[1]].set(top_value)


def steps_of(stream_key, extent, shards, low, top_value):
    level, own = 1.0, jax.random.fold_in(stream_key, 6)
    for axis_at, parts in shards:
        heights = jnp.exp(jax.random.uniform(jax.random.fold_in(own, axis_at), (parts,), jnp.float32, low / len(shards), top_value / len(shards)))
        level = level * jnp.repeat(heights, extent[axis_at] // parts).reshape([-1 if axis == axis_at else 1 for axis in range(len(extent))])
    return level


def normal_values(stream_key, dims, scale, most, cuts=(), held_as=jnp.bfloat16):
    values = scale * jax.random.normal(stream_key, dims, jnp.float32)
    if cuts:
        values = values * steps_of(stream_key, dims, cuts, -0.22, 0.18)
    return jnp.clip(values, -most, most).astype(held_as)


def setup_inputs(seed: int = 0) -> dict:
    seeds = jax.random.split(jax.random.key(seed), 24)
    tokens = normal_values(seeds[0], (NSEQ, SEQ, D), 1.0, 6.0, ((0, 8), (1, 4)))
    cotangent = normal_values(seeds[1], (NSEQ, SEQ, D), 1.0, 6.0, ((0, 8), (1, 4)))
    adapter_ids = with_ends(jax.random.randint(seeds[2], (NSEQ,), 0, ADAPTERS), jax.random.fold_in(seeds[2], 1), 0, ADAPTERS - 1).astype(jnp.int32)
    attend_weight = normal_values(seeds[3], (LAYERS, D, 3 * D), D ** -0.5, 0.1875, ((1, 32),))
    output_weight = normal_values(seeds[4], (LAYERS, D, D), (max(1, 2 * D // SEQ)) ** -0.5, 4.0, ((1, 32),))
    expand_weight = normal_values(seeds[5], (LAYERS, D, FF), D ** -0.5, 0.1875, ((1, 32),))
    reduce_weight = normal_values(seeds[6], (LAYERS, FF, D), FF ** -0.5, 0.09375, ((1, 32),))
    attend_bias = normal_values(seeds[7], (LAYERS, 2 * D), 0.5, 3.0, (), jnp.float32)
    output_bias = normal_values(seeds[8], (LAYERS, D), 0.5, 3.0, (), jnp.float32)
    expand_bias = normal_values(seeds[9], (LAYERS, FF), 0.5, 3.0, (), jnp.float32)
    reduce_bias = normal_values(seeds[10], (LAYERS, D), 0.5, 3.0, (), jnp.float32)
    first_gain = jnp.clip(1.0 + 0.18 * jax.random.normal(seeds[11], (LAYERS, D), jnp.float32), 0.1, 1.9)
    first_shift = normal_values(seeds[12], (LAYERS, D), 0.5, 3.0, (), jnp.float32)
    second_gain = jnp.clip(1.0 + 0.18 * jax.random.normal(seeds[13], (LAYERS, D), jnp.float32), 0.1, 1.9)
    second_shift = normal_values(seeds[14], (LAYERS, D), 0.5, 3.0, (), jnp.float32)
    attend_left = normal_values(seeds[15], (LAYERS, ADAPTERS, D, RANK), D ** -0.5, 0.1875, ((2, 32),))
    attend_right = normal_values(seeds[16], (LAYERS, ADAPTERS, 3 * D, RANK), (4 * RANK) ** -0.5, 0.75, ((2, 32),))
    output_left = normal_values(seeds[17], (LAYERS, ADAPTERS, D, RANK), (max(1, 2 * D // SEQ)) ** -0.5, 4.0, ((2, 32),))
    output_right = normal_values(seeds[18], (LAYERS, ADAPTERS, D, RANK), (4 * RANK) ** -0.5, 0.75, ((2, 32),))
    expand_left = normal_values(seeds[19], (LAYERS, ADAPTERS, D, RANK), D ** -0.5, 0.1875, ((2, 32),))
    expand_right = normal_values(seeds[20], (LAYERS, ADAPTERS, FF, RANK), (4 * RANK) ** -0.5, 0.75, ((2, 32),))
    reduce_left = normal_values(seeds[21], (LAYERS, ADAPTERS, FF, RANK), FF ** -0.5, 0.09375, ((2, 32),))
    reduce_right = normal_values(seeds[22], (LAYERS, ADAPTERS, D, RANK), (4 * RANK) ** -0.5, 0.75, ((2, 32),))
    return {"tokens": tokens, "cotangent": cotangent, "adapter_ids": adapter_ids, "attend_weight": attend_weight, "output_weight": output_weight, "expand_weight": expand_weight, "reduce_weight": reduce_weight, "attend_bias": attend_bias, "output_bias": output_bias, "expand_bias": expand_bias, "reduce_bias": reduce_bias, "first_gain": first_gain, "first_shift": first_shift, "second_gain": second_gain, "second_shift": second_shift, "attend_left": attend_left, "attend_right": attend_right, "output_left": output_left, "output_right": output_right, "expand_left": expand_left, "expand_right": expand_right, "reduce_left": reduce_left, "reduce_right": reduce_right}


epsilon = 1e-05
masked_score = -1e+30
root_factor = 0.7978845608028654
highest = lax.Precision.HIGHEST

@jax.custom_vjp
def low(v):
    return lax.optimization_barrier(v.astype(jnp.bfloat16)).astype(jnp.float32)

@jax.custom_vjp
def low_back(v):
    return v

def low_keep(v):
    return (low(v), None)

def low_pass(kept, grad):
    return (grad,)

def back_keep(v):
    return (v, None)

def back_low(kept, grad):
    return (low(grad),)
low.defvjp(low_keep, low_pass)
low_back.defvjp(back_keep, back_low)

def normalize(values, gain_vector, shift_vector):
    center = lax.optimization_barrier(jnp.mean(values, axis=-1, keepdims=True))
    spread = values - center
    variance = lax.optimization_barrier(jnp.mean(spread * spread, axis=-1, keepdims=True))
    return spread * lax.rsqrt(variance + epsilon) * gain_vector + shift_vector

def gelu_tanh(values):
    return 0.5 * values * (1.0 + jnp.tanh(root_factor * (values + 0.044715 * values * values * values)))

def product(left_side, right_side):
    return jnp.dot(left_side, right_side, precision=highest)

def adapted(inputs, weight, left_factor, right_factor):
    low_rank = low(low_back(product(inputs, left_factor)))
    rank_term = lax.dot_general(low_rank, right_factor, (((1,), (1,)), ((), ())), precision=highest)
    return product(inputs, weight) + rank_term

def attention(queries, key_rows, value_rows):
    length = queries.shape[0]
    block_rows = min(512, length)
    query_heads = queries.reshape(length, HEADS, HEAD_DIM)
    key_heads = key_rows.reshape(length, HEADS, HEAD_DIM)
    value_heads = value_rows.reshape(length, HEADS, HEAD_DIM)
    key_block = jnp.arange(length, dtype=jnp.int32) // BLK

    def one_block(offset):
        query_part = lax.dynamic_slice_in_dim(query_heads, offset, block_rows, 0)
        scores = jnp.einsum('qhd,khd->hqk', query_part, key_heads, precision=highest) * HEAD_DIM ** (-0.5)
        scores = low_back(scores)
        query_block = (offset + jnp.arange(block_rows, dtype=jnp.int32)) // BLK
        visible = key_block[None, :] <= query_block[:, None]
        scores = jnp.where(visible[None], scores, masked_score)
        row_peak = lax.optimization_barrier(jnp.max(scores, axis=-1, keepdims=True))
        weights = jnp.exp(scores - row_peak)
        weights = weights / lax.optimization_barrier(jnp.sum(weights, axis=-1, keepdims=True))
        mixed_heads = jnp.einsum('hqk,khd->qhd', low(weights), value_heads, precision=highest)
        return mixed_heads.reshape(block_rows, HEADS * HEAD_DIM)
    starts = jnp.arange(length // block_rows, dtype=jnp.int32) * block_rows
    return lax.map(jax.checkpoint(one_block), starts).reshape(length, HEADS * HEAD_DIM)

def layer(current, weights, picked, extras):
    attend_weight, output_weight, expand_weight, reduce_weight = weights
    attend_left, attend_right, output_left, output_right, expand_left, expand_right, reduce_left, reduce_right = picked
    attend_bias, output_bias, expand_bias, reduce_bias, first_gain, first_shift, second_gain, second_shift = extras
    columns = current.shape[1]
    normed_one = low(normalize(current, first_gain, first_shift))
    bias_full = jnp.concatenate([attend_bias[:columns], jnp.zeros((columns,), attend_bias.dtype), attend_bias[columns:]])
    joined_rows = low(low_back(adapted(normed_one, attend_weight, attend_left, attend_right) + bias_full))
    attended = low(low_back(attention(joined_rows[:, :columns], joined_rows[:, columns:2 * columns], joined_rows[:, 2 * columns:])))
    middle = current + low_back(adapted(attended, output_weight, output_left, output_right) + output_bias)
    normed_two = low(normalize(middle, second_gain, second_shift))
    expanded = low_back(adapted(normed_two, expand_weight, expand_left, expand_right) + expand_bias)
    active = low(gelu_tanh(expanded))
    return middle + low_back(adapted(active, reduce_weight, reduce_left, reduce_right) + reduce_bias)

def reference(tokens, cotangent, adapter_ids, attend_weight, output_weight, expand_weight, reduce_weight, attend_bias, output_bias, expand_bias, reduce_bias, first_gain, first_shift, second_gain, second_shift, attend_left, attend_right, output_left, output_right, expand_left, expand_right, reduce_left, reduce_right):
    frozen = tuple((member.astype(jnp.float32) for member in (attend_weight, output_weight, expand_weight, reduce_weight)))
    fixed_set = tuple((member.astype(jnp.float32) for member in (attend_bias, output_bias, expand_bias, reduce_bias, first_gain, first_shift, second_gain, second_shift)))
    adapters = tuple((member.astype(jnp.float32) for member in (attend_left, attend_right, output_left, output_right, expand_left, expand_right, reduce_left, reduce_right)))

    def network(current, adapter_set, adapter_pick):
        for layer_index in range(LAYERS):
            picked = tuple((member[layer_index, adapter_pick] for member in adapter_set))
            weights = tuple((member[layer_index] for member in frozen))
            extras = tuple((member[layer_index] for member in fixed_set))
            current = layer(current, weights, picked, extras)
        return current

    def sequence_step(totals, inputs):
        seq_tokens, seq_cotangent, adapter_pick = inputs

        def forward(current, adapter_set):
            return network(current, adapter_set, adapter_pick)
        result, pullback = jax.vjp(forward, seq_tokens.astype(jnp.float32), adapters)
        grad_tokens, grad_adapters = pullback(seq_cotangent.astype(jnp.float32))
        totals = tuple((running + grad_term for running, grad_term in zip(totals, grad_adapters)))
        return (totals, (result.astype(jnp.bfloat16), grad_tokens))
    start_totals = tuple((jnp.zeros_like(member) for member in adapters))
    totals, (outputs, input_grads) = lax.scan(sequence_step, start_totals, (tokens, cotangent, adapter_ids))
    return (outputs, input_grads, totals[0], totals[1], totals[2], totals[3], totals[4], totals[5], totals[6], totals[7])
```

```python
import functools

import jax
import jax.numpy as jnp
from jax import lax
from jax.experimental import pallas as pl
from jax.experimental.pallas import tpu as pltpu
from jax.sharding import Mesh
from jax.sharding import PartitionSpec as P

HEADS = 16
HEAD_DIM = 64
RANK = 16
ADAPTERS = 8
LAYERS = 2
BLK = 256

epsilon = 1e-05
root_factor = 0.7978845608028654
low_type = jnp.bfloat16
wide = jnp.float32

ROWS_BY_ROWS = (((1,), (1,)), ((), ()))
COLS_BY_COLS = (((0,), (0,)), ((), ()))
PLAIN = (((1,), (0,)), ((), ()))
EVERY = ("dp", "chip", "core")
LANE = ("dp", "chip")
CTX = ("chip", "core")


def times(left_side, right_side, dims=PLAIN):
    return lax.dot_general(left_side, right_side, dims, preferred_element_type=wide)


def normalize(values, gain_vector, shift_vector):
    center = jnp.mean(values, axis=-1, keepdims=True)
    spread = values - center
    variance = jnp.mean(spread * spread, axis=-1, keepdims=True)
    return spread * lax.rsqrt(variance + epsilon) * gain_vector + shift_vector


def gelu_tanh(values):
    return (
        0.5
        * values
        * (1.0 + jnp.tanh(root_factor * (values + 0.044715 * values * values * values)))
    )


def block_pair(step, place, blocks):
    half = blocks // 2
    late = step > place
    slot = jnp.where(late, 1, 0)
    key_block = jnp.where(late, step - place - 1, step)
    owner = jnp.where(key_block < half, key_block, blocks - 1 - key_block)
    owner_slot = jnp.where(key_block < half, 0, 1)
    piece = lax.rem(place - owner + half, half)
    return slot, pl.multiple_of((piece * 2 + owner_slot) * BLK, BLK)


def stack_heads(rows, mask):
    zero = jnp.zeros_like(rows)
    return jnp.concatenate([jnp.where(mask, rows, zero), jnp.where(mask, zero, rows)], axis=0)


def attend_forward_kernel(blocks, place_ref, q_ref, k_ref, v_ref, o_ref, stat_ref, queries, scores, total):
    place = place_ref[0]
    mask = lax.broadcasted_iota(jnp.int32, (BLK, 2 * HEAD_DIM), 1) < HEAD_DIM
    for slot in range(2):
        queries[slot] = stack_heads(q_ref[slot * BLK : (slot + 1) * BLK, :] * HEAD_DIM**-0.5, mask)
    steps = [block_pair(step, place, blocks) for step in range(blocks + 1)]
    peaks = [jnp.full((1, 2 * BLK), -1e30, wide)] * 2
    for step, (slot, row) in enumerate(steps):
        block = times(k_ref[pl.ds(row, BLK), :], queries[slot], ROWS_BY_ROWS)
        scores[step] = block
        top = jnp.max(block, axis=0, keepdims=True)
        peaks = [
            jnp.where(slot == which, jnp.maximum(peaks[which], top), peaks[which])
            for which in range(2)
        ]
    total[...] = jnp.zeros_like(total)
    sums = [jnp.zeros((1, 2 * BLK), wide)] * 2
    for step, (slot, row) in enumerate(steps):
        weights = jnp.exp(scores[step] - jnp.where(slot == 0, peaks[0], peaks[1]))
        part = jnp.sum(weights, axis=0, keepdims=True)
        sums = [sums[which] + jnp.where(slot == which, part, 0.0) for which in range(2)]
        weights = weights.astype(low_type)
        turned = v_ref[pl.ds(row, BLK), :].T
        total[slot] = total[slot] + jnp.concatenate(
            [
                times(turned[:HEAD_DIM], weights[:, :BLK]),
                times(turned[HEAD_DIM:], weights[:, BLK:]),
            ],
            axis=0,
        )
    for slot in range(2):
        share = 1.0 / sums[slot]
        held = total[slot]
        held = jnp.concatenate(
            [held[:HEAD_DIM] * share[:, :BLK], held[HEAD_DIM:] * share[:, BLK:]], axis=0
        )
        o_ref[slot * BLK : (slot + 1) * BLK, :] = held.T
        stat_ref[0, slot : slot + 1, :] = peaks[slot] + jnp.log(sums[slot])


def attend_backward_kernel(
    blocks, place_ref, q_ref, k_ref, v_ref, g_ref, o_ref, stat_ref,
    dq_ref, dk_ref, dv_ref, queries, grads, key_sum, value_sum, query_sum, inner,
):
    place = place_ref[0]
    mask = lax.broadcasted_iota(jnp.int32, (BLK, 2 * HEAD_DIM), 1) < HEAD_DIM
    for slot in range(2):
        rows = slice(slot * BLK, (slot + 1) * BLK)
        queries[slot] = stack_heads(q_ref[rows, :] * HEAD_DIM**-0.5, mask)
        grad = g_ref[rows, :]
        grads[slot] = stack_heads(grad, mask)
        both = (grad.astype(wide) * o_ref[rows, :]).T
        inner[slot] = jnp.concatenate(
            [
                jnp.sum(both[:HEAD_DIM], axis=0, keepdims=True),
                jnp.sum(both[HEAD_DIM:], axis=0, keepdims=True),
            ],
            axis=1,
        )
    key_sum[...] = jnp.zeros_like(key_sum)
    value_sum[...] = jnp.zeros_like(value_sum)
    query_sum[...] = jnp.zeros_like(query_sum)
    for step in range(blocks + 1):
        slot, row = block_pair(step, place, blocks)
        at = pl.ds(row, BLK)
        keys, values = k_ref[at, :], v_ref[at, :]
        own, grad = queries[slot], grads[slot]
        probs = jnp.exp(times(keys, own, ROWS_BY_ROWS) - stat_ref[0, pl.ds(slot, 1), :])
        dscores = probs * (times(values, grad, ROWS_BY_ROWS) - inner[slot])
        dscores = dscores.astype(low_type)
        value_sum[at, :] = value_sum[at, :] + times(probs.astype(low_type), grad)
        key_sum[at, :] = key_sum[at, :] + times(dscores, own)
        turned = keys.T
        query_sum[slot] = query_sum[slot] + jnp.concatenate(
            [
                times(turned[:HEAD_DIM], dscores[:, :BLK]),
                times(turned[HEAD_DIM:], dscores[:, BLK:]),
            ],
            axis=0,
        )
    for slot in range(2):
        dq_ref[slot * BLK : (slot + 1) * BLK, :] = (query_sum[slot].T * HEAD_DIM**-0.5).astype(
            low_type
        )
    dk_ref[...] = key_sum[...].astype(low_type)
    dv_ref[...] = value_sum[...].astype(low_type)


def attention_specs(blocks):
    own = pl.BlockSpec((2 * BLK, 2 * HEAD_DIM), lambda pair, place: (0, pair))
    every = pl.BlockSpec((blocks * BLK, 2 * HEAD_DIM), lambda pair, place: (0, pair))
    stats = pl.BlockSpec((1, 2, 2 * BLK), lambda pair, place: (pair, 0, 0))
    return own, every, stats


def attend_forward(place, queries, keys, values):
    blocks, columns = keys.shape[0] // BLK, queries.shape[1]
    pairs = columns // (2 * HEAD_DIM)
    own, every, stats = attention_specs(blocks)
    return pl.pallas_call(
        functools.partial(attend_forward_kernel, blocks),
        out_shape=(
            jax.ShapeDtypeStruct(queries.shape, wide),
            jax.ShapeDtypeStruct((pairs, 2, 2 * BLK), wide),
        ),
        grid_spec=pltpu.PrefetchScalarGridSpec(
            num_scalar_prefetch=1,
            grid=(pairs,),
            in_specs=[own, every, every],
            out_specs=[own, stats],
            scratch_shapes=[
                pltpu.VMEM((2, 2 * BLK, 2 * HEAD_DIM), low_type),
                pltpu.VMEM((blocks + 1, BLK, 2 * BLK), wide),
                pltpu.VMEM((2, 2 * HEAD_DIM, BLK), wide),
            ],
        ),
        compiler_params=pltpu.CompilerParams(vmem_limit_bytes=48 * 2**20),
        name="attend_forward",
    )(place, queries, keys, values)


def attend_backward(place, queries, keys, values, grads, attended, stat):
    blocks, columns = keys.shape[0] // BLK, queries.shape[1]
    pairs = columns // (2 * HEAD_DIM)
    own, every, stats = attention_specs(blocks)
    return pl.pallas_call(
        functools.partial(attend_backward_kernel, blocks),
        out_shape=(
            jax.ShapeDtypeStruct(queries.shape, low_type),
            jax.ShapeDtypeStruct(keys.shape, low_type),
            jax.ShapeDtypeStruct(keys.shape, low_type),
        ),
        grid_spec=pltpu.PrefetchScalarGridSpec(
            num_scalar_prefetch=1,
            grid=(pairs,),
            in_specs=[own, every, every, own, own, stats],
            out_specs=[own, every, every],
            scratch_shapes=[
                pltpu.VMEM((2, 2 * BLK, 2 * HEAD_DIM), low_type),
                pltpu.VMEM((2, 2 * BLK, 2 * HEAD_DIM), low_type),
                pltpu.VMEM((blocks * BLK, 2 * HEAD_DIM), wide),
                pltpu.VMEM((blocks * BLK, 2 * HEAD_DIM), wide),
                pltpu.VMEM((2, 2 * HEAD_DIM, BLK), wide),
                pltpu.VMEM((2, 1, 2 * BLK), wide),
            ],
        ),
        compiler_params=pltpu.CompilerParams(vmem_limit_bytes=48 * 2**20),
        name="attend_backward",
    )(place, queries, keys, values, grads, attended, stat)


def spread_tokens(pair, below, count):
    half = count // 2
    across = [(b, half + b if b < half else count - 1 - b) for b in range(count)]
    inside = [(b, half + count - 1 - b) for b in range(half, count)]
    got = lax.ppermute(jnp.where(below, pair[1], pair[0]), CTX, across)
    other = lax.ppermute(pair[1], CTX, inside)
    return jnp.concatenate(
        [jnp.where(below, pair[0], got), jnp.where(below, got, other)], axis=0
    )


def collect_tokens(rows, below, count):
    half = count // 2
    across = [(half + b if b < half else count - 1 - b, b) for b in range(count)]
    inside = [(half + count - 1 - b, b) for b in range(half, count)]
    early, late = rows[:BLK], rows[BLK:]
    got = lax.ppermute(jnp.where(below, late, early), CTX, across)
    other = lax.ppermute(late, CTX, inside)
    return jnp.stack([jnp.where(below, early, got), jnp.where(below, got, other)])


def ring_gather(rows, count):
    half = count // 2
    pieces = [rows]
    for step in range(1, half):
        pairs = [
            (side * half + b, side * half + (b + step) % half)
            for side in range(2)
            for b in range(half)
        ]
        pieces.append(lax.ppermute(rows, CTX, pairs))
    return jnp.concatenate(pieces, axis=0)


def ring_scatter(rows, count):
    half = count // 2
    size = rows.shape[0] // half
    total = rows[:size].astype(wide)
    for step in range(1, half):
        pairs = [
            (side * half + b, side * half + (b - step) % half)
            for side in range(2)
            for b in range(half)
        ]
        part = rows[step * size : (step + 1) * size]
        total = total + lax.ppermute(part, CTX, pairs).astype(wide)
    return total


def layer_forward(current, frozen, picked, extras, place, count):
    attend_weight, output_weight, expand_weight, reduce_weight = frozen
    (
        attend_left, attend_right, output_left, output_right,
        expand_left, expand_right, reduce_left, reduce_right,
    ) = picked
    (
        attend_bias, output_bias, expand_bias, reduce_bias,
        first_gain, first_shift, second_gain, second_shift,
    ) = extras
    columns = current.shape[1]
    normed_one = normalize(current, first_gain, first_shift).astype(low_type)
    rank_attend = times(normed_one, attend_left, ROWS_BY_ROWS).astype(low_type)
    biases = [attend_bias[:columns], jnp.zeros((columns,), wide), attend_bias[columns:]]
    queries, keys, values = (
        (
            times(normed_one, attend_weight[part])
            + times(rank_attend, attend_right[:, part * columns : (part + 1) * columns])
            + biases[part]
        ).astype(low_type)
        for part in range(3)
    )
    key_all, value_all = ring_gather(keys, count), ring_gather(values, count)
    attended, stat = attend_forward(place, queries, key_all, value_all)
    attended_low = attended.astype(low_type)
    rank_output = times(attended_low, output_left, ROWS_BY_ROWS).astype(low_type)
    middle = (
        current + times(attended_low, output_weight) + times(rank_output, output_right) + output_bias
    )
    normed_two = normalize(middle, second_gain, second_shift).astype(low_type)
    rank_expand = times(normed_two, expand_left, ROWS_BY_ROWS).astype(low_type)
    parts = len(expand_weight)
    expanded = [
        times(normed_two, expand_weight[part])
        + times(rank_expand, expand_right[:, part * columns : (part + 1) * columns])
        + expand_bias[part * columns : (part + 1) * columns]
        for part in range(parts)
    ]
    active = [gelu_tanh(member).astype(low_type) for member in expanded]
    rank_reduce = sum(
        times(active[part], reduce_left[:, part * columns : (part + 1) * columns], ROWS_BY_ROWS)
        for part in range(parts)
    ).astype(low_type)
    result = (
        middle
        + sum(times(active[part], reduce_weight[part]) for part in range(parts))
        + times(rank_reduce, reduce_right)
        + reduce_bias
    )
    kept = (
        current, normed_one, rank_attend, queries, key_all, value_all, attended, attended_low, stat,
        rank_output, middle, normed_two, rank_expand, expanded, active, rank_reduce,
    )
    return result, kept


def layer_backward(grad_result, kept, frozen, picked, extras, place, count):
    attend_weight, output_weight, expand_weight, reduce_weight = frozen
    (
        attend_left, attend_right, output_left, output_right,
        expand_left, expand_right, reduce_left, reduce_right,
    ) = picked
    first_gain, first_shift, second_gain, second_shift = extras[4:]
    (
        current, normed_one, rank_attend, queries, key_all, value_all, attended, attended_low, stat,
        rank_output, middle, normed_two, rank_expand, expanded, active, rank_reduce,
    ) = kept
    columns = current.shape[1]
    parts = len(expand_weight)

    def piece(member, part):
        return member[:, part * columns : (part + 1) * columns]

    grad_reduce = grad_result.astype(low_type)
    turn_reduce = times(grad_reduce, reduce_right, ROWS_BY_ROWS).astype(low_type)
    grad_expand = []
    for part in range(parts):
        grad_active = times(grad_reduce, reduce_weight[part], ROWS_BY_ROWS) + times(
            turn_reduce, piece(reduce_left, part)
        )
        grad_expand.append(jax.vjp(gelu_tanh, expanded[part])[1](grad_active)[0].astype(low_type))
    reduce_left_g = jnp.concatenate(
        [times(turn_reduce, active[part], COLS_BY_COLS) for part in range(parts)], axis=1
    )
    reduce_right_g = times(rank_reduce, grad_reduce, COLS_BY_COLS)
    turn_expand = sum(
        times(grad_expand[part], piece(expand_right, part), ROWS_BY_ROWS) for part in range(parts)
    ).astype(low_type)
    grad_second = sum(
        times(grad_expand[part], expand_weight[part], ROWS_BY_ROWS) for part in range(parts)
    ) + times(turn_expand, expand_left)
    expand_left_g = times(turn_expand, normed_two, COLS_BY_COLS)
    expand_right_g = jnp.concatenate(
        [times(rank_expand, grad_expand[part], COLS_BY_COLS) for part in range(parts)], axis=1
    )
    pull = jax.vjp(lambda rows: normalize(rows, second_gain, second_shift), middle)[1]
    grad_middle = grad_result + pull(grad_second)[0]
    grad_project = grad_middle.astype(low_type)
    turn_output = times(grad_project, output_right, ROWS_BY_ROWS).astype(low_type)
    grad_attended = (
        times(grad_project, output_weight, ROWS_BY_ROWS) + times(turn_output, output_left)
    ).astype(low_type)
    output_left_g = times(turn_output, attended_low, COLS_BY_COLS)
    output_right_g = times(rank_output, grad_project, COLS_BY_COLS)
    grad_query, grad_keys, grad_values = attend_backward(
        place, queries, key_all, value_all, grad_attended, attended, stat
    )
    joined = (
        grad_query,
        ring_scatter(grad_keys, count).astype(low_type),
        ring_scatter(grad_values, count).astype(low_type),
    )
    turn_attend = sum(
        times(joined[part], piece(attend_right, part), ROWS_BY_ROWS) for part in range(3)
    ).astype(low_type)
    grad_first = sum(
        times(joined[part], attend_weight[part], ROWS_BY_ROWS) for part in range(3)
    ) + times(turn_attend, attend_left)
    attend_left_g = times(turn_attend, normed_one, COLS_BY_COLS)
    attend_right_g = jnp.concatenate(
        [times(rank_attend, joined[part], COLS_BY_COLS) for part in range(3)], axis=1
    )
    pull = jax.vjp(lambda rows: normalize(rows, first_gain, first_shift), current)[1]
    grad_current = grad_middle + pull(grad_first)[0]
    return grad_current, (
        attend_left_g, attend_right_g, output_left_g, output_right_g,
        expand_left_g, expand_right_g, reduce_left_g, reduce_right_g,
    )


def local(
    tokens, cotangent, adapter_ids, attend_weight, output_weight, expand_weight, reduce_weight,
    attend_bias, output_bias, expand_bias, reduce_bias, first_gain, first_shift, second_gain, second_shift,
    *adapters,
):
    data_count, chips = lax.axis_size("dp"), lax.axis_size("chip")
    count = chips * lax.axis_size("core")
    half = count // 2
    devices = data_count * count
    data_rank, core = lax.axis_index("dp"), lax.axis_index("core")
    rank = lax.axis_index("chip") * 2 + core
    below = rank < half
    place = jnp.reshape(lax.rem(rank, half), (1,)).astype(jnp.int32)
    columns = tokens.shape[2]

    lane_chip = jnp.arange(data_count * chips, dtype=jnp.int32)
    lane_sequence = (lane_chip // chips) * 2 + (lane_chip % chips) // (chips // 2)
    lane_adapter = jnp.take(adapter_ids, lane_sequence)

    current = spread_tokens(tokens, below, count).astype(wide)
    grad_current = spread_tokens(cotangent, below, count).astype(wide)

    sizes = [member.shape[2] for member in adapters]
    packed = jnp.concatenate([jnp.swapaxes(member, 2, 3) for member in adapters], axis=3)
    chosen = jnp.moveaxis(jnp.take(packed, lane_adapter, axis=1), 1, 0)
    mine = lax.all_to_all(chosen, LANE, split_axis=0, concat_axis=0, tiled=True)
    theirs = lax.ppermute(mine, "core", [(0, 1), (1, 0)])
    both = jnp.stack(
        [jnp.where(core == 0, mine, theirs), jnp.where(core == 0, theirs, mine)], axis=1
    )

    def factors(layer_index):
        found, first = [], 0
        for size in sizes:
            part = both[:, :, layer_index, :, first : first + size]
            found.append(jnp.transpose(part, (2, 0, 1, 3)).reshape(RANK, devices * size))
            first += size
        return tuple(found)

    def shards(layer_index):
        lists = [attend_weight[layer_index], output_weight[layer_index], expand_weight[layer_index]]
        blocks = [
            member[:, first : first + columns]
            for member in lists
            for first in range(0, member.shape[1], columns)
        ]
        return jnp.concatenate(blocks + [reduce_weight[layer_index]], axis=0)

    def frozen_of(whole):
        rows = columns // devices
        blocks = [
            whole[:, part * rows : (part + 1) * rows, :].reshape(columns, columns)
            for part in range(8)
        ]
        members = devices // 4
        reduce_blocks = [
            whole[part * members : (part + 1) * members, 8 * rows :, :].reshape(columns, columns)
            for part in range(4)
        ]
        return blocks[:3], blocks[3], blocks[4:8], reduce_blocks

    extras = [
        tuple(
            member[layer_index]
            for member in (
                attend_bias, output_bias, expand_bias, reduce_bias,
                first_gain, first_shift, second_gain, second_shift,
            )
        )
        for layer_index in range(LAYERS)
    ]
    gathered = [
        lax.all_gather(shards(layer_index), EVERY, axis=0) for layer_index in range(LAYERS)
    ]
    frozen = [frozen_of(member) for member in gathered]
    picked = [factors(layer_index) for layer_index in range(LAYERS)]
    kept = []
    for layer_index in range(LAYERS):
        current, keep = layer_forward(
            current, frozen[layer_index], picked[layer_index], extras[layer_index], place, count
        )
        kept.append(keep)

    owner_adapter = (lane_adapter[:, None] == jnp.arange(ADAPTERS)[None, :]).astype(wide)
    summed = [None] * LAYERS
    for layer_index in reversed(range(LAYERS)):
        grad_current, terms = layer_backward(
            grad_current,
            kept[layer_index],
            frozen[layer_index],
            picked[layer_index],
            extras[layer_index],
            place,
            count,
        )
        owned = jnp.concatenate(
            [
                jnp.transpose(
                    term.astype(low_type).reshape(RANK, data_count * chips, 2, size), (2, 1, 0, 3)
                )
                for term, size in zip(terms, sizes)
            ],
            axis=3,
        )
        sent = lax.ppermute(jnp.where(core == 0, owned[1], owned[0]), "core", [(0, 1), (1, 0)])
        total = jnp.where(core == 0, owned[0], owned[1]).astype(wide) + sent.astype(wide)
        received = lax.all_to_all(
            total.astype(low_type), LANE, split_axis=0, concat_axis=0, tiled=True
        )
        summed[layer_index] = jnp.einsum(
            "sa,srp->arp", owner_adapter, received.astype(wide), precision=lax.Precision.HIGHEST
        )
    results, first = [], 0
    for size in sizes:
        member = jnp.stack([layer[:, :, first : first + size] for layer in summed])
        results.append(jnp.swapaxes(member, 2, 3))
        first += size
    outputs = collect_tokens(current.astype(low_type), below, count)
    early_late = grad_current
    moved = collect_tokens(early_late, below, count)
    return (outputs, moved, *results)


def solution(mesh):
    count = mesh.shape["ctx"]
    inner = Mesh(mesh.devices.reshape(mesh.shape["dp"], count // 2, 2), EVERY)
    token_spec, factor_spec = P("dp", CTX, None), P(None, None, EVERY, None)
    in_specs = (
        (token_spec,) * 2 + (P(),) + (P(None, EVERY, None),) * 4 + (P(),) * 8 + (factor_spec,) * 8
    )
    out_specs = (token_spec,) * 2 + (factor_spec,) * 8
    return jax.shard_map(local, mesh=inner, in_specs=in_specs, out_specs=out_specs, check_vma=False)
```

```python
import functools

import jax
import jax.numpy as jnp
from jax import lax
from jax.experimental import pallas as pl
from jax.experimental.pallas import tpu as pltpu
from jax.sharding import Mesh
from jax.sharding import PartitionSpec as P

HEADS = 16
HEAD_DIM = 64
RANK = 16
ADAPTERS = 8
LAYERS = 2
BLK = 256

epsilon = 1e-05
root_factor = 0.7978845608028654
low_type = jnp.bfloat16
wide = jnp.float32

ROWS_BY_ROWS = (((1,), (1,)), ((), ()))
COLS_BY_COLS = (((0,), (0,)), ((), ()))
PLAIN = (((1,), (0,)), ((), ()))
EVERY = ("dp", "chip", "core")
LANE = ("dp", "chip")
CTX = ("chip", "core")


def times(left_side, right_side, dims=PLAIN):
    return lax.dot_general(left_side, right_side, dims, preferred_element_type=wide)


def block_pair(step, place, blocks):
    half = blocks // 2
    late = step > place
    slot = jnp.where(late, 1, 0)
    key_block = jnp.where(late, step - place - 1, step)
    owner = jnp.where(key_block < half, key_block, blocks - 1 - key_block)
    owner_slot = jnp.where(key_block < half, 0, 1)
    piece = lax.rem(place - owner + half, half)
    return slot, pl.multiple_of((piece * 2 + owner_slot) * BLK, BLK)


def stack_heads(rows, mask):
    zero = jnp.zeros_like(rows)
    return jnp.concatenate([jnp.where(mask, rows, zero), jnp.where(mask, zero, rows)], axis=0)


def attend_forward_kernel(blocks, place_ref, q_ref, k_ref, v_ref, o_ref, stat_ref, queries, scores, total):
    place = place_ref[0]
    mask = lax.broadcasted_iota(jnp.int32, (BLK, 2 * HEAD_DIM), 1) < HEAD_DIM
    for slot in range(2):
        queries[slot] = stack_heads(q_ref[slot * BLK : (slot + 1) * BLK, :] * HEAD_DIM**-0.5, mask)
    steps = [block_pair(step, place, blocks) for step in range(blocks + 1)]
    peaks = [jnp.full((1, 2 * BLK), -1e30, wide)] * 2
    for step, (slot, row) in enumerate(steps):
        block = times(k_ref[pl.ds(row, BLK), :], queries[slot], ROWS_BY_ROWS)
        scores[step] = block
        top = jnp.max(block, axis=0, keepdims=True)
        peaks = [
            jnp.where(slot == which, jnp.maximum(peaks[which], top), peaks[which])
            for which in range(2)
        ]
    total[...] = jnp.zeros_like(total)
    sums = [jnp.zeros((1, 2 * BLK), wide)] * 2
    for step, (slot, row) in enumerate(steps):
        weights = jnp.exp(scores[step] - jnp.where(slot == 0, peaks[0], peaks[1]))
        part = jnp.sum(weights, axis=0, keepdims=True)
        sums = [sums[which] + jnp.where(slot == which, part, 0.0) for which in range(2)]
        weights = weights.astype(low_type)
        turned = v_ref[pl.ds(row, BLK), :].T
        total[slot] = total[slot] + jnp.concatenate(
            [
                times(turned[:HEAD_DIM], weights[:, :BLK]),
                times(turned[HEAD_DIM:], weights[:, BLK:]),
            ],
            axis=0,
        )
    for slot in range(2):
        share = 1.0 / sums[slot]
        held = total[slot]
        held = jnp.concatenate(
            [held[:HEAD_DIM] * share[:, :BLK], held[HEAD_DIM:] * share[:, BLK:]], axis=0
        )
        o_ref[slot * BLK : (slot + 1) * BLK, :] = held.T
        stat_ref[0, slot : slot + 1, :] = peaks[slot] + jnp.log(sums[slot])


def attend_backward_kernel(
    blocks, place_ref, q_ref, k_ref, v_ref, g_ref, o_ref, stat_ref,
    dq_ref, dk_ref, dv_ref, queries, grads, key_sum, value_sum, query_sum, inner,
):
    place = place_ref[0]
    mask = lax.broadcasted_iota(jnp.int32, (BLK, 2 * HEAD_DIM), 1) < HEAD_DIM
    for slot in range(2):
        rows = slice(slot * BLK, (slot + 1) * BLK)
        queries[slot] = stack_heads(q_ref[rows, :] * HEAD_DIM**-0.5, mask)
        grad = g_ref[rows, :]
        grads[slot] = stack_heads(grad, mask)
        both = (grad.astype(wide) * o_ref[rows, :]).T
        inner[slot] = jnp.concatenate(
            [
                jnp.sum(both[:HEAD_DIM], axis=0, keepdims=True),
                jnp.sum(both[HEAD_DIM:], axis=0, keepdims=True),
            ],
            axis=1,
        )
    key_sum[...] = jnp.zeros_like(key_sum)
    value_sum[...] = jnp.zeros_like(value_sum)
    query_sum[...] = jnp.zeros_like(query_sum)
    for step in range(blocks + 1):
        slot, row = block_pair(step, place, blocks)
        at = pl.ds(row, BLK)
        keys, values = k_ref[at, :], v_ref[at, :]
        own, grad = queries[slot], grads[slot]
        probs = jnp.exp(times(keys, own, ROWS_BY_ROWS) - stat_ref[0, pl.ds(slot, 1), :])
        dscores = probs * (times(values, grad, ROWS_BY_ROWS) - inner[slot])
        dscores = dscores.astype(low_type)
        value_sum[at, :] = value_sum[at, :] + times(probs.astype(low_type), grad)
        key_sum[at, :] = key_sum[at, :] + times(dscores, own)
        turned = keys.T
        query_sum[slot] = query_sum[slot] + jnp.concatenate(
            [
                times(turned[:HEAD_DIM], dscores[:, :BLK]),
                times(turned[HEAD_DIM:], dscores[:, BLK:]),
            ],
            axis=0,
        )
    for slot in range(2):
        dq_ref[slot * BLK : (slot + 1) * BLK, :] = (query_sum[slot].T * HEAD_DIM**-0.5).astype(
            low_type
        )
    dk_ref[...] = key_sum[...].astype(low_type)
    dv_ref[...] = value_sum[...].astype(low_type)


def attention_specs(blocks):
    own = pl.BlockSpec((2 * BLK, 2 * HEAD_DIM), lambda pair, place: (0, pair))
    every = pl.BlockSpec((blocks * BLK, 2 * HEAD_DIM), lambda pair, place: (0, pair))
    stats = pl.BlockSpec((1, 2, 2 * BLK), lambda pair, place: (pair, 0, 0))
    return own, every, stats


def attend_forward(place, queries, keys, values):
    blocks, columns = keys.shape[0] // BLK, queries.shape[1]
    pairs = columns // (2 * HEAD_DIM)
    own, every, stats = attention_specs(blocks)
    return pl.pallas_call(
        functools.partial(attend_forward_kernel, blocks),
        out_shape=(
            jax.ShapeDtypeStruct(queries.shape, wide),
            jax.ShapeDtypeStruct((pairs, 2, 2 * BLK), wide),
        ),
        grid_spec=pltpu.PrefetchScalarGridSpec(
            num_scalar_prefetch=1,
            grid=(pairs,),
            in_specs=[own, every, every],
            out_specs=[own, stats],
            scratch_shapes=[
                pltpu.VMEM((2, 2 * BLK, 2 * HEAD_DIM), low_type),
                pltpu.VMEM((blocks + 1, BLK, 2 * BLK), wide),
                pltpu.VMEM((2, 2 * HEAD_DIM, BLK), wide),
            ],
        ),
        compiler_params=pltpu.CompilerParams(vmem_limit_bytes=48 * 2**20),
        name="attend_forward",
    )(place, queries, keys, values)


def attend_backward(place, queries, keys, values, grads, attended, stat):
    blocks, columns = keys.shape[0] // BLK, queries.shape[1]
    pairs = columns // (2 * HEAD_DIM)
    own, every, stats = attention_specs(blocks)
    return pl.pallas_call(
        functools.partial(attend_backward_kernel, blocks),
        out_shape=(
            jax.ShapeDtypeStruct(queries.shape, low_type),
            jax.ShapeDtypeStruct(keys.shape, low_type),
            jax.ShapeDtypeStruct(keys.shape, low_type),
        ),
        grid_spec=pltpu.PrefetchScalarGridSpec(
            num_scalar_prefetch=1,
            grid=(pairs,),
            in_specs=[own, every, every, own, own, stats],
            out_specs=[own, every, every],
            scratch_shapes=[
                pltpu.VMEM((2, 2 * BLK, 2 * HEAD_DIM), low_type),
                pltpu.VMEM((2, 2 * BLK, 2 * HEAD_DIM), low_type),
                pltpu.VMEM((blocks * BLK, 2 * HEAD_DIM), wide),
                pltpu.VMEM((blocks * BLK, 2 * HEAD_DIM), wide),
                pltpu.VMEM((2, 2 * HEAD_DIM, BLK), wide),
                pltpu.VMEM((2, 1, 2 * BLK), wide),
            ],
        ),
        compiler_params=pltpu.CompilerParams(vmem_limit_bytes=48 * 2**20),
        name="attend_backward",
    )(place, queries, keys, values, grads, attended, stat)


def spread_tokens(pair, below, count):
    half = count // 2
    across = [(b, half + b if b < half else count - 1 - b) for b in range(count)]
    inside = [(b, half + count - 1 - b) for b in range(half, count)]
    got = lax.ppermute(jnp.where(below, pair[1], pair[0]), CTX, across)
    other = lax.ppermute(pair[1], CTX, inside)
    return jnp.concatenate(
        [jnp.where(below, pair[0], got), jnp.where(below, got, other)], axis=0
    )


def collect_tokens(rows, below, count):
    half = count // 2
    across = [(half + b if b < half else count - 1 - b, b) for b in range(count)]
    inside = [(half + count - 1 - b, b) for b in range(half, count)]
    early, late = rows[:BLK], rows[BLK:]
    got = lax.ppermute(jnp.where(below, late, early), CTX, across)
    other = lax.ppermute(late, CTX, inside)
    return jnp.stack([jnp.where(below, early, got), jnp.where(below, got, other)])


def ring_gather(rows, count):
    half = count // 2
    pieces = [rows]
    for step in range(1, half):
        pairs = [
            (side * half + b, side * half + (b + step) % half)
            for side in range(2)
            for b in range(half)
        ]
        pieces.append(lax.ppermute(rows, CTX, pairs))
    return jnp.concatenate(pieces, axis=0)


def ring_scatter(rows, count):
    half = count // 2
    size = rows.shape[0] // half
    total = rows[:size].astype(wide)
    for step in range(1, half):
        pairs = [
            (side * half + b, side * half + (b - step) % half)
            for side in range(2)
            for b in range(half)
        ]
        part = rows[step * size : (step + 1) * size]
        total = total + lax.ppermute(part, CTX, pairs).astype(wide)
    return total


def ring_position(z):
    return jnp.where(z == 2, 3, jnp.where(z == 3, 2, z))


SWAP = [(0, 1), (1, 0)]
RING = [(z * 2 + x, after * 2 + x) for z, after in enumerate((1, 3, 0, 2)) for x in range(2)]
ACROSS_X = [(d, d ^ 1) for d in range(8)]


def along_z(rows):
    return lax.ppermute(rows, "dp", RING)


def along_x(rows):
    return lax.ppermute(rows, "dp", ACROSS_X)


def along_y(rows):
    return lax.ppermute(rows, "chip", SWAP)


def on_chip(rows):
    return lax.ppermute(rows, "core", SWAP)


def join(*members):
    return jnp.concatenate(members, axis=0)


def after(members, earlier):
    return lax.optimization_barrier(tuple(members) + tuple(earlier))[: len(members)]


def over_z(rows):
    members = [rows]
    for _ in range(3):
        members.append(along_z(members[-1]))
    return members


def by_z(ring, first, rows, position):
    parts = [member[first : first + rows] for member in ring]
    placed = []
    for spot in (0, 1, 3, 2):
        step = lax.rem(position + 4 - spot, 4)
        chosen = parts[3]
        for index in (2, 1, 0):
            chosen = jnp.where(step == index, parts[index], chosen)
        placed.append(chosen)
    return jnp.stack(placed)


def gather_chunks(plan, position):
    started = []
    for rows, z_first in plan:
        if not z_first:
            size = rows.shape[0] // 2
            one, two = rows[:size], rows[size:]
            rows = join(one, along_x(one), two, along_y(two))
        started.append(rows)
    rings = []
    for rows in started:
        rings.append(over_z(after((rows,), rings[-1][3:])[0] if rings else rows))
    found, far = [], ()
    for ring, (rows, z_first) in zip(rings, plan):
        size = ring[0].shape[0] // 2
        near = [by_z(ring, part * size, size, position) for part in range(2)]
        if z_first:
            near = after(near, far)
            near = [
                jnp.stack([near[0], along_x(near[0])]),
                jnp.stack([near[1], along_y(near[1])]),
            ]
        else:
            near = [member.reshape(4, 2, size // 2, member.shape[2]) for member in near]
        near = after(near, far)
        far = (along_y(near[0]), along_x(near[1]))
        own = [near[0], far[0], near[1], far[1]]
        found.append(tuple(own + [on_chip(member) for member in own]))
    return found


SQUARE = (4, 2, 2, 2, 32, 1024)
TALL = (4, 2, 2, 2, 128, 1024)
QKVO_UNITS = ((0, 0), (0, 32), (1, 0), (1, 32))
EXPAND_UNITS = ((0, 0), (0, 32), (0, 64), (0, 96))
REDUCE_UNIT = (1, 0)


def fetch(form, at_ref, sources, unit, rows, held, arrived, by_quarter=None):
    if form == "whole":
        source = sources[unit]
        if by_quarter is None:
            pltpu.make_async_copy(source, held, arrived).start()
        else:
            pltpu.make_async_copy(source.at[by_quarter], held.at[by_quarter], arrived).start()
        return
    part, first = unit
    x, y, core = at_ref[1], at_ref[2], at_ref[3]
    spread_z = slice(None) if by_quarter is None else by_quarter
    for other in range(2):
        for far in range(2):
            source = sources[other * 4 + part * 2 + far]
            for over in range(2):
                over_x, over_y = (over, far) if part == 0 else (far, over)
                where = (over, spread_z) if form == "z first" else (spread_z, over)
                pltpu.make_async_copy(
                    source.at[(*where, pl.ds(first, rows), slice(None))],
                    held.at[
                        spread_z,
                        lax.rem(x + over_x, 2),
                        lax.rem(y + over_y, 2),
                        lax.rem(core + other, 2),
                    ],
                    arrived,
                ).start()


def wait_for(held, arrived):
    pltpu.make_async_copy(held, held, arrived).wait()


def square(held):
    return held[...].reshape(1024, 1024)


TILE = 256
STRIP = 32
COLUMNS = 1024


def strips(count, body):
    def step(index, carry):
        body(pl.ds(pl.multiple_of(index * STRIP, STRIP), STRIP))
        return carry

    lax.fori_loop(0, count // STRIP, step, 0)


def normalize_rows(values, gain, shift):
    center = jnp.mean(values, axis=-1, keepdims=True)
    spread = values - center
    scale = lax.rsqrt(jnp.mean(spread * spread, axis=-1, keepdims=True) + epsilon)
    unit = spread * scale
    return unit, scale, unit * gain + shift


def normalize_pull(grad, unit, scale, gain):
    scaled = grad * gain
    first = jnp.mean(scaled, axis=-1, keepdims=True)
    second = jnp.mean(scaled * unit, axis=-1, keepdims=True)
    return scale * (scaled - first - unit * second)


def qkv_kernel(form, at_ref, x_ref, gain_ref, shift_ref, left_ref, right_ref, bias_ref, *refs):
    sources, (normed_ref, unit_ref, scale_ref, rank_ref, *outs) = refs[:-9], refs[-9:-2]
    held, arrived = refs[-2:]
    for part in range(3):
        unit = part if form == "whole" else QKVO_UNITS[part]
        fetch(form, at_ref, sources, unit, 32, held.at[part], arrived.at[part])

    def norm(rows):
        unit, scale, normed = normalize_rows(x_ref[rows, :], gain_ref[...], shift_ref[...])
        normed_ref[rows, :] = normed.astype(low_type)
        unit_ref[rows, :] = unit.astype(low_type)
        scale_ref[rows, :] = jnp.broadcast_to(scale, (STRIP, 128))

    strips(x_ref.shape[0], norm)
    rank_ref[...] = times(normed_ref[...], left_ref[...], ROWS_BY_ROWS).astype(low_type)
    for part, out in enumerate(outs):
        wait_for(held.at[part], arrived.at[part])
        columns = slice(part * COLUMNS, (part + 1) * COLUMNS)
        for first in range(0, x_ref.shape[0], TILE):
            rows = slice(first, first + TILE)
            out[rows, :] = (
                times(normed_ref[rows, :], square(held.at[part]))
                + times(rank_ref[rows, :], right_ref[:, columns])
                + bias_ref[:, columns]
            ).astype(low_type)


def output_kernel(form, at_ref, x_ref, attended_ref, left_ref, right_ref, bias_ref, gain_ref, shift_ref, *refs):
    sources, (low_ref, middle_ref, normed_ref, unit_ref, scale_ref, rank_ref) = refs[:-8], refs[-8:-2]
    held, arrived = refs[-2:]
    fetch(form, at_ref, sources, 3 if form == "whole" else QKVO_UNITS[3], 32, held, arrived)
    low_ref[...] = attended_ref[...].astype(low_type)
    rank_ref[...] = times(low_ref[...], left_ref[...], ROWS_BY_ROWS).astype(low_type)
    wait_for(held, arrived)
    for first in range(0, x_ref.shape[0], TILE):
        rows = slice(first, first + TILE)
        middle_ref[rows, :] = (
            x_ref[rows, :]
            + times(low_ref[rows, :], square(held))
            + times(rank_ref[rows, :], right_ref[...])
            + bias_ref[...]
        )

    def norm(rows):
        unit, scale, normed = normalize_rows(middle_ref[rows, :], gain_ref[...], shift_ref[...])
        normed_ref[rows, :] = normed.astype(low_type)
        unit_ref[rows, :] = unit.astype(low_type)
        scale_ref[rows, :] = jnp.broadcast_to(scale, (STRIP, 128))

    strips(x_ref.shape[0], norm)


def fetch_feed_forward(form, at_ref, sources, expand, reduce, arrived, reduce_first):
    for part in range(4):
        whole = form == "whole"
        jobs = [
            (part if whole else EXPAND_UNITS[part], 32, expand.at[part], arrived.at[0, part], None),
            (4 if whole else REDUCE_UNIT, 128, reduce, arrived.at[1, part], part),
        ]
        for unit, rows, held, semaphore, quarter in jobs[::-1] if reduce_first else jobs:
            fetch(form, at_ref, sources, unit, rows, held, semaphore, quarter)


def feed_forward_kernel(
    form, at_ref, normed_ref, middle_ref, expand_left_ref, expand_right_ref, expand_bias_ref,
    reduce_left_ref, reduce_right_ref, reduce_bias_ref, *refs,
):
    sources, (result_ref, slope_ref, active_ref, rank_expand_ref, rank_reduce_ref) = refs[:-9], refs[-9:-4]
    expand, reduce, rank_sum, arrived = refs[-4:]
    fetch_feed_forward(form, at_ref, sources, expand, reduce, arrived, False)
    count = normed_ref.shape[0]
    rank_expand_ref[...] = times(normed_ref[...], expand_left_ref[...], ROWS_BY_ROWS).astype(low_type)
    result_ref[...] = middle_ref[...] + reduce_bias_ref[...]
    rank_sum[...] = jnp.zeros_like(rank_sum)

    def part_step(part, carry):
        columns = pl.ds(pl.multiple_of(part * COLUMNS, COLUMNS), COLUMNS)
        wait_for(expand.at[part], arrived.at[0, part])
        wait_for(reduce.at[part], arrived.at[1, part])
        for first in range(0, count, TILE):
            rows = slice(first, first + TILE)
            value = (
                times(normed_ref[rows, :], square(expand.at[part]))
                + times(rank_expand_ref[rows, :], expand_right_ref[:, columns])
                + expand_bias_ref[:, columns]
            )
            squared = value * value
            bent = jnp.tanh(root_factor * value * (1.0 + 0.044715 * squared))
            half = 0.5 * (1.0 + bent)
            slope_ref[rows, columns] = (
                half
                + 0.5 * value * (1.0 - bent * bent) * (root_factor + 3 * 0.044715 * root_factor * squared)
            ).astype(low_type)
            active = (value * half).astype(low_type)
            active_ref[rows, columns] = active
            result_ref[rows, :] = result_ref[rows, :] + times(active, square(reduce.at[part]))
            rank_sum[rows, :] = rank_sum[rows, :] + times(
                active, reduce_left_ref[:, columns], ROWS_BY_ROWS
            )
        return carry

    lax.fori_loop(0, 4, part_step, 0)
    rank_reduce_ref[...] = rank_sum[...].astype(low_type)
    result_ref[...] = result_ref[...] + times(rank_reduce_ref[...], reduce_right_ref[...])


def feed_backward_kernel(
    form, at_ref, grad_ref, slope_ref, active_ref, normed_ref, unit_ref, scale_ref, rank_expand_ref, rank_reduce_ref,
    gain_ref, expand_left_ref, expand_right_ref, reduce_left_ref, reduce_right_ref, *refs,
):
    sources, (out_ref, expand_left_g, expand_right_g, reduce_left_g, reduce_right_g) = refs[:-13], refs[-13:-8]
    expand, reduce, arrived, low_grad, turned, bent, total, turn_sum = refs[-8:]
    fetch_feed_forward(form, at_ref, sources, expand, reduce, arrived, True)
    count = grad_ref.shape[0]
    low_grad[...] = grad_ref[...].astype(low_type)
    turned[...] = times(low_grad[...], reduce_right_ref[...], ROWS_BY_ROWS).astype(low_type)
    reduce_right_g[...] = times(rank_reduce_ref[...], low_grad[...], COLS_BY_COLS).astype(low_type)
    total[...] = jnp.zeros_like(total)
    turn_sum[...] = jnp.zeros_like(turn_sum)

    def part_step(part, carry):
        columns = pl.ds(pl.multiple_of(part * COLUMNS, COLUMNS), COLUMNS)
        wait_for(reduce.at[part], arrived.at[1, part])
        wait_for(expand.at[part], arrived.at[0, part])
        for first in range(0, count, TILE):
            rows = slice(first, first + TILE)
            grad_active = times(low_grad[rows, :], square(reduce.at[part]), ROWS_BY_ROWS) + times(
                turned[rows, :], reduce_left_ref[:, columns]
            )
            grad_expand = (grad_active * slope_ref[rows, columns].astype(wide)).astype(low_type)
            bent[rows, :] = grad_expand
            total[rows, :] = total[rows, :] + times(grad_expand, square(expand.at[part]), ROWS_BY_ROWS)
            turn_sum[rows, :] = turn_sum[rows, :] + times(
                grad_expand, expand_right_ref[:, columns], ROWS_BY_ROWS
            )
        reduce_left_g[:, columns] = times(turned[...], active_ref[:, columns], COLS_BY_COLS).astype(
            low_type
        )
        expand_right_g[:, columns] = times(rank_expand_ref[...], bent[...], COLS_BY_COLS).astype(low_type)
        return carry

    lax.fori_loop(0, 4, part_step, 0)
    turned[...] = turn_sum[...].astype(low_type)
    expand_left_g[...] = times(turned[...], normed_ref[...], COLS_BY_COLS).astype(low_type)
    total[...] = total[...] + times(turned[...], expand_left_ref[...])

    def pull(rows):
        out_ref[rows, :] = grad_ref[rows, :] + normalize_pull(
            total[rows, :], unit_ref[rows, :].astype(wide), scale_ref[rows, :1], gain_ref[...]
        )

    strips(count, pull)


def output_backward_kernel(form, at_ref, grad_ref, attended_ref, rank_ref, left_ref, right_ref, *refs):
    sources, (out_ref, left_g, right_g) = refs[:-7], refs[-7:-4]
    held, arrived, low_grad, turned = refs[-4:]
    fetch(form, at_ref, sources, 3 if form == "whole" else QKVO_UNITS[3], 32, held, arrived)
    low_grad[...] = grad_ref[...].astype(low_type)
    turned[...] = times(low_grad[...], right_ref[...], ROWS_BY_ROWS).astype(low_type)
    right_g[...] = times(rank_ref[...], low_grad[...], COLS_BY_COLS).astype(low_type)
    left_g[...] = times(turned[...], attended_ref[...], COLS_BY_COLS).astype(low_type)
    wait_for(held, arrived)
    for first in range(0, grad_ref.shape[0], TILE):
        rows = slice(first, first + TILE)
        out_ref[rows, :] = (
            times(low_grad[rows, :], square(held), ROWS_BY_ROWS) + times(turned[rows, :], left_ref[...])
        ).astype(low_type)


def qkv_backward_kernel(
    form, at_ref, dq_ref, dk_ref, dv_ref, grad_ref, normed_ref, unit_ref, scale_ref, rank_ref,
    gain_ref, left_ref, right_ref, *refs,
):
    sources, (out_ref, left_g, right_g) = refs[:-7], refs[-7:-4]
    held, arrived, turned, total = refs[-4:]
    count = grad_ref.shape[0]
    for part in range(3):
        unit = part if form == "whole" else QKVO_UNITS[part]
        fetch(form, at_ref, sources, unit, 32, held.at[part], arrived.at[part])
    grads = (dq_ref, dk_ref, dv_ref)
    spans = [slice(part * COLUMNS, (part + 1) * COLUMNS) for part in range(3)]
    turned[...] = sum(
        times(grads[part][...], right_ref[:, spans[part]], ROWS_BY_ROWS) for part in range(3)
    ).astype(low_type)
    for part in range(3):
        right_g[:, spans[part]] = times(rank_ref[...], grads[part][...], COLS_BY_COLS).astype(low_type)
    left_g[...] = times(turned[...], normed_ref[...], COLS_BY_COLS).astype(low_type)
    for part in range(3):
        wait_for(held.at[part], arrived.at[part])
        for first in range(0, count, TILE):
            rows = slice(first, first + TILE)
            value = times(grads[part][rows, :], square(held.at[part]), ROWS_BY_ROWS)
            if part == 0:
                total[rows, :] = value + times(turned[rows, :], left_ref[...])
            else:
                total[rows, :] = total[rows, :] + value

    def pull(rows):
        out_ref[rows, :] = grad_ref[rows, :] + normalize_pull(
            total[rows, :], unit_ref[rows, :].astype(wide), scale_ref[rows, :1], gain_ref[...]
        )

    strips(count, pull)


def frozen_call(kernel, name, at, weights, members, outs, scratch, cost):
    form, sources = weights
    local_spec = pl.BlockSpec(memory_space=pltpu.VMEM)
    return pl.pallas_call(
        functools.partial(kernel, form),
        out_shape=tuple(jax.ShapeDtypeStruct(shape, kind) for shape, kind in outs),
        in_specs=[pl.BlockSpec(memory_space=pltpu.SMEM)]
        + [local_spec] * len(members)
        + [pl.BlockSpec(memory_space=pl.ANY)] * len(sources),
        out_specs=(local_spec,) * len(outs),
        scratch_shapes=scratch,
        compiler_params=pltpu.CompilerParams(vmem_limit_bytes=56 * 2**20),
        cost_estimate=pl.CostEstimate(flops=cost, bytes_accessed=0, transcendentals=0),
        name=name,
    )(at, *members, *sources)


def row(vector):
    return vector.reshape(1, -1)


DMA = pltpu.SemaphoreType.DMA


def layer_forward(current, frozen, picked, extras, at, place, count):
    first_weights, second_weights = frozen
    (
        attend_left, attend_right, output_left, output_right,
        expand_left, expand_right, reduce_left, reduce_right,
    ) = picked
    (
        attend_bias, output_bias, expand_bias, reduce_bias,
        first_gain, first_shift, second_gain, second_shift,
    ) = extras
    rows, columns = current.shape
    full, full_low = ((rows, columns), wide), ((rows, columns), low_type)
    scales, ranks = ((rows, 128), wide), ((rows, RANK), low_type)
    bias = jnp.concatenate([attend_bias[:columns], jnp.zeros((columns,), wide), attend_bias[columns:]])
    normed_one, unit_one, scale_one, rank_attend, queries, keys, values = frozen_call(
        qkv_kernel, "qkv_forward", at, first_weights,
        (current, row(first_gain), row(first_shift), attend_left, attend_right, row(bias)),
        (full_low, full_low, scales, ranks, full_low, full_low, full_low),
        [pltpu.VMEM((3, *SQUARE), low_type), DMA((3,))], 10**6,
    )
    key_all, value_all = ring_gather(keys, count), ring_gather(values, count)
    attended, stat = attend_forward(place, queries, key_all, value_all)
    attended_low, middle, normed_two, unit_two, scale_two, rank_output = frozen_call(
        output_kernel, "output_forward", at, first_weights,
        (current, attended, output_left, output_right, row(output_bias), row(second_gain), row(second_shift)),
        (full_low, full, full_low, full_low, scales, ranks),
        [pltpu.VMEM(SQUARE, low_type), DMA], 10**6,
    )
    tall = ((rows, expand_right.shape[1]), low_type)
    result, slope, active, rank_expand, rank_reduce = frozen_call(
        feed_forward_kernel, "feed_forward", at, second_weights,
        (normed_two, middle, expand_left, expand_right, row(expand_bias), reduce_left, reduce_right, row(reduce_bias)),
        (full, tall, tall, ranks, ranks),
        [
            pltpu.VMEM((4, *SQUARE), low_type), pltpu.VMEM(TALL, low_type),
            pltpu.VMEM((rows, RANK), wide), DMA((2, 4)),
        ], 10**6,
    )
    kept = (
        normed_one, unit_one, scale_one, rank_attend, queries, key_all, value_all, attended, attended_low, stat,
        rank_output, normed_two, unit_two, scale_two, rank_expand, slope, active, rank_reduce,
    )
    return result, kept


def layer_backward(grad_result, kept, frozen, picked, extras, at, place, count):
    first_weights, second_weights = frozen
    (
        attend_left, attend_right, output_left, output_right,
        expand_left, expand_right, reduce_left, reduce_right,
    ) = picked
    first_gain, second_gain = extras[4], extras[6]
    (
        normed_one, unit_one, scale_one, rank_attend, queries, key_all, value_all, attended, attended_low, stat,
        rank_output, normed_two, unit_two, scale_two, rank_expand, slope, active, rank_reduce,
    ) = kept
    rows, columns = grad_result.shape
    full, full_low = ((rows, columns), wide), ((rows, columns), low_type)

    def like(member):
        return (member.shape, low_type)

    grad_middle, expand_left_g, expand_right_g, reduce_left_g, reduce_right_g = frozen_call(
        feed_backward_kernel, "feed_backward", at, second_weights,
        (
            grad_result, slope, active, normed_two, unit_two, scale_two, rank_expand, rank_reduce,
            row(second_gain), expand_left, expand_right, reduce_left, reduce_right,
        ),
        (full, like(expand_left), like(expand_right), like(reduce_left), like(reduce_right)),
        [
            pltpu.VMEM((4, *SQUARE), low_type), pltpu.VMEM(TALL, low_type), DMA((2, 4)),
            pltpu.VMEM((rows, columns), low_type), pltpu.VMEM((rows, RANK), low_type),
            pltpu.VMEM((rows, columns), low_type), pltpu.VMEM((rows, columns), wide),
            pltpu.VMEM((rows, RANK), wide),
        ], 10**6,
    )
    grad_attended, output_left_g, output_right_g = frozen_call(
        output_backward_kernel, "output_backward", at, first_weights,
        (grad_middle, attended_low, rank_output, output_left, output_right),
        (full_low, like(output_left), like(output_right)),
        [
            pltpu.VMEM(SQUARE, low_type), DMA,
            pltpu.VMEM((rows, columns), low_type), pltpu.VMEM((rows, RANK), low_type),
        ], 10**6,
    )
    grad_query, grad_keys, grad_values = attend_backward(
        place, queries, key_all, value_all, grad_attended, attended, stat
    )
    grad_current, attend_left_g, attend_right_g = frozen_call(
        qkv_backward_kernel, "qkv_backward", at, first_weights,
        (
            grad_query,
            ring_scatter(grad_keys, count).astype(low_type),
            ring_scatter(grad_values, count).astype(low_type),
            grad_middle, normed_one, unit_one, scale_one, rank_attend, row(first_gain), attend_left, attend_right,
        ),
        (full, like(attend_left), like(attend_right)),
        [
            pltpu.VMEM((3, *SQUARE), low_type), DMA((3,)),
            pltpu.VMEM((rows, RANK), low_type), pltpu.VMEM((rows, columns), wide),
        ], 10**6,
    )
    return grad_current, (
        attend_left_g, attend_right_g, output_left_g, output_right_g,
        expand_left_g, expand_right_g, reduce_left_g, reduce_right_g,
    )


def local(
    tokens, cotangent, adapter_ids, attend_weight, output_weight, expand_weight, reduce_weight,
    attend_bias, output_bias, expand_bias, reduce_bias, first_gain, first_shift, second_gain, second_shift,
    *adapters,
):
    data_count, chips = lax.axis_size("dp"), lax.axis_size("chip")
    count = chips * lax.axis_size("core")
    half = count // 2
    devices = data_count * count
    data_rank, core = lax.axis_index("dp"), lax.axis_index("core")
    rank = lax.axis_index("chip") * 2 + core
    below = rank < half
    place = jnp.reshape(lax.rem(rank, half), (1,)).astype(jnp.int32)
    columns = tokens.shape[2]
    linked = (data_count, chips, columns) == (8, 2, 1024)

    lane_chip = jnp.arange(data_count * chips, dtype=jnp.int32)
    lane_sequence = (lane_chip // chips) * 2 + (lane_chip % chips) // (chips // 2)
    lane_adapter = jnp.take(adapter_ids, lane_sequence)

    current = spread_tokens(tokens, below, count).astype(wide)
    grad_current = spread_tokens(cotangent, below, count).astype(wide)

    sizes = [member.shape[2] for member in adapters]
    packed = jnp.concatenate([jnp.swapaxes(member, 2, 3) for member in adapters], axis=3)
    chosen = jnp.moveaxis(jnp.take(packed, lane_adapter, axis=1), 1, 0)
    mine = lax.all_to_all(chosen, LANE, split_axis=0, concat_axis=0, tiled=True)
    theirs = lax.ppermute(mine, "core", [(0, 1), (1, 0)])
    both = jnp.stack(
        [jnp.where(core == 0, mine, theirs), jnp.where(core == 0, theirs, mine)], axis=1
    )

    def factors(layer_index):
        found, first = [], 0
        for size in sizes:
            part = both[:, :, layer_index, :, first : first + size]
            found.append(jnp.transpose(part, (2, 0, 1, 3)).reshape(RANK, devices * size))
            first += size
        return tuple(found)

    def shards(layer_index):
        lists = [attend_weight[layer_index], output_weight[layer_index], expand_weight[layer_index]]
        blocks = [
            member[:, first : first + columns]
            for member in lists
            for first in range(0, member.shape[1], columns)
        ]
        return jnp.concatenate(blocks + [reduce_weight[layer_index]], axis=0)

    def frozen_of(whole):
        rows = columns // devices
        squares = [
            whole[:, part * rows : (part + 1) * rows, :].reshape(SQUARE) for part in range(8)
        ]
        tall = whole[:, 8 * rows :, :].reshape(TALL)
        return ("whole", tuple(squares[:4])), ("whole", (*squares[4:], tall))

    extras = [
        tuple(
            member[layer_index]
            for member in (
                attend_bias, output_bias, expand_bias, reduce_bias,
                first_gain, first_shift, second_gain, second_shift,
            )
        )
        for layer_index in range(LAYERS)
    ]
    position = ring_position(data_rank // 2)
    at = jnp.stack([position, data_rank % 2, lax.axis_index("chip"), core]).astype(jnp.int32)
    if linked:
        first, second = shards(0), shards(1)
        found = gather_chunks(
            ((first[:128], True), (first[128:], True), (second[:128], False), (second[128:], False)),
            position,
        )
        frozen = [
            (("z first", found[0]), ("z first", found[1])),
            (("z between", found[2]), ("z between", found[3])),
        ]
    else:
        gathered = [
            lax.all_gather(shards(layer_index), EVERY, axis=0) for layer_index in range(LAYERS)
        ]
        frozen = [frozen_of(member) for member in gathered]
    picked = [factors(layer_index) for layer_index in range(LAYERS)]
    kept = []
    for layer_index in range(LAYERS):
        current, keep = layer_forward(
            current, frozen[layer_index], picked[layer_index], extras[layer_index], at, place, count
        )
        kept.append(keep)

    owner_adapter = (lane_adapter[:, None] == jnp.arange(ADAPTERS)[None, :]).astype(wide)
    summed = [None] * LAYERS
    for layer_index in reversed(range(LAYERS)):
        grad_current, terms = layer_backward(
            grad_current,
            kept[layer_index],
            frozen[layer_index],
            picked[layer_index],
            extras[layer_index],
            at,
            place,
            count,
        )
        owned = jnp.concatenate(
            [
                jnp.transpose(
                    term.astype(low_type).reshape(RANK, data_count * chips, 2, size), (2, 1, 0, 3)
                )
                for term, size in zip(terms, sizes)
            ],
            axis=3,
        )
        sent = lax.ppermute(jnp.where(core == 0, owned[1], owned[0]), "core", [(0, 1), (1, 0)])
        total = jnp.where(core == 0, owned[0], owned[1]).astype(wide) + sent.astype(wide)
        received = lax.all_to_all(
            total.astype(low_type), LANE, split_axis=0, concat_axis=0, tiled=True
        )
        summed[layer_index] = jnp.einsum(
            "sa,srp->arp", owner_adapter, received.astype(wide), precision=lax.Precision.HIGHEST
        )
    results, first = [], 0
    for size in sizes:
        member = jnp.stack([layer[:, :, first : first + size] for layer in summed])
        results.append(jnp.swapaxes(member, 2, 3))
        first += size
    outputs = collect_tokens(current.astype(low_type), below, count)
    early_late = grad_current
    moved = collect_tokens(early_late, below, count)
    return (outputs, moved, *results)


def solution(mesh):
    count = mesh.shape["ctx"]
    inner = Mesh(mesh.devices.reshape(mesh.shape["dp"], count // 2, 2), EVERY)
    token_spec, factor_spec = P("dp", CTX, None), P(None, None, EVERY, None)
    in_specs = (
        (token_spec,) * 2 + (P(),) + (P(None, EVERY, None),) * 4 + (P(),) * 8 + (factor_spec,) * 8
    )
    out_specs = (token_spec,) * 2 + (factor_spec,) * 8
    return jax.shard_map(local, mesh=inner, in_specs=in_specs, out_specs=out_specs, check_vma=False)
```

```python
import functools

import jax
import jax.numpy as jnp
from jax import lax
from jax.experimental import pallas as pl
from jax.experimental.pallas import tpu as pltpu
from jax.sharding import Mesh
from jax.sharding import PartitionSpec as P

HEADS = 16
HEAD_DIM = 64
RANK = 16
ADAPTERS = 8
LAYERS = 2

WHOLE, PIECES, GATHERED, MIXED = range(4)
MICROSECOND = 10**8
BLK = 256

epsilon = 1e-05
root_factor = 0.7978845608028654
low_type = jnp.bfloat16
wide = jnp.float32

ROWS_BY_ROWS = (((1,), (1,)), ((), ()))
COLS_BY_COLS = (((0,), (0,)), ((), ()))
PLAIN = (((1,), (0,)), ((), ()))
EVERY = ("dp", "chip", "core")
LANE = ("dp", "chip")
CTX = ("chip", "core")


def times(left_side, right_side, dims=PLAIN):
    return lax.dot_general(left_side, right_side, dims, preferred_element_type=wide)


def block_steps(place, pieces):
    steps = [(0, 0, 0), (0, 1, 0), (0, 1, 1)]
    for piece in range(1, pieces):
        slot = jnp.where(place >= piece, 0, 1)
        steps += [(piece, slot, 0), (piece, 1, slot)]
    return steps


def block_rows(slot):
    return pl.ds(slot * BLK if isinstance(slot, int) else pl.multiple_of(slot * BLK, BLK), BLK)


def stack_heads(rows, mask):
    zero = jnp.zeros_like(rows)
    return jnp.concatenate([jnp.where(mask, rows, zero), jnp.where(mask, zero, rows)], axis=0)


def update_slot(held, slot, change):
    if isinstance(slot, int):
        return [change(member) if which == slot else member for which, member in enumerate(held)]
    return [jnp.where(slot == which, change(member), member) for which, member in enumerate(held)]


def pick_slot(held, slot):
    return held[slot] if isinstance(slot, int) else jnp.where(slot == 0, held[0], held[1])


def attend_forward_kernel(pieces, place_ref, q_ref, *refs):
    k_refs, v_refs = refs[:pieces], refs[pieces : 2 * pieces]
    o_ref, stat_ref, queries, scores, total = refs[2 * pieces :]
    mask = lax.broadcasted_iota(jnp.int32, (BLK, 2 * HEAD_DIM), 1) < HEAD_DIM
    for slot in range(2):
        queries[slot] = stack_heads(q_ref[block_rows(slot), :] * HEAD_DIM**-0.5, mask)
    steps = block_steps(place_ref[0], pieces)
    peaks = [jnp.full((1, 2 * BLK), -1e30, wide)] * 2
    for step, (piece, slot, key_slot) in enumerate(steps):
        block = times(k_refs[piece][block_rows(key_slot), :], queries[slot], ROWS_BY_ROWS)
        scores[step] = block
        top = jnp.max(block, axis=0, keepdims=True)
        peaks = update_slot(peaks, slot, lambda held, top=top: jnp.maximum(held, top))
    total[...] = jnp.zeros_like(total)
    sums = [jnp.zeros((1, 2 * BLK), wide)] * 2
    for step, (piece, slot, key_slot) in enumerate(steps):
        weights = jnp.exp(scores[step] - pick_slot(peaks, slot))
        part = jnp.sum(weights, axis=0, keepdims=True)
        sums = update_slot(sums, slot, lambda held, part=part: held + part)
        weights = weights.astype(low_type)
        turned = v_refs[piece][block_rows(key_slot), :].T
        total[slot] = total[slot] + jnp.concatenate(
            [
                times(turned[:HEAD_DIM], weights[:, :BLK]),
                times(turned[HEAD_DIM:], weights[:, BLK:]),
            ],
            axis=0,
        )
    for slot in range(2):
        share = 1.0 / sums[slot]
        held = total[slot]
        held = jnp.concatenate(
            [held[:HEAD_DIM] * share[:, :BLK], held[HEAD_DIM:] * share[:, BLK:]], axis=0
        )
        o_ref[block_rows(slot), :] = held.T
        stat_ref[0, slot : slot + 1, :] = peaks[slot] + jnp.log(sums[slot])


def attend_backward_kernel(pieces, place_ref, q_ref, g_ref, o_ref, stat_ref, *refs):
    k_refs, v_refs = refs[:pieces], refs[pieces : 2 * pieces]
    dq_ref, dk_refs, dv_refs = refs[2 * pieces], refs[2 * pieces + 1 : 3 * pieces + 1], refs[3 * pieces + 1 : 4 * pieces + 1]
    queries, grads, key_sum, value_sum, query_sum, inner = refs[4 * pieces + 1 :]
    mask = lax.broadcasted_iota(jnp.int32, (BLK, 2 * HEAD_DIM), 1) < HEAD_DIM
    for slot in range(2):
        rows = block_rows(slot)
        queries[slot] = stack_heads(q_ref[rows, :] * HEAD_DIM**-0.5, mask)
        grad = g_ref[rows, :]
        grads[slot] = stack_heads(grad, mask)
        both = (grad.astype(wide) * o_ref[rows, :]).T
        inner[slot] = jnp.concatenate(
            [
                jnp.sum(both[:HEAD_DIM], axis=0, keepdims=True),
                jnp.sum(both[HEAD_DIM:], axis=0, keepdims=True),
            ],
            axis=1,
        )
    key_sum[...] = jnp.zeros_like(key_sum)
    value_sum[...] = jnp.zeros_like(value_sum)
    query_sum[...] = jnp.zeros_like(query_sum)
    for piece, slot, key_slot in block_steps(place_ref[0], pieces):
        at = block_rows(key_slot)
        keys, values = k_refs[piece][at, :], v_refs[piece][at, :]
        own, grad = queries[slot], grads[slot]
        probs = jnp.exp(times(keys, own, ROWS_BY_ROWS) - stat_ref[0, pl.ds(slot, 1), :])
        dscores = probs * (times(values, grad, ROWS_BY_ROWS) - inner[slot])
        dscores = dscores.astype(low_type)
        value_sum[piece, at, :] = value_sum[piece, at, :] + times(probs.astype(low_type), grad)
        key_sum[piece, at, :] = key_sum[piece, at, :] + times(dscores, own)
        turned = keys.T
        query_sum[slot] = query_sum[slot] + jnp.concatenate(
            [
                times(turned[:HEAD_DIM], dscores[:, :BLK]),
                times(turned[HEAD_DIM:], dscores[:, BLK:]),
            ],
            axis=0,
        )
    for slot in range(2):
        dq_ref[block_rows(slot), :] = (query_sum[slot].T * HEAD_DIM**-0.5).astype(low_type)
    for piece in range(pieces):
        dk_refs[piece][...] = key_sum[piece].astype(low_type)
        dv_refs[piece][...] = value_sum[piece].astype(low_type)


def attention_specs():
    own = pl.BlockSpec((2 * BLK, 2 * HEAD_DIM), lambda pair, place: (0, pair))
    stats = pl.BlockSpec((1, 2, 2 * BLK), lambda pair, place: (pair, 0, 0))
    return own, stats


def attend_forward(place, queries, keys, values):
    pieces, pairs = len(keys), queries.shape[1] // (2 * HEAD_DIM)
    own, stats = attention_specs()
    return pl.pallas_call(
        functools.partial(attend_forward_kernel, pieces),
        out_shape=(
            jax.ShapeDtypeStruct(queries.shape, wide),
            jax.ShapeDtypeStruct((pairs, 2, 2 * BLK), wide),
        ),
        grid_spec=pltpu.PrefetchScalarGridSpec(
            num_scalar_prefetch=1,
            grid=(pairs,),
            in_specs=[own] * (1 + 2 * pieces),
            out_specs=[own, stats],
            scratch_shapes=[
                pltpu.VMEM((2, 2 * BLK, 2 * HEAD_DIM), low_type),
                pltpu.VMEM((2 * pieces + 1, BLK, 2 * BLK), wide),
                pltpu.VMEM((2, 2 * HEAD_DIM, BLK), wide),
            ],
        ),
        compiler_params=pltpu.CompilerParams(vmem_limit_bytes=48 * 2**20),
        cost_estimate=pl.CostEstimate(flops=13 * MICROSECOND, bytes_accessed=0, transcendentals=0),
        name="attend_forward",
    )(place, queries, *keys, *values)


def attend_backward(place, queries, keys, values, grads, attended, stat):
    pieces, pairs = len(keys), queries.shape[1] // (2 * HEAD_DIM)
    own, stats = attention_specs()
    query_grad, *others = pl.pallas_call(
        functools.partial(attend_backward_kernel, pieces),
        out_shape=(jax.ShapeDtypeStruct(queries.shape, low_type),) * (1 + 2 * pieces),
        grid_spec=pltpu.PrefetchScalarGridSpec(
            num_scalar_prefetch=1,
            grid=(pairs,),
            in_specs=[own, own, own, stats] + [own] * (2 * pieces),
            out_specs=[own] * (1 + 2 * pieces),
            scratch_shapes=[
                pltpu.VMEM((2, 2 * BLK, 2 * HEAD_DIM), low_type),
                pltpu.VMEM((2, 2 * BLK, 2 * HEAD_DIM), low_type),
                pltpu.VMEM((pieces, 2 * BLK, 2 * HEAD_DIM), wide),
                pltpu.VMEM((pieces, 2 * BLK, 2 * HEAD_DIM), wide),
                pltpu.VMEM((2, 2 * HEAD_DIM, BLK), wide),
                pltpu.VMEM((2, 1, 2 * BLK), wide),
            ],
        ),
        compiler_params=pltpu.CompilerParams(vmem_limit_bytes=48 * 2**20),
        cost_estimate=pl.CostEstimate(flops=21 * MICROSECOND, bytes_accessed=0, transcendentals=0),
        name="attend_backward",
    )(place, queries, grads, attended, stat, *keys, *values)
    return query_grad, others[:pieces], others[pieces:]


def spread_tokens(pair, below, count):
    half = count // 2
    across = [(b, half + b if b < half else count - 1 - b) for b in range(count)]
    inside = [(b, half + count - 1 - b) for b in range(half, count)]
    got = lax.ppermute(jnp.where(below, pair[1], pair[0]), CTX, across)
    other = lax.ppermute(pair[1], CTX, inside)
    return jnp.concatenate(
        [jnp.where(below, pair[0], got), jnp.where(below, got, other)], axis=0
    )


def collect_tokens(rows, below, count):
    half = count // 2
    across = [(half + b if b < half else count - 1 - b, b) for b in range(count)]
    inside = [(half + count - 1 - b, b) for b in range(half, count)]
    early, late = rows[:BLK], rows[BLK:]
    got = lax.ppermute(jnp.where(below, late, early), CTX, across)
    other = lax.ppermute(late, CTX, inside)
    return jnp.stack([jnp.where(below, early, got), jnp.where(below, got, other)])


def collect_own(rows, below):
    mask = jnp.stack([below, jnp.zeros_like(below)])[:, None, None]
    return mask, jnp.stack([rows[:BLK], rows[:BLK]])


def ring_gather(rows, count):
    half = count // 2
    pieces = [rows]
    for step in range(1, half):
        pairs = [
            (side * half + b, side * half + (b + step) % half)
            for side in range(2)
            for b in range(half)
        ]
        pieces.append(lax.ppermute(rows, CTX, pairs))
    return pieces


def ring_scatter(pieces, count):
    half = count // 2
    arrived = []
    for step in range(1, half):
        pairs = [
            (side * half + b, side * half + (b - step) % half)
            for side in range(2)
            for b in range(half)
        ]
        arrived.append(lax.ppermute(pieces[step], CTX, pairs))
    return arrived


def add_up(members):
    return sum(member.astype(wide) for member in members).astype(low_type)


def ring_position(z):
    return jnp.where(z == 2, 3, jnp.where(z == 3, 2, z))


SWAP = [(0, 1), (1, 0)]
RING = [(z * 2 + x, after * 2 + x) for z, after in enumerate((1, 3, 0, 2)) for x in range(2)]
ACROSS_X = [(d, d ^ 1) for d in range(8)]


def along_z(rows):
    return lax.ppermute(rows, "dp", RING)


def along_x(rows):
    return lax.ppermute(rows, "dp", ACROSS_X)


def along_y(rows):
    return lax.ppermute(rows, "chip", SWAP)


def on_chip(rows):
    return lax.ppermute(rows, "core", SWAP)


def join(*members):
    return jnp.concatenate(members, axis=0)


def by_z(ring, first, rows, position):
    parts = [member[first : first + rows] for member in ring]
    placed = []
    for spot in (0, 1, 3, 2):
        step = lax.rem(position + 4 - spot, 4)
        chosen = parts[3]
        for index in (2, 1, 0):
            chosen = jnp.where(step == index, parts[index], chosen)
        placed.append(chosen)
    return jnp.stack(placed)


def z_halves(ring, position):
    size = ring[0].shape[0] // 2
    return [by_z(ring, part * size, size, position) for part in range(2)]


def cross(halves):
    return [along_x(halves[0]), along_y(halves[1])]


def cross_other(halves):
    return [along_y(halves[0]), along_x(halves[1])]


def paired(halves, crossed):
    return [jnp.stack([halves[part], crossed[part]]) for part in range(2)]


def swapped(members):
    return [on_chip(member) for member in members]


def linked_forward(
    first, second, chosen, tokens, cotangent, sizes, at, below, count, kept, attention_step, output_step, feed_step
):
    position = at[0]

    def gather(rows):
        whole = lax.all_gather(rows, EVERY, axis=0)
        return whole.reshape(4, 2, 2, 2, *rows.shape)

    v = Bag()
    v.f, v.g, v.h = [first[:128]], [second[:128]], [second[128:256]]
    first_feed, second_reduce = gather(first[128:]), gather(second[256:])

    def advance(ring):
        ring.append(along_z(ring[-1]))

    def mix(near, far):
        return near[0], far[0], near[1], far[1]

    def weights_f():
        return mix(v.f_near, v.f_far) + mix(v.f_near_other, v.f_far_other)

    def weights_g():
        return mix(v.g_near, v.g_far) + mix(v.g_near_other, v.g_far_other)

    def weights_h():
        return mix(v.h_near, v.h_far) + mix(v.h_near_other, v.h_far_other)

    for _ in range(3):
        advance(v.f)
    v.tokens = spread_tokens(tokens, below, count)
    v.chosen = chosen
    v = sync(v)
    v.f_half = z_halves(v.f, position)
    del v.f
    v.f_cross = cross(v.f_half)
    v.factors = lax.all_to_all(v.chosen, LANE, split_axis=0, concat_axis=0, tiled=True)
    del v.chosen
    advance(v.g)
    v = sync(v)
    v.f_near = paired(v.f_half, v.f_cross)
    del v.f_half, v.f_cross
    v.f_far = cross_other(v.f_near)
    v.f_near_other = swapped(v.f_near)
    v.factors_other = on_chip(v.factors)
    advance(v.g)
    advance(v.g)
    v = sync(v)
    v.g_half = z_halves(v.g, position)
    del v.g
    v.g_cross = cross(v.g_half)
    v.f_far_other = swapped(v.f_far)
    v.picked = unpack_factors(at, v.factors, v.factors_other, sizes)
    del v.factors, v.factors_other
    advance(v.h)
    v = sync(v)
    v.g_near = paired(v.g_half, v.g_cross)
    del v.g_half, v.g_cross
    v.g_far = cross_other(v.g_near)
    v.g_near_other = swapped(v.g_near)
    advance(v.h)
    advance(v.h)
    v.current = v.tokens.astype(wide)
    del v.tokens
    v.cotangent = spread_tokens(cotangent, below, count)
    attention_step(v.current, (PIECES, weights_f()), v.picked[0], 0)
    v.middle = output_step(v.current, (PIECES, weights_f()), v.picked[0], 0)
    del v.current
    v.kept = kept
    v = sync(v)
    kept[:] = v.kept
    v.h_half = z_halves(v.h, position)
    del v.h
    v.h_cross = cross(v.h_half)
    v.g_far_other = swapped(v.g_far)
    v.current = feed_step(v.middle, (GATHERED, (first_feed,)), v.picked[0], 0)
    v.kept = kept
    v = sync(v)
    kept[:] = v.kept
    v.h_near = paired(v.h_half, v.h_cross)
    del v.h_half, v.h_cross
    v.h_far = cross_other(v.h_near)
    v.h_near_other = swapped(v.h_near)
    attention_step(v.current, (PIECES, weights_g()), v.picked[1], 1)
    v.middle = output_step(v.current, (PIECES, weights_g()), v.picked[1], 1)
    del v.current
    v.kept = kept
    v = sync(v)
    kept[:] = v.kept
    v.h_far_other = swapped(v.h_far)
    frozen = [
        ((PIECES, weights_f()), (GATHERED, (first_feed,))),
        ((PIECES, weights_g()), (MIXED, (*weights_h(), second_reduce))),
    ]
    current = feed_step(v.middle, frozen[1][1], v.picked[1], 1)
    return current, v.cotangent.astype(wide), v.picked, frozen


SQUARE = (4, 2, 2, 2, 32, 1024)
TALL = (4, 2, 2, 2, 128, 1024)


def square_unit(form, part):
    return part if form == WHOLE else (part // 2, part % 2 * 32)


def expand_unit(form, part):
    return {WHOLE: part, GATHERED: 32 * part}.get(form, (part // 2, part % 2 * 32))


def fetch(form, at_ref, sources, unit, rows, held, arrived, by_quarter=None):
    spread_z = slice(None) if by_quarter is None else by_quarter
    if not isinstance(unit, tuple):
        if form == WHOLE:
            source = sources[unit].at[spread_z]
        else:
            source = sources[-1].at[(spread_z, *[slice(None)] * 3, pl.ds(unit, rows), slice(None))]
        pltpu.make_async_copy(source, held.at[spread_z], arrived).start()
        return
    part, first = unit
    x, y, core = at_ref[1], at_ref[2], at_ref[3]
    for other in range(2):
        for far in range(2):
            source = sources[other * 4 + part * 2 + far]
            for over in range(2):
                over_x, over_y = (over, far) if part == 0 else (far, over)
                pltpu.make_async_copy(
                    source.at[over, spread_z, pl.ds(first, rows), :],
                    held.at[
                        spread_z,
                        lax.rem(x + over_x, 2),
                        lax.rem(y + over_y, 2),
                        lax.rem(core + other, 2),
                    ],
                    arrived,
                ).start()


def wait_for(held, arrived):
    pltpu.make_async_copy(held, held, arrived).wait()


def square(held):
    return held[...].reshape(1024, 1024)


TILE = 256
STRIP = 32
COLUMNS = 1024


def strips(count, body):
    def step(index, carry):
        body(pl.ds(pl.multiple_of(index * STRIP, STRIP), STRIP))
        return carry

    lax.fori_loop(0, count // STRIP, step, 0)


def normalize_rows(values, gain, shift):
    center = jnp.mean(values, axis=-1, keepdims=True)
    spread = values - center
    scale = lax.rsqrt(jnp.mean(spread * spread, axis=-1, keepdims=True) + epsilon)
    unit = spread * scale
    return unit, scale, unit * gain + shift


def normalize_pull(grad, unit, scale, gain):
    scaled = grad * gain
    first = jnp.mean(scaled, axis=-1, keepdims=True)
    second = jnp.mean(scaled * unit, axis=-1, keepdims=True)
    return scale * (scaled - first - unit * second)


def qkv_kernel(form, at_ref, x_ref, gain_ref, shift_ref, left_ref, right_ref, bias_ref, *refs):
    sources, (normed_ref, unit_ref, scale_ref, rank_ref, *outs) = refs[:-9], refs[-9:-2]
    held, arrived = refs[-2:]
    for part in range(3):
        fetch(form, at_ref, sources, square_unit(form, part), 32, held.at[part], arrived.at[part])

    def norm(rows):
        unit, scale, normed = normalize_rows(x_ref[rows, :], gain_ref[...], shift_ref[...])
        normed_ref[rows, :] = normed.astype(low_type)
        unit_ref[rows, :] = unit.astype(low_type)
        scale_ref[rows, :] = jnp.broadcast_to(scale, (STRIP, 128))

    strips(x_ref.shape[0], norm)
    rank_ref[...] = times(normed_ref[...], left_ref[...], ROWS_BY_ROWS).astype(low_type)
    for part, out in enumerate(outs):
        wait_for(held.at[part], arrived.at[part])
        columns = slice(part * COLUMNS, (part + 1) * COLUMNS)
        for first in range(0, x_ref.shape[0], TILE):
            rows = slice(first, first + TILE)
            out[rows, :] = (
                times(normed_ref[rows, :], square(held.at[part]))
                + times(rank_ref[rows, :], right_ref[:, columns])
                + bias_ref[:, columns]
            ).astype(low_type)


def output_kernel(form, at_ref, x_ref, attended_ref, left_ref, right_ref, bias_ref, gain_ref, shift_ref, *refs):
    sources, (low_ref, middle_ref, normed_ref, unit_ref, scale_ref, rank_ref) = refs[:-8], refs[-8:-2]
    held, arrived = refs[-2:]
    fetch(form, at_ref, sources, square_unit(form, 3), 32, held, arrived)
    low_ref[...] = attended_ref[...].astype(low_type)
    rank_ref[...] = times(low_ref[...], left_ref[...], ROWS_BY_ROWS).astype(low_type)
    wait_for(held, arrived)
    for first in range(0, x_ref.shape[0], TILE):
        rows = slice(first, first + TILE)
        middle_ref[rows, :] = (
            x_ref[rows, :]
            + times(low_ref[rows, :], square(held))
            + times(rank_ref[rows, :], right_ref[...])
            + bias_ref[...]
        )

    def norm(rows):
        unit, scale, normed = normalize_rows(middle_ref[rows, :], gain_ref[...], shift_ref[...])
        normed_ref[rows, :] = normed.astype(low_type)
        unit_ref[rows, :] = unit.astype(low_type)
        scale_ref[rows, :] = jnp.broadcast_to(scale, (STRIP, 128))

    strips(x_ref.shape[0], norm)


def fetch_feed_forward(form, at_ref, sources, expand, reduce, arrived, reduce_first):
    for part in range(4):
        jobs = [
            (expand_unit(form, part), 32, expand.at[part], arrived.at[0, part], None),
            ({WHOLE: 4, GATHERED: 128, MIXED: 0}[form], 128, reduce, arrived.at[1, part], part),
        ]
        for unit, rows, held, semaphore, quarter in jobs[::-1] if reduce_first else jobs:
            fetch(form, at_ref, sources, unit, rows, held, semaphore, quarter)


def feed_forward_kernel(
    form, at_ref, normed_ref, middle_ref, expand_left_ref, expand_right_ref, expand_bias_ref,
    reduce_left_ref, reduce_right_ref, reduce_bias_ref, *refs,
):
    sources, (result_ref, slope_ref, active_ref, rank_expand_ref, rank_reduce_ref) = refs[:-9], refs[-9:-4]
    expand, reduce, rank_sum, arrived = refs[-4:]
    fetch_feed_forward(form, at_ref, sources, expand, reduce, arrived, False)
    count = normed_ref.shape[0]
    rank_expand_ref[...] = times(normed_ref[...], expand_left_ref[...], ROWS_BY_ROWS).astype(low_type)
    result_ref[...] = middle_ref[...] + reduce_bias_ref[...]
    rank_sum[...] = jnp.zeros_like(rank_sum)

    def part_step(part, carry):
        columns = pl.ds(pl.multiple_of(part * COLUMNS, COLUMNS), COLUMNS)
        wait_for(expand.at[part], arrived.at[0, part])
        wait_for(reduce.at[part], arrived.at[1, part])
        for first in range(0, count, TILE):
            rows = slice(first, first + TILE)
            value = (
                times(normed_ref[rows, :], square(expand.at[part]))
                + times(rank_expand_ref[rows, :], expand_right_ref[:, columns])
                + expand_bias_ref[:, columns]
            )
            squared = value * value
            bent = jnp.tanh(root_factor * value * (1.0 + 0.044715 * squared))
            half = 0.5 * (1.0 + bent)
            slope_ref[rows, columns] = (
                half
                + 0.5 * value * (1.0 - bent * bent) * (root_factor + 3 * 0.044715 * root_factor * squared)
            ).astype(low_type)
            active = (value * half).astype(low_type)
            active_ref[rows, columns] = active
            result_ref[rows, :] = result_ref[rows, :] + times(active, square(reduce.at[part]))
            rank_sum[rows, :] = rank_sum[rows, :] + times(
                active, reduce_left_ref[:, columns], ROWS_BY_ROWS
            )
        return carry

    lax.fori_loop(0, 4, part_step, 0)
    rank_reduce_ref[...] = rank_sum[...].astype(low_type)
    result_ref[...] = result_ref[...] + times(rank_reduce_ref[...], reduce_right_ref[...])


def feed_backward_kernel(
    form, at_ref, grad_ref, slope_ref, active_ref, normed_ref, unit_ref, scale_ref, rank_expand_ref, rank_reduce_ref,
    gain_ref, expand_left_ref, expand_right_ref, reduce_left_ref, reduce_right_ref, *refs,
):
    sources, (out_ref, expand_left_g, expand_right_g, reduce_left_g, reduce_right_g) = refs[:-13], refs[-13:-8]
    expand, reduce, arrived, low_grad, turned, bent, total, turn_sum = refs[-8:]
    fetch_feed_forward(form, at_ref, sources, expand, reduce, arrived, True)
    count = grad_ref.shape[0]
    low_grad[...] = grad_ref[...].astype(low_type)
    turned[...] = times(low_grad[...], reduce_right_ref[...], ROWS_BY_ROWS).astype(low_type)
    reduce_right_g[...] = times(rank_reduce_ref[...], low_grad[...], COLS_BY_COLS).astype(low_type)
    total[...] = jnp.zeros_like(total)
    turn_sum[...] = jnp.zeros_like(turn_sum)

    def part_step(part, carry):
        columns = pl.ds(pl.multiple_of(part * COLUMNS, COLUMNS), COLUMNS)
        wait_for(reduce.at[part], arrived.at[1, part])
        wait_for(expand.at[part], arrived.at[0, part])
        for first in range(0, count, TILE):
            rows = slice(first, first + TILE)
            grad_active = times(low_grad[rows, :], square(reduce.at[part]), ROWS_BY_ROWS) + times(
                turned[rows, :], reduce_left_ref[:, columns]
            )
            grad_expand = (grad_active * slope_ref[rows, columns].astype(wide)).astype(low_type)
            bent[rows, :] = grad_expand
            total[rows, :] = total[rows, :] + times(grad_expand, square(expand.at[part]), ROWS_BY_ROWS)
            turn_sum[rows, :] = turn_sum[rows, :] + times(
                grad_expand, expand_right_ref[:, columns], ROWS_BY_ROWS
            )
        reduce_left_g[:, columns] = times(turned[...], active_ref[:, columns], COLS_BY_COLS).astype(
            low_type
        )
        expand_right_g[:, columns] = times(rank_expand_ref[...], bent[...], COLS_BY_COLS).astype(low_type)
        return carry

    lax.fori_loop(0, 4, part_step, 0)
    turned[...] = turn_sum[...].astype(low_type)
    expand_left_g[...] = times(turned[...], normed_ref[...], COLS_BY_COLS).astype(low_type)
    total[...] = total[...] + times(turned[...], expand_left_ref[...])

    def pull(rows):
        out_ref[rows, :] = grad_ref[rows, :] + normalize_pull(
            total[rows, :], unit_ref[rows, :].astype(wide), scale_ref[rows, :1], gain_ref[...]
        )

    strips(count, pull)


def output_backward_kernel(form, at_ref, grad_ref, attended_ref, rank_ref, left_ref, right_ref, *refs):
    sources, (out_ref, left_g, right_g) = refs[:-7], refs[-7:-4]
    held, arrived, low_grad, turned = refs[-4:]
    fetch(form, at_ref, sources, square_unit(form, 3), 32, held, arrived)
    low_grad[...] = grad_ref[...].astype(low_type)
    turned[...] = times(low_grad[...], right_ref[...], ROWS_BY_ROWS).astype(low_type)
    right_g[...] = times(rank_ref[...], low_grad[...], COLS_BY_COLS).astype(low_type)
    left_g[...] = times(turned[...], attended_ref[...], COLS_BY_COLS).astype(low_type)
    wait_for(held, arrived)
    for first in range(0, grad_ref.shape[0], TILE):
        rows = slice(first, first + TILE)
        out_ref[rows, :] = (
            times(low_grad[rows, :], square(held), ROWS_BY_ROWS) + times(turned[rows, :], left_ref[...])
        ).astype(low_type)


def qkv_backward_kernel(
    pieces, form, at_ref, grad_ref, normed_ref, unit_ref, scale_ref, rank_ref, gain_ref, left_ref, right_ref, dq_ref, *refs
):
    dk_refs, dv_refs, refs = refs[:pieces], refs[pieces : 2 * pieces], refs[2 * pieces :]
    sources, (out_ref, left_g, right_g) = refs[:-9], refs[-9:-6]
    held, arrived, turned, total, dk_ref, dv_ref = refs[-6:]
    count = grad_ref.shape[0]
    for part in range(3):
        fetch(form, at_ref, sources, square_unit(form, part), 32, held.at[part], arrived.at[part])
    dk_ref[...] = add_up([member[...] for member in dk_refs])
    dv_ref[...] = add_up([member[...] for member in dv_refs])
    grads = (dq_ref, dk_ref, dv_ref)
    spans = [slice(part * COLUMNS, (part + 1) * COLUMNS) for part in range(3)]
    turned[...] = sum(
        times(grads[part][...], right_ref[:, spans[part]], ROWS_BY_ROWS) for part in range(3)
    ).astype(low_type)
    for part in range(3):
        right_g[:, spans[part]] = times(rank_ref[...], grads[part][...], COLS_BY_COLS).astype(low_type)
    left_g[...] = times(turned[...], normed_ref[...], COLS_BY_COLS).astype(low_type)
    for part in range(3):
        wait_for(held.at[part], arrived.at[part])
        for first in range(0, count, TILE):
            rows = slice(first, first + TILE)
            value = times(grads[part][rows, :], square(held.at[part]), ROWS_BY_ROWS)
            if part == 0:
                total[rows, :] = value + times(turned[rows, :], left_ref[...])
            else:
                total[rows, :] = total[rows, :] + value

    def pull(rows):
        out_ref[rows, :] = grad_ref[rows, :] + normalize_pull(
            total[rows, :], unit_ref[rows, :].astype(wide), scale_ref[rows, :1], gain_ref[...]
        )

    strips(count, pull)


def frozen_call(kernel, name, at, weights, members, outs, scratch, cost):
    form, sources = weights
    local_spec = pl.BlockSpec(memory_space=pltpu.VMEM)
    return pl.pallas_call(
        functools.partial(kernel, form),
        out_shape=tuple(jax.ShapeDtypeStruct(shape, kind) for shape, kind in outs),
        in_specs=[pl.BlockSpec(memory_space=pltpu.SMEM)]
        + [local_spec] * len(members)
        + [pl.BlockSpec(memory_space=pl.ANY)] * len(sources),
        out_specs=(local_spec,) * len(outs),
        scratch_shapes=scratch,
        compiler_params=pltpu.CompilerParams(vmem_limit_bytes=56 * 2**20),
        cost_estimate=pl.CostEstimate(flops=cost * MICROSECOND, bytes_accessed=0, transcendentals=0),
        name=name,
    )(at, *members, *sources)


def row(vector):
    return vector.reshape(1, -1)


DMA = pltpu.SemaphoreType.DMA


PACKED = ((5, 0), (6, 128), (1, 256), (0, 352), (2, 384), (3, 416), (4, 448), (7, 480))
PACKED_EARLY = ((5, 0), (6, 128), (2, 256), (3, 288), (4, 320), (7, 352))
PACKED_LATE = ((1, 0), (0, 96))


def unpack_kernel(order, at_ref, own_ref, other_ref, *outs):
    layers, groups = own_ref.shape[1], own_ref.shape[0] // 2
    swapped = at_ref[3] == 1
    for layer_index in range(layers):
        for group in range(groups):
            lanes = []
            for chip in range(2):
                own = own_ref[group * 2 + chip, layer_index]
                other = other_ref[group * 2 + chip, layer_index]
                lanes += [jnp.where(swapped, other, own), jnp.where(swapped, own, other)]
            for kind, first in order:
                out = outs[layer_index * len(order) + kind]
                size = out.shape[1] // (4 * groups)
                out[:, group * 4 * size : (group + 1) * 4 * size] = jnp.concatenate(
                    [lane[:, first : first + size] for lane in lanes], axis=1
                )


def unpack_factors(at, own, other, sizes):
    lanes, layers = own.shape[:2]
    local_spec = pl.BlockSpec(memory_space=pltpu.VMEM)
    found = pl.pallas_call(
        functools.partial(unpack_kernel, PACKED),
        out_shape=tuple(
            jax.ShapeDtypeStruct((RANK, size * lanes * 2), low_type) for _ in range(layers) for size in sizes
        ),
        in_specs=[pl.BlockSpec(memory_space=pltpu.SMEM), local_spec, local_spec],
        out_specs=(local_spec,) * (layers * len(sizes)),
        compiler_params=pltpu.CompilerParams(vmem_limit_bytes=32 * 2**20),
        cost_estimate=pl.CostEstimate(flops=4 * MICROSECOND, bytes_accessed=0, transcendentals=0),
        name="unpack_factors",
    )(at, own, other)
    return [found[layer * len(sizes) : (layer + 1) * len(sizes)] for layer in range(layers)]


def pack_kernel(orders, at_ref, *refs):
    members, out_ref = refs[:-1], refs[-1]
    core, base, offset = at_ref[3], 0, 0
    for order in orders:
        for lane_chip in range(out_ref.shape[1]):
            for owner_core in range(2):
                owner = lane_chip * 2 + owner_core
                parts = []
                for index, _ in enumerate(order):
                    member = members[base + index]
                    size = member.shape[1] // (2 * out_ref.shape[1])
                    parts.append(member[:, owner * size : (owner + 1) * size])
                joined = jnp.concatenate(parts, axis=1)
                out_ref[lax.rem(owner_core + core, 2), lane_chip, :, offset : offset + joined.shape[1]] = joined
        base += len(order)
        offset += joined.shape[1]


def pack_gradients(at, groups, lanes):
    members, width = [], 0
    for order, terms in groups:
        members += [terms[kind] for kind, _ in order]
        width += sum(terms[kind].shape[1] for kind, _ in order) // (2 * lanes)
    local_spec = pl.BlockSpec(memory_space=pltpu.VMEM)
    return pl.pallas_call(
        functools.partial(pack_kernel, [order for order, _ in groups]),
        out_shape=jax.ShapeDtypeStruct((2, lanes, RANK, width), low_type),
        in_specs=[pl.BlockSpec(memory_space=pltpu.SMEM)] + [local_spec] * len(members),
        out_specs=local_spec,
        compiler_params=pltpu.CompilerParams(vmem_limit_bytes=32 * 2**20),
        cost_estimate=pl.CostEstimate(flops=4 * MICROSECOND, bytes_accessed=0, transcendentals=0),
        name="pack_gradients",
    )(at, *members)


LOW, WIDE = low_type, wide


def forward_qkv(current, weights, picked, extras, at):
    rows, columns = current.shape
    full_low = ((rows, columns), LOW)
    bias = jnp.concatenate([extras[0][:columns], jnp.zeros((columns,), WIDE), extras[0][columns:]])
    return frozen_call(
        qkv_kernel, "qkv_forward", at, weights,
        (current, row(extras[4]), row(extras[5]), picked[0], picked[1], row(bias)),
        (full_low, full_low, ((rows, 128), WIDE), ((rows, RANK), LOW), full_low, full_low, full_low),
        [pltpu.VMEM((3, *SQUARE), LOW), DMA((3,))], 9,
    )


def forward_output(current, attended, weights, picked, extras, at):
    rows, columns = current.shape
    full, full_low = ((rows, columns), WIDE), ((rows, columns), LOW)
    return frozen_call(
        output_kernel, "output_forward", at, weights,
        (current, attended, picked[2], picked[3], row(extras[1]), row(extras[6]), row(extras[7])),
        (full_low, full, full_low, full_low, ((rows, 128), WIDE), ((rows, RANK), LOW)),
        [pltpu.VMEM(SQUARE, LOW), DMA], 8,
    )


def forward_feed(normed, middle, weights, picked, extras, at):
    rows, columns = middle.shape
    tall, ranks = ((rows, picked[5].shape[1]), LOW), ((rows, RANK), LOW)
    return frozen_call(
        feed_forward_kernel, "feed_forward", at, weights,
        (normed, middle, picked[4], picked[5], row(extras[2]), picked[6], picked[7], row(extras[3])),
        (((rows, columns), WIDE), tall, tall, ranks, ranks),
        [
            pltpu.VMEM((4, *SQUARE), LOW), pltpu.VMEM(TALL, LOW), pltpu.VMEM((rows, RANK), WIDE), DMA((2, 4)),
        ], 20,
    )


def like(member):
    return (member.shape, LOW)


def backward_feed(grad, kept, weights, picked, extras, at):
    rows, columns = grad.shape
    full_low, ranks = pltpu.VMEM((rows, columns), LOW), pltpu.VMEM((rows, RANK), LOW)
    return frozen_call(
        feed_backward_kernel, "feed_backward", at, weights,
        (
            grad, kept.slope, kept.active, kept.normed_two, kept.unit_two, kept.scale_two,
            kept.rank_expand, kept.rank_reduce, row(extras[6]), *picked[4:],
        ),
        (((rows, columns), WIDE), *map(like, picked[4:])),
        [
            pltpu.VMEM((4, *SQUARE), LOW), pltpu.VMEM(TALL, LOW), DMA((2, 4)), full_low, ranks, full_low,
            pltpu.VMEM((rows, columns), WIDE), pltpu.VMEM((rows, RANK), WIDE),
        ], 22,
    )


def backward_output(grad, kept, weights, picked, at):
    rows, columns = grad.shape
    return frozen_call(
        output_backward_kernel, "output_backward", at, weights,
        (grad, kept.attended_low, kept.rank_output, picked[2], picked[3]),
        (((rows, columns), LOW), like(picked[2]), like(picked[3])),
        [pltpu.VMEM(SQUARE, LOW), DMA, pltpu.VMEM((rows, columns), LOW), pltpu.VMEM((rows, RANK), LOW)], 5,
    )


def backward_qkv(grad, grads, kept, weights, picked, extras, at):
    rows, columns = grad.shape
    query_grad, key_grads, value_grads = grads
    return frozen_call(
        functools.partial(qkv_backward_kernel, len(key_grads)), "qkv_backward", at, weights,
        (
            grad, kept.normed_one, kept.unit_one, kept.scale_one, kept.rank_attend, row(extras[4]),
            picked[0], picked[1], query_grad, *key_grads, *value_grads,
        ),
        (((rows, columns), WIDE), like(picked[0]), like(picked[1])),
        [
            pltpu.VMEM((3, *SQUARE), LOW), DMA((3,)), pltpu.VMEM((rows, RANK), LOW),
            pltpu.VMEM((rows, columns), WIDE), pltpu.VMEM((rows, columns), LOW), pltpu.VMEM((rows, columns), LOW),
        ], 11,
    )


class Bag:
    pass


def open_bag(bag):
    names = tuple(sorted(vars(bag)))
    return tuple(getattr(bag, name) for name in names), names


def close_bag(names, members):
    bag = Bag()
    for name, member in zip(names, members):
        setattr(bag, name, member)
    return bag


jax.tree_util.register_pytree_node(Bag, open_bag, close_bag)


def sync(values):
    leaves, shape = jax.tree.flatten(values)
    return jax.tree.unflatten(shape, lax.optimization_barrier(tuple(leaves)))


def local(
    tokens, cotangent, adapter_ids, attend_weight, output_weight, expand_weight, reduce_weight,
    attend_bias, output_bias, expand_bias, reduce_bias, first_gain, first_shift, second_gain, second_shift,
    *adapters,
):
    data_count, chips = lax.axis_size("dp"), lax.axis_size("chip")
    count = chips * lax.axis_size("core")
    half = count // 2
    devices = data_count * count
    data_rank, core = lax.axis_index("dp"), lax.axis_index("core")
    rank = lax.axis_index("chip") * 2 + core
    below = rank < half
    place = jnp.reshape(lax.rem(rank, half), (1,)).astype(jnp.int32)
    columns = tokens.shape[2]
    linked = (data_count, chips, columns) == (8, 2, 1024)

    lane_chip = jnp.arange(data_count * chips, dtype=jnp.int32)
    lane_sequence = (lane_chip // chips) * 2 + (lane_chip % chips) // (chips // 2)
    lane_adapter = jnp.take(adapter_ids, lane_sequence)

    sizes = [member.shape[2] for member in adapters]
    packed = jnp.concatenate([jnp.swapaxes(adapters[kind], 2, 3) for kind, _ in PACKED], axis=3)
    chosen = jnp.moveaxis(jnp.take(packed, lane_adapter, axis=1), 1, 0)

    def shards(layer_index):
        lists = [attend_weight[layer_index], output_weight[layer_index], expand_weight[layer_index]]
        blocks = [
            member[:, first : first + columns]
            for member in lists
            for first in range(0, member.shape[1], columns)
        ]
        return jnp.concatenate(blocks + [reduce_weight[layer_index]], axis=0)

    extras = [
        tuple(
            member[layer_index]
            for member in (
                attend_bias, output_bias, expand_bias, reduce_bias,
                first_gain, first_shift, second_gain, second_shift,
            )
        )
        for layer_index in range(LAYERS)
    ]
    position = ring_position(data_rank // 2)
    at = jnp.stack([position, data_rank % 2, lax.axis_index("chip"), core]).astype(jnp.int32)
    kept = [Bag(), Bag()]

    def attention_step(current, weights, picked, layer_index):
        keep = kept[layer_index]
        (
            keep.normed_one, keep.unit_one, keep.scale_one, keep.rank_attend,
            keep.queries, keys, values,
        ) = forward_qkv(current, weights, picked, extras[layer_index], at)
        keep.keys, keep.values = ring_gather(keys, count), ring_gather(values, count)
        keep.attended, keep.stat = attend_forward(place, keep.queries, keep.keys, keep.values)

    def output_step(current, weights, picked, layer_index):
        keep = kept[layer_index]
        (
            keep.attended_low, middle, keep.normed_two, keep.unit_two, keep.scale_two,
            keep.rank_output,
        ) = forward_output(current, keep.attended, weights, picked, extras[layer_index], at)
        return middle

    def feed_step(middle, weights, picked, layer_index):
        keep = kept[layer_index]
        result, keep.slope, keep.active, keep.rank_expand, keep.rank_reduce = forward_feed(
            keep.normed_two, middle, weights, picked, extras[layer_index], at
        )
        return result

    if linked:
        first, second = shards(0), shards(1)
        current, grad_current, picked, frozen = linked_forward(
            first, second, chosen, tokens, cotangent, sizes, at, below, count, kept,
            attention_step, output_step, feed_step,
        )
    else:
        current = spread_tokens(tokens, below, count).astype(wide)
        grad_current = spread_tokens(cotangent, below, count).astype(wide)
        mine = lax.all_to_all(chosen, LANE, split_axis=0, concat_axis=0, tiled=True)
        theirs = lax.ppermute(mine, "core", SWAP)
        both = jnp.stack(
            [jnp.where(core == 0, mine, theirs), jnp.where(core == 0, theirs, mine)], axis=1
        )
        places, spot = {}, 0
        for kind, _ in PACKED:
            places[kind] = spot
            spot += sizes[kind]
        picked = [
            tuple(
                jnp.transpose(
                    both[:, :, layer_index, :, places[kind] : places[kind] + size], (2, 0, 1, 3)
                ).reshape(RANK, devices * size)
                for kind, size in enumerate(sizes)
            )
            for layer_index in range(LAYERS)
        ]
        frozen = []
        for layer_index in range(LAYERS):
            whole = lax.all_gather(shards(layer_index), EVERY, axis=0)
            size = columns // devices
            squares = [whole[:, part * size : (part + 1) * size, :].reshape(SQUARE) for part in range(8)]
            tall = whole[:, 8 * size :, :].reshape(TALL)
            frozen.append(((WHOLE, tuple(squares[:4])), (WHOLE, (*squares[4:], tall))))
            first_weights, second_weights = frozen[layer_index]
            attention_step(current, first_weights, picked[layer_index], layer_index)
            middle = output_step(current, first_weights, picked[layer_index], layer_index)
            current = feed_step(middle, second_weights, picked[layer_index], layer_index)

    outputs = collect_tokens(current.astype(low_type), below, count)
    owner_adapter = (lane_adapter[:, None] == jnp.arange(ADAPTERS)[None, :]).astype(wide)
    lanes = data_count * chips

    def to_owners(groups):
        if linked:
            both = pack_gradients(at, groups, lanes)
            own, sent = both[0], both[1]
        else:
            both = jnp.concatenate(
                [
                    jnp.transpose(
                        terms[kind].reshape(RANK, lanes, 2, sizes[kind]), (2, 1, 0, 3)
                    )
                    for order, terms in groups
                    for kind, _ in order
                ],
                axis=3,
            )
            own, sent = jnp.where(core == 0, both[0], both[1]), jnp.where(core == 0, both[1], both[0])
        total = add_up([own, lax.ppermute(sent, "core", SWAP)])
        received = lax.all_to_all(total, LANE, split_axis=0, concat_axis=0, tiled=True)
        return jnp.einsum(
            "sa,srp->arp", owner_adapter, received.astype(wide), precision=lax.Precision.HIGHEST
        )

    terms = [None] * LAYERS
    summed = []
    for layer_index in reversed(range(LAYERS)):
        keep, extra, factors = kept[layer_index], extras[layer_index], picked[layer_index]
        first_weights, second_weights = frozen[layer_index]
        middle_grad, *feed_terms = backward_feed(grad_current, keep, second_weights, factors, extra, at)
        attended_grad, *output_terms = backward_output(middle_grad, keep, first_weights, factors, at)
        if layer_index == 0:
            terms[0] = [None, None, *output_terms, *feed_terms]
            summed.append(to_owners([(PACKED, terms[1]), (PACKED_EARLY, terms[0])]))
        query_grad, key_grads, value_grads = attend_backward(
            place, keep.queries, keep.keys, keep.values, attended_grad, keep.attended, keep.stat
        )
        grads = (
            query_grad,
            [key_grads[0], *ring_scatter(key_grads, count)],
            [value_grads[0], *ring_scatter(value_grads, count)],
        )
        grad_current, *attend_terms = backward_qkv(
            middle_grad, grads, keep, first_weights, factors, extra, at
        )
        terms[layer_index] = [*attend_terms, *output_terms, *feed_terms]
    summed.append(to_owners([(PACKED_LATE, terms[0])]))
    found = [[None] * len(sizes) for _ in range(LAYERS)]
    for held, orders in zip(summed, (((1, PACKED), (0, PACKED_EARLY)), ((0, PACKED_LATE),))):
        spot = 0
        for layer_index, order in orders:
            for kind, _ in order:
                found[layer_index][kind] = held[:, :, spot : spot + sizes[kind]]
                spot += sizes[kind]
    results = [
        jnp.swapaxes(jnp.stack([found[layer_index][kind] for layer_index in range(LAYERS)]), 2, 3)
        for kind in range(len(sizes))
    ]
    moved = collect_tokens(grad_current.astype(low_type), below, count)
    kept_part = collect_own(grad_current, below)
    return (outputs, jnp.where(kept_part[0], kept_part[1], moved.astype(wide)), *results)


def solution(mesh):
    count = mesh.shape["ctx"]
    inner = Mesh(mesh.devices.reshape(mesh.shape["dp"], count // 2, 2), EVERY)
    token_spec, factor_spec = P("dp", CTX, None), P(None, None, EVERY, None)
    in_specs = (
        (token_spec,) * 2 + (P(),) + (P(None, EVERY, None),) * 4 + (P(),) * 8 + (factor_spec,) * 8
    )
    out_specs = (token_spec,) * 2 + (factor_spec,) * 8
    return jax.shard_map(local, mesh=inner, in_specs=in_specs, out_specs=out_specs, check_vma=False)
```

```python
import functools

import jax
import jax.numpy as jnp
from jax import lax
from jax.experimental import pallas as pl
from jax.experimental.pallas import tpu as pltpu
from jax.sharding import Mesh
from jax.sharding import PartitionSpec as P

HEADS = 16
HEAD_DIM = 64
RANK = 16
ADAPTERS = 8
LAYERS = 2

WHOLE, PIECES, GATHERED, MIXED = range(4)
MICROSECOND = 10**8
BLK = 256

epsilon = 1e-05
root_factor = 0.7978845608028654
low_type = jnp.bfloat16
wide = jnp.float32

ROWS_BY_ROWS = (((1,), (1,)), ((), ()))
COLS_BY_COLS = (((0,), (0,)), ((), ()))
PLAIN = (((1,), (0,)), ((), ()))
EVERY = ("dp", "chip", "core")
LANE = ("dp", "chip")
CTX = ("chip", "core")


def times(left_side, right_side, dims=PLAIN):
    return lax.dot_general(left_side, right_side, dims, preferred_element_type=wide)


def block_steps(place, pieces):
    steps = [(0, 0, 0), (0, 1, 0), (0, 1, 1)]
    for piece in range(1, pieces):
        slot = jnp.where(place >= piece, 0, 1)
        steps += [(piece, slot, 0), (piece, 1, slot)]
    return steps


def block_rows(slot):
    return pl.ds(slot * BLK if isinstance(slot, int) else pl.multiple_of(slot * BLK, BLK), BLK)


def stack_heads(rows, mask):
    zero = jnp.zeros_like(rows)
    return jnp.concatenate([jnp.where(mask, rows, zero), jnp.where(mask, zero, rows)], axis=0)


def update_slot(held, slot, change):
    if isinstance(slot, int):
        return [change(member) if which == slot else member for which, member in enumerate(held)]
    return [jnp.where(slot == which, change(member), member) for which, member in enumerate(held)]


def pick_slot(held, slot):
    return held[slot] if isinstance(slot, int) else jnp.where(slot == 0, held[0], held[1])


def attend_forward_kernel(pieces, place_ref, q_ref, *refs):
    k_refs, v_refs = refs[:pieces], refs[pieces : 2 * pieces]
    o_ref, stat_ref, queries, scores, total = refs[2 * pieces :]
    mask = lax.broadcasted_iota(jnp.int32, (BLK, 2 * HEAD_DIM), 1) < HEAD_DIM
    for slot in range(2):
        queries[slot] = stack_heads(q_ref[block_rows(slot), :] * HEAD_DIM**-0.5, mask)
    steps = block_steps(place_ref[0], pieces)
    peaks = [jnp.full((1, 2 * BLK), -1e30, wide)] * 2
    for step, (piece, slot, key_slot) in enumerate(steps):
        block = times(k_refs[piece][block_rows(key_slot), :], queries[slot], ROWS_BY_ROWS)
        scores[step] = block
        top = jnp.max(block, axis=0, keepdims=True)
        peaks = update_slot(peaks, slot, lambda held, top=top: jnp.maximum(held, top))
    total[...] = jnp.zeros_like(total)
    sums = [jnp.zeros((1, 2 * BLK), wide)] * 2
    for step, (piece, slot, key_slot) in enumerate(steps):
        weights = jnp.exp(scores[step] - pick_slot(peaks, slot))
        part = jnp.sum(weights, axis=0, keepdims=True)
        sums = update_slot(sums, slot, lambda held, part=part: held + part)
        weights = weights.astype(low_type)
        turned = v_refs[piece][block_rows(key_slot), :].T
        total[slot] = total[slot] + jnp.concatenate(
            [
                times(turned[:HEAD_DIM], weights[:, :BLK]),
                times(turned[HEAD_DIM:], weights[:, BLK:]),
            ],
            axis=0,
        )
    for slot in range(2):
        share = 1.0 / sums[slot]
        held = total[slot]
        held = jnp.concatenate(
            [held[:HEAD_DIM] * share[:, :BLK], held[HEAD_DIM:] * share[:, BLK:]], axis=0
        )
        o_ref[block_rows(slot), :] = held.T
        stat_ref[0, slot : slot + 1, :] = peaks[slot] + jnp.log(sums[slot])


def attend_backward_kernel(pieces, place_ref, q_ref, g_ref, o_ref, stat_ref, *refs):
    k_refs, v_refs = refs[:pieces], refs[pieces : 2 * pieces]
    dq_ref, dk_refs, dv_refs = refs[2 * pieces], refs[2 * pieces + 1 : 3 * pieces + 1], refs[3 * pieces + 1 : 4 * pieces + 1]
    queries, grads, key_sum, value_sum, query_sum, inner = refs[4 * pieces + 1 :]
    mask = lax.broadcasted_iota(jnp.int32, (BLK, 2 * HEAD_DIM), 1) < HEAD_DIM
    for slot in range(2):
        rows = block_rows(slot)
        queries[slot] = stack_heads(q_ref[rows, :] * HEAD_DIM**-0.5, mask)
        grad = g_ref[rows, :]
        grads[slot] = stack_heads(grad, mask)
        both = (grad.astype(wide) * o_ref[rows, :]).T
        inner[slot] = jnp.concatenate(
            [
                jnp.sum(both[:HEAD_DIM], axis=0, keepdims=True),
                jnp.sum(both[HEAD_DIM:], axis=0, keepdims=True),
            ],
            axis=1,
        )
    key_sum[...] = jnp.zeros_like(key_sum)
    value_sum[...] = jnp.zeros_like(value_sum)
    query_sum[...] = jnp.zeros_like(query_sum)
    for piece, slot, key_slot in block_steps(place_ref[0], pieces):
        at = block_rows(key_slot)
        keys, values = k_refs[piece][at, :], v_refs[piece][at, :]
        own, grad = queries[slot], grads[slot]
        probs = jnp.exp(times(keys, own, ROWS_BY_ROWS) - stat_ref[0, pl.ds(slot, 1), :])
        dscores = probs * (times(values, grad, ROWS_BY_ROWS) - inner[slot])
        dscores = dscores.astype(low_type)
        value_sum[piece, at, :] = value_sum[piece, at, :] + times(probs.astype(low_type), grad)
        key_sum[piece, at, :] = key_sum[piece, at, :] + times(dscores, own)
        turned = keys.T
        query_sum[slot] = query_sum[slot] + jnp.concatenate(
            [
                times(turned[:HEAD_DIM], dscores[:, :BLK]),
                times(turned[HEAD_DIM:], dscores[:, BLK:]),
            ],
            axis=0,
        )
    for slot in range(2):
        dq_ref[block_rows(slot), :] = (query_sum[slot].T * HEAD_DIM**-0.5).astype(low_type)
    for piece in range(pieces):
        dk_refs[piece][...] = key_sum[piece].astype(low_type)
        dv_refs[piece][...] = value_sum[piece].astype(low_type)


def attention_specs():
    own = pl.BlockSpec((2 * BLK, 2 * HEAD_DIM), lambda pair, place: (0, pair))
    stats = pl.BlockSpec((1, 2, 2 * BLK), lambda pair, place: (pair, 0, 0))
    return own, stats


def attend_forward(place, queries, keys, values):
    pieces, pairs = len(keys), queries.shape[1] // (2 * HEAD_DIM)
    own, stats = attention_specs()
    return pl.pallas_call(
        functools.partial(attend_forward_kernel, pieces),
        out_shape=(
            jax.ShapeDtypeStruct(queries.shape, wide),
            jax.ShapeDtypeStruct((pairs, 2, 2 * BLK), wide),
        ),
        grid_spec=pltpu.PrefetchScalarGridSpec(
            num_scalar_prefetch=1,
            grid=(pairs,),
            in_specs=[own] * (1 + 2 * pieces),
            out_specs=[own, stats],
            scratch_shapes=[
                pltpu.VMEM((2, 2 * BLK, 2 * HEAD_DIM), low_type),
                pltpu.VMEM((2 * pieces + 1, BLK, 2 * BLK), wide),
                pltpu.VMEM((2, 2 * HEAD_DIM, BLK), wide),
            ],
        ),
        compiler_params=pltpu.CompilerParams(vmem_limit_bytes=48 * 2**20),
        cost_estimate=pl.CostEstimate(flops=13 * MICROSECOND, bytes_accessed=0, transcendentals=0),
        name="attend_forward",
    )(place, queries, *keys, *values)


def attend_backward(place, queries, keys, values, grads, attended, stat):
    pieces, pairs = len(keys), queries.shape[1] // (2 * HEAD_DIM)
    own, stats = attention_specs()
    query_grad, *others = pl.pallas_call(
        functools.partial(attend_backward_kernel, pieces),
        out_shape=(jax.ShapeDtypeStruct(queries.shape, low_type),) * (1 + 2 * pieces),
        grid_spec=pltpu.PrefetchScalarGridSpec(
            num_scalar_prefetch=1,
            grid=(pairs,),
            in_specs=[own, own, own, stats] + [own] * (2 * pieces),
            out_specs=[own] * (1 + 2 * pieces),
            scratch_shapes=[
                pltpu.VMEM((2, 2 * BLK, 2 * HEAD_DIM), low_type),
                pltpu.VMEM((2, 2 * BLK, 2 * HEAD_DIM), low_type),
                pltpu.VMEM((pieces, 2 * BLK, 2 * HEAD_DIM), wide),
                pltpu.VMEM((pieces, 2 * BLK, 2 * HEAD_DIM), wide),
                pltpu.VMEM((2, 2 * HEAD_DIM, BLK), wide),
                pltpu.VMEM((2, 1, 2 * BLK), wide),
            ],
        ),
        compiler_params=pltpu.CompilerParams(vmem_limit_bytes=48 * 2**20),
        cost_estimate=pl.CostEstimate(flops=21 * MICROSECOND, bytes_accessed=0, transcendentals=0),
        name="attend_backward",
    )(place, queries, grads, attended, stat, *keys, *values)
    return query_grad, others[:pieces], others[pieces:]


def spread_across(pair, below, count):
    half = count // 2
    across = [(b, half + b if b < half else count - 1 - b) for b in range(count)]
    return lax.ppermute(jnp.where(below, pair[1], pair[0]), CTX, across)


def spread_inside(pair, count):
    half = count // 2
    return lax.ppermute(pair[1], CTX, [(b, half + count - 1 - b) for b in range(half, count)])


def joined_tokens(pair, got, other, below):
    return jnp.concatenate(
        [jnp.where(below, pair[0], got), jnp.where(below, got, other)], axis=0
    )


def spread_tokens(pair, below, count):
    return joined_tokens(pair, spread_across(pair, below, count), spread_inside(pair, count), below)


def send_across(rows, below, count):
    half = count // 2
    across = [(half + b if b < half else count - 1 - b, b) for b in range(count)]
    return lax.ppermute(jnp.where(below, rows[BLK:], rows[:BLK]), CTX, across)


def send_inside(rows, count):
    half = count // 2
    inside = [(half + count - 1 - b, b) for b in range(half, count)]
    return lax.ppermute(rows[BLK:], CTX, inside)


def collect_tokens(rows, got, other, below):
    return jnp.stack([jnp.where(below, rows[:BLK], got), jnp.where(below, got, other)])


def collect_own(rows, below):
    mask = jnp.stack([below, jnp.zeros_like(below)])[:, None, None]
    return mask, jnp.stack([rows[:BLK], rows[:BLK]])


def ring_gather(rows, count):
    half = count // 2
    pieces = [rows]
    for step in range(1, half):
        pairs = [
            (side * half + b, side * half + (b + step) % half)
            for side in range(2)
            for b in range(half)
        ]
        pieces.append(lax.ppermute(rows, CTX, pairs))
    return pieces


def ring_scatter(pieces, count):
    half = count // 2
    arrived = []
    for step in range(1, half):
        pairs = [
            (side * half + b, side * half + (b - step) % half)
            for side in range(2)
            for b in range(half)
        ]
        arrived.append(lax.ppermute(pieces[step], CTX, pairs))
    return arrived


def add_up(members):
    return sum(member.astype(wide) for member in members).astype(low_type)


def ring_position(z):
    return jnp.where(z == 2, 3, jnp.where(z == 3, 2, z))


SWAP = [(0, 1), (1, 0)]
RING = [(z * 2 + x, after * 2 + x) for z, after in enumerate((1, 3, 0, 2)) for x in range(2)]
ACROSS_X = [(d, d ^ 1) for d in range(8)]


def along_z(rows):
    return lax.ppermute(rows, "dp", RING)


def along_x(rows):
    return lax.ppermute(rows, "dp", ACROSS_X)


def along_y(rows):
    return lax.ppermute(rows, "chip", SWAP)


def on_chip(rows):
    return lax.ppermute(rows, "core", SWAP)


def join(*members):
    return jnp.concatenate(members, axis=0)


def by_z(ring, first, rows, position):
    parts = [member[first : first + rows] for member in ring]
    placed = []
    for spot in (0, 1, 3, 2):
        step = lax.rem(position + 4 - spot, 4)
        chosen = parts[3]
        for index in (2, 1, 0):
            chosen = jnp.where(step == index, parts[index], chosen)
        placed.append(chosen)
    return jnp.stack(placed)


def z_halves(ring, position):
    size = ring[0].shape[0] // 2
    return [by_z(ring, part * size, size, position) for part in range(2)]


def cross(halves):
    return [along_x(halves[0]), along_y(halves[1])]


def cross_other(halves):
    return [along_y(halves[0]), along_x(halves[1])]


def paired(halves, crossed):
    return [jnp.stack([halves[part], crossed[part]]) for part in range(2)]


def swapped(members):
    return [on_chip(member) for member in members]


def linked_forward(
    first, second, chosen, tokens, cotangent, sizes, at, below, count, kept, attention_step, output_step, feed_step
):
    position = at[0]

    def gather(rows):
        whole = lax.all_gather(rows, EVERY, axis=0)
        return whole.reshape(4, 2, 2, 2, *rows.shape)

    v = Bag()
    v.f, v.g, v.h = [first[:128]], [second[:128]], [second[128:256]]
    first_feed, second_reduce = gather(first[128:]), gather(second[256:])

    def advance(ring):
        ring.append(along_z(ring[-1]))

    def mix(near, far):
        return near[0], far[0], near[1], far[1]

    def weights_f():
        return mix(v.f_near, v.f_far) + mix(v.f_near_other, v.f_far_other)

    def weights_g():
        return mix(v.g_near, v.g_far) + mix(v.g_near_other, v.g_far_other)

    def weights_h():
        return mix(v.h_near, v.h_far) + mix(v.h_near_other, v.h_far_other)

    for _ in range(3):
        advance(v.f)
    v.tokens = spread_tokens(tokens, below, count)
    v.chosen = chosen
    v = sync(v)
    v.f_half = z_halves(v.f, position)
    del v.f
    v.f_cross = cross(v.f_half)
    v.factors = lax.all_to_all(v.chosen, LANE, split_axis=0, concat_axis=0, tiled=True)
    del v.chosen
    advance(v.g)
    v = sync(v)
    v.f_near = paired(v.f_half, v.f_cross)
    del v.f_half, v.f_cross
    v.f_far = cross_other(v.f_near)
    v.f_near_other = swapped(v.f_near)
    v.factors_other = on_chip(v.factors)
    advance(v.g)
    advance(v.g)
    v = sync(v)
    v.g_half = z_halves(v.g, position)
    del v.g
    v.g_cross = cross(v.g_half)
    v.f_far_other = swapped(v.f_far)
    v.picked = unpack_factors(at, v.factors, v.factors_other, sizes)
    del v.factors, v.factors_other
    advance(v.h)
    v = sync(v)
    v.g_near = paired(v.g_half, v.g_cross)
    del v.g_half, v.g_cross
    v.g_far = cross_other(v.g_near)
    v.g_near_other = swapped(v.g_near)
    advance(v.h)
    advance(v.h)
    v.current = v.tokens.astype(wide)
    del v.tokens
    attention_step(v.current, (PIECES, weights_f()), v.picked[0], 0)
    v.middle = output_step(v.current, (PIECES, weights_f()), v.picked[0], 0)
    del v.current
    v.kept = kept
    v = sync(v)
    kept[:] = v.kept
    v.h_half = z_halves(v.h, position)
    del v.h
    v.h_cross = cross(v.h_half)
    v.g_far_other = swapped(v.g_far)
    v.current = feed_step(v.middle, (GATHERED, (first_feed,)), v.picked[0], 0)
    v.kept = kept
    v = sync(v)
    kept[:] = v.kept
    v.h_near = paired(v.h_half, v.h_cross)
    del v.h_half, v.h_cross
    v.h_far = cross_other(v.h_near)
    v.h_near_other = swapped(v.h_near)
    v.cotangent_other = spread_inside(cotangent, count)
    attention_step(v.current, (PIECES, weights_g()), v.picked[1], 1)
    v.middle = output_step(v.current, (PIECES, weights_g()), v.picked[1], 1)
    del v.current
    v.kept = kept
    v = sync(v)
    kept[:] = v.kept
    v.h_far_other = swapped(v.h_far)
    cotangent_got = spread_across(cotangent, below, count)
    frozen = [
        ((PIECES, weights_f()), (GATHERED, (first_feed,))),
        ((PIECES, weights_g()), (MIXED, (*weights_h(), second_reduce))),
    ]
    current = feed_step(v.middle, frozen[1][1], v.picked[1], 1)
    current, cotangent_got = sync((current, cotangent_got))
    cotangent = joined_tokens(cotangent, cotangent_got, v.cotangent_other, below)
    return current, cotangent.astype(wide), v.picked, frozen


SQUARE = (4, 2, 2, 2, 32, 1024)
TALL = (4, 2, 2, 2, 128, 1024)


def square_unit(form, part):
    return part if form == WHOLE else (part // 2, part % 2 * 32)


def expand_unit(form, part):
    return {WHOLE: part, GATHERED: 32 * part}.get(form, (part // 2, part % 2 * 32))


def fetch(form, at_ref, sources, unit, rows, held, arrived, by_quarter=None):
    spread_z = slice(None) if by_quarter is None else by_quarter
    if not isinstance(unit, tuple):
        if form == WHOLE:
            source = sources[unit].at[spread_z]
        else:
            source = sources[-1].at[(spread_z, *[slice(None)] * 3, pl.ds(unit, rows), slice(None))]
        pltpu.make_async_copy(source, held.at[spread_z], arrived).start()
        return
    part, first = unit
    x, y, core = at_ref[1], at_ref[2], at_ref[3]
    for other in range(2):
        for far in range(2):
            source = sources[other * 4 + part * 2 + far]
            for over in range(2):
                over_x, over_y = (over, far) if part == 0 else (far, over)
                pltpu.make_async_copy(
                    source.at[over, spread_z, pl.ds(first, rows), :],
                    held.at[
                        spread_z,
                        lax.rem(x + over_x, 2),
                        lax.rem(y + over_y, 2),
                        lax.rem(core + other, 2),
                    ],
                    arrived,
                ).start()


def wait_for(held, arrived):
    pltpu.make_async_copy(held, held, arrived).wait()


def square(held):
    return held[...].reshape(1024, 1024)


QKV_TILE, OUTPUT_TILE, FEED_TILE, FEED_BACK_TILE, OUTPUT_BACK_TILE, TURN_TILE, QKV_BACK_TILE = 0, 0, 512, 512, 0, 0, 0
STRIP = 64
QKV_ROWS, OUTPUT_ROWS, QKV_BACK_ROWS, FEED_BACK_ROWS = 256, 256, 256, 256
COLUMNS = 1024


def strips(count, body):
    def step(index, carry):
        body(pl.ds(pl.multiple_of(index * STRIP, STRIP), STRIP))
        return carry

    lax.fori_loop(0, count // STRIP, step, 0, unroll=True)


def normalize_rows(values, gain, shift):
    center = jnp.mean(values, axis=-1, keepdims=True)
    spread = values - center
    scale = lax.rsqrt(jnp.mean(spread * spread, axis=-1, keepdims=True) + epsilon)
    unit = spread * scale
    return unit, scale, unit * gain + shift


def normalize_pull(grad, unit, scale, gain):
    scaled = grad * gain
    first = jnp.mean(scaled, axis=-1, keepdims=True)
    second = jnp.mean(scaled * unit, axis=-1, keepdims=True)
    return scale * (scaled - first - unit * second)


def store_norm(values_ref, gain_ref, shift_ref, normed_ref, unit_ref, scale_ref):
    def norm(rows):
        unit, scale, normed = normalize_rows(values_ref[rows, :], gain_ref[...], shift_ref[...])
        normed_ref[rows, :] = normed.astype(low_type)
        unit_ref[rows, :] = unit.astype(low_type)
        scale_ref[rows, :] = jnp.broadcast_to(scale, (STRIP, 128))

    strips(values_ref.shape[0], norm)


def store_pull(out_ref, grad_ref, inner_ref, unit_ref, scale_ref, gain_ref):
    def pull(rows):
        out_ref[rows, :] = grad_ref[rows, :] + normalize_pull(
            inner_ref[rows, :], unit_ref[rows, :].astype(wide), scale_ref[rows, :1], gain_ref[...]
        )

    strips(out_ref.shape[0], pull)


def row_tiles(count, size):
    return [slice(first, first + size) for first in range(0, count, size)]


def span(part):
    return slice(part * COLUMNS, (part + 1) * COLUMNS)


TILED = [False]


def at_first(body):
    if TILED[0]:
        pl.when(pl.program_id(0) == 0)(body)
    else:
        body()


def at_last(body):
    if TILED[0]:
        pl.when(pl.program_id(0) == pl.num_programs(0) - 1)(body)
    else:
        body()


def await_first(held, arrived):
    at_first(lambda: wait_for(held, arrived))


def gather_sum(total, step_value):
    @at_first
    def _():
        total[...] = step_value

    if TILED[0]:

        @pl.when(pl.program_id(0) > 0)
        def _():
            total[...] = total[...] + step_value


def qkv_kernel(form, at_ref, x_ref, gain_ref, shift_ref, left_ref, right_ref, bias_ref, *refs):
    sources, (normed_ref, unit_ref, scale_ref, rank_ref, *outs) = refs[:-9], refs[-9:-2]
    held, arrived = refs[-2:]

    @at_first
    def _():
        for part in range(3):
            fetch(form, at_ref, sources, square_unit(form, part), 32, held.at[part], arrived.at[part])

    store_norm(x_ref, gain_ref, shift_ref, normed_ref, unit_ref, scale_ref)
    rank_ref[...] = times(normed_ref[...], left_ref[...], ROWS_BY_ROWS).astype(low_type)
    for part, out in enumerate(outs):
        await_first(held.at[part], arrived.at[part])
        for rows in row_tiles(out.shape[0], QKV_ROWS):
            out[rows, :] = (
                times(normed_ref[rows, :], square(held.at[part]))
                + times(rank_ref[rows, :], right_ref[:, span(part)])
                + bias_ref[:, span(part)]
            ).astype(low_type)


def output_kernel(form, at_ref, x_ref, attended_ref, left_ref, right_ref, bias_ref, gain_ref, shift_ref, *refs):
    sources, (low_ref, middle_ref, normed_ref, unit_ref, scale_ref, rank_ref) = refs[:-8], refs[-8:-2]
    held, arrived = refs[-2:]
    at_first(lambda: fetch(form, at_ref, sources, square_unit(form, 3), 32, held, arrived))
    low_ref[...] = attended_ref[...].astype(low_type)
    rank_ref[...] = times(low_ref[...], left_ref[...], ROWS_BY_ROWS).astype(low_type)
    await_first(held, arrived)
    for rows in row_tiles(x_ref.shape[0], OUTPUT_ROWS):
        middle_ref[rows, :] = (
            x_ref[rows, :]
            + times(low_ref[rows, :], square(held))
            + times(rank_ref[rows, :], right_ref[...])
            + bias_ref[...]
        )
    store_norm(middle_ref, gain_ref, shift_ref, normed_ref, unit_ref, scale_ref)


def fetch_feed_forward(form, at_ref, sources, expand, reduce, arrived, reduce_first):
    for part in range(4):
        jobs = [
            (expand_unit(form, part), 32, expand.at[part], arrived.at[0, part], None),
            ({WHOLE: 4, GATHERED: 128, MIXED: 0}[form], 128, reduce, arrived.at[1, part], part),
        ]
        for unit, rows, held, semaphore, quarter in jobs[::-1] if reduce_first else jobs:
            fetch(form, at_ref, sources, unit, rows, held, semaphore, quarter)


def feed_forward_kernel(
    form, at_ref, normed_ref, middle_ref, expand_left_ref, expand_right_ref, expand_bias_ref,
    reduce_left_ref, reduce_right_ref, reduce_bias_ref, *refs,
):
    sources, (result_ref, slope_ref, active_ref, rank_expand_ref, rank_reduce_ref) = refs[:-9], refs[-9:-4]
    expand, reduce, rank_sum, arrived = refs[-4:]
    at_first(lambda: fetch_feed_forward(form, at_ref, sources, expand, reduce, arrived, False))
    rank_expand_ref[...] = times(normed_ref[...], expand_left_ref[...], ROWS_BY_ROWS).astype(low_type)
    result_ref[...] = middle_ref[...] + reduce_bias_ref[...]
    rank_sum[...] = jnp.zeros_like(rank_sum)

    def part_step(part, carry):
        columns = pl.ds(pl.multiple_of(part * COLUMNS, COLUMNS), COLUMNS)
        await_first(expand.at[part], arrived.at[0, part])
        await_first(reduce.at[part], arrived.at[1, part])
        value = (
            times(normed_ref[...], square(expand.at[part]))
            + times(rank_expand_ref[...], expand_right_ref[:, columns])
            + expand_bias_ref[:, columns]
        )
        squared = value * value
        bent = jnp.tanh(value * (root_factor + 0.044715 * root_factor * squared))
        half = 0.5 + 0.5 * bent
        slope_ref[:, columns] = (
            half
            + value * (0.5 - 0.5 * bent * bent) * (root_factor + 3 * 0.044715 * root_factor * squared)
        ).astype(low_type)
        active = (value * half).astype(low_type)
        active_ref[:, columns] = active
        result_ref[...] = result_ref[...] + times(active, square(reduce.at[part]))
        rank_sum[...] = rank_sum[...] + times(active, reduce_left_ref[:, columns], ROWS_BY_ROWS)
        return carry

    lax.fori_loop(0, 4, part_step, 0)
    rank_reduce_ref[...] = rank_sum[...].astype(low_type)
    result_ref[...] = result_ref[...] + times(rank_reduce_ref[...], reduce_right_ref[...])


def feed_backward_kernel(
    form, at_ref, grad_ref, slope_ref, active_ref, normed_ref, unit_ref, scale_ref, rank_expand_ref, rank_reduce_ref,
    gain_ref, expand_left_ref, expand_right_ref, reduce_left_ref, reduce_right_ref, *refs,
):
    sources, (out_ref, *grads) = refs[:-17], refs[-17:-12]
    expand, reduce, arrived, low_grad, turned, bent, total, turn_sum, *sums = refs[-12:]
    expand_left_sum, expand_right_sum, reduce_left_sum, reduce_right_sum = sums
    at_first(lambda: fetch_feed_forward(form, at_ref, sources, expand, reduce, arrived, True))

    @at_first
    def _():
        for member in sums:
            member[...] = jnp.zeros_like(member)

    low_grad[...] = grad_ref[...].astype(low_type)
    turned[...] = times(low_grad[...], reduce_right_ref[...], ROWS_BY_ROWS).astype(low_type)
    reduce_right_sum[...] = reduce_right_sum[...] + times(rank_reduce_ref[...], low_grad[...], COLS_BY_COLS)
    total[...] = jnp.zeros_like(total)
    turn_sum[...] = jnp.zeros_like(turn_sum)

    def part_step(part, carry):
        columns = pl.ds(pl.multiple_of(part * COLUMNS, COLUMNS), COLUMNS)
        await_first(reduce.at[part], arrived.at[1, part])
        await_first(expand.at[part], arrived.at[0, part])
        for rows in row_tiles(grad_ref.shape[0], FEED_BACK_ROWS):
            grad_active = times(low_grad[rows, :], square(reduce.at[part]), ROWS_BY_ROWS) + times(
                turned[rows, :], reduce_left_ref[:, columns]
            )
            bent[rows, :] = (grad_active * slope_ref[rows, columns].astype(wide)).astype(low_type)
            total[rows, :] = total[rows, :] + times(bent[rows, :], square(expand.at[part]), ROWS_BY_ROWS)
        grad_expand = bent[...]
        turn_sum[...] = turn_sum[...] + times(grad_expand, expand_right_ref[:, columns], ROWS_BY_ROWS)
        reduce_left_sum[:, columns] = reduce_left_sum[:, columns] + times(
            turned[...], active_ref[:, columns], COLS_BY_COLS
        )
        expand_right_sum[:, columns] = expand_right_sum[:, columns] + times(
            rank_expand_ref[...], grad_expand, COLS_BY_COLS
        )
        return carry

    lax.fori_loop(0, 4, part_step, 0)
    turned[...] = turn_sum[...].astype(low_type)
    expand_left_sum[...] = expand_left_sum[...] + times(turned[...], normed_ref[...], COLS_BY_COLS)
    total[...] = total[...] + times(turned[...], expand_left_ref[...])
    store_pull(out_ref, grad_ref, total, unit_ref, scale_ref, gain_ref)

    @at_last
    def _():
        for member, summed in zip(grads, sums):
            member[...] = summed[...].astype(low_type)


def output_backward_kernel(form, at_ref, grad_ref, attended_ref, rank_ref, left_ref, right_ref, *refs):
    sources, (out_ref, left_g, right_g) = refs[:-7], refs[-7:-4]
    held, arrived, left_sum, right_sum = refs[-4:]
    at_first(lambda: fetch(form, at_ref, sources, square_unit(form, 3), 32, held, arrived))
    low_grad = grad_ref[...].astype(low_type)
    turned = times(low_grad, right_ref[...], ROWS_BY_ROWS).astype(low_type)
    gather_sum(right_sum, times(rank_ref[...], low_grad, COLS_BY_COLS))
    gather_sum(left_sum, times(turned, attended_ref[...], COLS_BY_COLS))
    await_first(held, arrived)
    out_ref[...] = (
        times(low_grad, square(held), ROWS_BY_ROWS) + times(turned, left_ref[...])
    ).astype(low_type)

    @at_last
    def _():
        left_g[...] = left_sum[...].astype(low_type)
        right_g[...] = right_sum[...].astype(low_type)


def qkv_turn_kernel(pieces, form, at_ref, normed_ref, rank_ref, dq_ref, *refs):
    dk_refs, dv_refs, (right_ref, *refs) = refs[:pieces], refs[pieces : 2 * pieces], refs[2 * pieces :]
    dk_ref, dv_ref, turned_ref, left_g, right_g, left_sum, right_sum = refs
    dk_ref[...] = add_up([member[...] for member in dk_refs])
    dv_ref[...] = add_up([member[...] for member in dv_refs])
    grads = (dq_ref, dk_ref, dv_ref)
    turned = sum(
        times(grads[part][...], right_ref[:, span(part)], ROWS_BY_ROWS) for part in range(3)
    ).astype(low_type)
    turned_ref[...] = turned
    gather_sum(left_sum, times(turned, normed_ref[...], COLS_BY_COLS))
    for part in range(3):
        gather_sum(right_sum.at[part], times(rank_ref[...], grads[part][...], COLS_BY_COLS))

    @at_last
    def _():
        left_g[...] = left_sum[...].astype(low_type)
        for part in range(3):
            right_g[:, span(part)] = right_sum[part].astype(low_type)


def qkv_backward_kernel(
    form, at_ref, grad_ref, unit_ref, scale_ref, turned_ref, dq_ref, dk_ref, dv_ref, gain_ref, left_ref, *refs
):
    sources, out_ref, (held, arrived, total) = refs[:-4], refs[-4], refs[-3:]

    @at_first
    def _():
        for part in range(3):
            fetch(form, at_ref, sources, square_unit(form, part), 32, held.at[part], arrived.at[part])

    total[...] = times(turned_ref[...], left_ref[...])
    for part, member in enumerate((dq_ref, dk_ref, dv_ref)):
        await_first(held.at[part], arrived.at[part])
        for rows in row_tiles(out_ref.shape[0], QKV_BACK_ROWS):
            total[rows, :] = total[rows, :] + times(member[rows, :], square(held.at[part]), ROWS_BY_ROWS)
    store_pull(out_ref, grad_ref, total, unit_ref, scale_ref, gain_ref)


def qkv_whole_kernel(
    pieces, form, at_ref, grad_ref, unit_ref, scale_ref, normed_ref, rank_ref, dq_ref, *refs
):
    dk_refs, dv_refs, (gain_ref, left_ref, right_ref, *refs) = refs[:pieces], refs[pieces : 2 * pieces], refs[2 * pieces :]
    sources, (out_ref, left_g, right_g) = refs[:-9], refs[-9:-6]
    held, arrived, turned, total, dk_ref, dv_ref = refs[-6:]
    for part in range(3):
        fetch(form, at_ref, sources, square_unit(form, part), 32, held.at[part], arrived.at[part])
    dk_ref[...] = add_up([member[...] for member in dk_refs])
    dv_ref[...] = add_up([member[...] for member in dv_refs])
    grads = (dq_ref, dk_ref, dv_ref)
    turned[...] = sum(
        times(grads[part][...], right_ref[:, span(part)], ROWS_BY_ROWS) for part in range(3)
    ).astype(low_type)
    for part in range(3):
        right_g[:, span(part)] = times(rank_ref[...], grads[part][...], COLS_BY_COLS).astype(low_type)
    left_g[...] = times(turned[...], normed_ref[...], COLS_BY_COLS).astype(low_type)
    for part, member in enumerate(grads):
        wait_for(held.at[part], arrived.at[part])
        for rows in row_tiles(out_ref.shape[0], QKV_BACK_ROWS):
            value = times(member[rows, :], square(held.at[part]), ROWS_BY_ROWS)
            before = total[rows, :] if part else times(turned[rows, :], left_ref[...])
            total[rows, :] = before + value
    store_pull(out_ref, grad_ref, total, unit_ref, scale_ref, gain_ref)


def frozen_call(kernel, name, at, weights, tile, tiled, fixed, outs, fixed_outs, scratch, cost):
    form, sources = weights
    count = tiled[0].shape[0]
    TILED[0] = tile > 0

    def by_rows(shape):
        if tile == 0:
            return pl.BlockSpec(memory_space=pltpu.VMEM)
        return pl.BlockSpec((tile, shape[1]), lambda step: (step, 0))

    def every(shape):
        if tile == 0:
            return pl.BlockSpec(memory_space=pltpu.VMEM)
        return pl.BlockSpec(shape, lambda step: (0, 0))

    return pl.pallas_call(
        functools.partial(kernel, form),
        grid=(count // tile,) if tile else (),
        out_shape=tuple(jax.ShapeDtypeStruct(shape, kind) for shape, kind in (*outs, *fixed_outs)),
        in_specs=[pl.BlockSpec(memory_space=pltpu.SMEM)]
        + [by_rows(member.shape) for member in tiled]
        + [every(member.shape) for member in fixed]
        + [pl.BlockSpec(memory_space=pl.ANY)] * len(sources),
        out_specs=tuple(by_rows(shape) for shape, _ in outs) + tuple(every(shape) for shape, _ in fixed_outs),
        scratch_shapes=scratch,
        compiler_params=pltpu.CompilerParams(vmem_limit_bytes=60 * 2**20),
        cost_estimate=pl.CostEstimate(flops=cost * MICROSECOND, bytes_accessed=0, transcendentals=0),
        name=name,
    )(at, *tiled, *fixed, *sources)


def row(vector):
    return vector.reshape(1, -1)


DMA = pltpu.SemaphoreType.DMA


PACKED = ((5, 0), (6, 128), (1, 256), (0, 352), (2, 384), (3, 416), (4, 448), (7, 480))


def unpack_kernel(order, at_ref, own_ref, other_ref, *outs):
    layers, groups = own_ref.shape[1], own_ref.shape[0] // 2
    swapped = at_ref[3] == 1
    for layer_index in range(layers):
        for group in range(groups):
            lanes = []
            for chip in range(2):
                own = own_ref[group * 2 + chip, layer_index]
                other = other_ref[group * 2 + chip, layer_index]
                lanes += [jnp.where(swapped, other, own), jnp.where(swapped, own, other)]
            for kind, first in order:
                out = outs[layer_index * len(order) + kind]
                size = out.shape[1] // (4 * groups)
                out[:, group * 4 * size : (group + 1) * 4 * size] = jnp.concatenate(
                    [lane[:, first : first + size] for lane in lanes], axis=1
                )


def unpack_factors(at, own, other, sizes):
    lanes, layers = own.shape[:2]
    local_spec = pl.BlockSpec(memory_space=pltpu.VMEM)
    found = pl.pallas_call(
        functools.partial(unpack_kernel, PACKED),
        out_shape=tuple(
            jax.ShapeDtypeStruct((RANK, size * lanes * 2), low_type) for _ in range(layers) for size in sizes
        ),
        in_specs=[pl.BlockSpec(memory_space=pltpu.SMEM), local_spec, local_spec],
        out_specs=(local_spec,) * (layers * len(sizes)),
        compiler_params=pltpu.CompilerParams(vmem_limit_bytes=32 * 2**20),
        cost_estimate=pl.CostEstimate(flops=4 * MICROSECOND, bytes_accessed=0, transcendentals=0),
        name="unpack_factors",
    )(at, own, other)
    return [found[layer * len(sizes) : (layer + 1) * len(sizes)] for layer in range(layers)]


def pack_kernel(orders, at_ref, *refs):
    members, out_ref = refs[:-1], refs[-1]
    core, base, offset = at_ref[3], 0, 0
    for order in orders:
        for lane_chip in range(out_ref.shape[1]):
            for owner_core in range(2):
                owner = lane_chip * 2 + owner_core
                parts = []
                for index, _ in enumerate(order):
                    member = members[base + index]
                    size = member.shape[1] // (2 * out_ref.shape[1])
                    parts.append(member[:, owner * size : (owner + 1) * size])
                joined = jnp.concatenate(parts, axis=1)
                out_ref[lax.rem(owner_core + core, 2), lane_chip, :, offset : offset + joined.shape[1]] = joined
        base += len(order)
        offset += joined.shape[1]


def pack_gradients(at, groups, lanes):
    members, width = [], 0
    for order, terms in groups:
        members += [terms[kind] for kind, _ in order]
        width += sum(terms[kind].shape[1] for kind, _ in order) // (2 * lanes)
    local_spec = pl.BlockSpec(memory_space=pltpu.VMEM)
    return pl.pallas_call(
        functools.partial(pack_kernel, [order for order, _ in groups]),
        out_shape=jax.ShapeDtypeStruct((2, lanes, RANK, width), low_type),
        in_specs=[pl.BlockSpec(memory_space=pltpu.SMEM)] + [local_spec] * len(members),
        out_specs=local_spec,
        compiler_params=pltpu.CompilerParams(vmem_limit_bytes=32 * 2**20),
        cost_estimate=pl.CostEstimate(flops=4 * MICROSECOND, bytes_accessed=0, transcendentals=0),
        name="pack_gradients",
    )(at, *members)


LOW, WIDE = low_type, wide


def forward_qkv(current, weights, picked, extras, at):
    rows, columns = current.shape
    full_low = ((rows, columns), LOW)
    bias = jnp.concatenate([extras[0][:columns], jnp.zeros((columns,), WIDE), extras[0][columns:]])
    return frozen_call(
        qkv_kernel, "qkv_forward", at, weights, QKV_TILE, (current,),
        (row(extras[4]), row(extras[5]), picked[0], picked[1], row(bias)),
        (full_low, full_low, ((rows, 128), WIDE), ((rows, RANK), LOW), full_low, full_low, full_low), (),
        [pltpu.VMEM((3, *SQUARE), LOW), DMA((3,))], 9,
    )


def forward_output(current, attended, weights, picked, extras, at):
    rows, columns = current.shape
    full, full_low = ((rows, columns), WIDE), ((rows, columns), LOW)
    return frozen_call(
        output_kernel, "output_forward", at, weights, OUTPUT_TILE, (current, attended),
        (picked[2], picked[3], row(extras[1]), row(extras[6]), row(extras[7])),
        (full_low, full, full_low, full_low, ((rows, 128), WIDE), ((rows, RANK), LOW)), (),
        [pltpu.VMEM(SQUARE, LOW), DMA], 8,
    )


def forward_feed(normed, middle, weights, picked, extras, at):
    rows, columns = middle.shape
    tall, ranks = ((rows, picked[5].shape[1]), LOW), ((rows, RANK), LOW)
    return frozen_call(
        feed_forward_kernel, "feed_forward", at, weights, FEED_TILE, (normed, middle),
        (picked[4], picked[5], row(extras[2]), picked[6], picked[7], row(extras[3])),
        (((rows, columns), WIDE), tall, tall, ranks, ranks), (),
        [
            pltpu.VMEM((4, *SQUARE), LOW), pltpu.VMEM(TALL, LOW), pltpu.VMEM((FEED_TILE or rows, RANK), WIDE),
            DMA((2, 4)),
        ], 20,
    )


def like(member):
    return (member.shape, LOW)


def backward_feed(grad, kept, weights, picked, extras, at):
    rows, columns = grad.shape
    tile = FEED_BACK_TILE or rows
    return frozen_call(
        feed_backward_kernel, "feed_backward", at, weights, FEED_BACK_TILE,
        (
            grad, kept.slope, kept.active, kept.normed_two, kept.unit_two, kept.scale_two,
            kept.rank_expand, kept.rank_reduce,
        ),
        (row(extras[6]), *picked[4:]), (((rows, columns), WIDE),), tuple(map(like, picked[4:])),
        [
            pltpu.VMEM((4, *SQUARE), LOW), pltpu.VMEM(TALL, LOW), DMA((2, 4)),
            pltpu.VMEM((tile, columns), LOW), pltpu.VMEM((tile, RANK), LOW), pltpu.VMEM((tile, columns), LOW),
            pltpu.VMEM((tile, columns), WIDE), pltpu.VMEM((tile, RANK), WIDE),
        ]
        + [pltpu.VMEM(member.shape, WIDE) for member in picked[4:]], 22,
    )


def backward_output(grad, kept, weights, picked, at):
    rows, columns = grad.shape
    return frozen_call(
        output_backward_kernel, "output_backward", at, weights, OUTPUT_BACK_TILE,
        (grad, kept.attended_low, kept.rank_output), (picked[2], picked[3]),
        (((rows, columns), LOW),), (like(picked[2]), like(picked[3])),
        [pltpu.VMEM(SQUARE, LOW), DMA, pltpu.VMEM(picked[2].shape, WIDE), pltpu.VMEM(picked[3].shape, WIDE)], 5,
    )


def backward_turn(grads, kept, picked, at):
    query_grad, key_grads, value_grads = grads
    full_low = (query_grad.shape, LOW)
    return frozen_call(
        functools.partial(qkv_turn_kernel, len(key_grads)), "qkv_turn", at, (WHOLE, ()), TURN_TILE,
        (kept.normed_one, kept.rank_attend, query_grad, *key_grads, *value_grads), (picked[1],),
        (full_low, full_low, like(kept.rank_attend)), (like(picked[0]), like(picked[1])),
        [pltpu.VMEM(picked[0].shape, WIDE), pltpu.VMEM((3, *picked[0].shape), WIDE)], 3,
    )


def backward_qkv_whole(grad, grads, kept, weights, picked, extras, at):
    rows, columns = grad.shape
    query_grad, key_grads, value_grads = grads
    return frozen_call(
        functools.partial(qkv_whole_kernel, len(key_grads)), "qkv_whole", at, weights, 0,
        (
            grad, kept.unit_one, kept.scale_one, kept.normed_one, kept.rank_attend, query_grad, *key_grads,
            *value_grads,
        ),
        (row(extras[4]), picked[0], picked[1]),
        (((rows, columns), WIDE),), (like(picked[0]), like(picked[1])),
        [
            pltpu.VMEM((3, *SQUARE), LOW), DMA((3,)), pltpu.VMEM((rows, RANK), LOW),
            pltpu.VMEM((rows, columns), WIDE), pltpu.VMEM((rows, columns), LOW), pltpu.VMEM((rows, columns), LOW),
        ], 11,
    )


def backward_qkv(grad, joined, turned, kept, weights, picked, extras, at):
    rows, columns = grad.shape
    return frozen_call(
        qkv_backward_kernel, "qkv_backward", at, weights, QKV_BACK_TILE,
        (grad, kept.unit_one, kept.scale_one, turned, *joined), (row(extras[4]), picked[0]),
        (((rows, columns), WIDE),), (),
        [pltpu.VMEM((3, *SQUARE), LOW), DMA((3,)), pltpu.VMEM((QKV_BACK_TILE or rows, columns), WIDE)], 9,
    )[0]


def combine_kernel(places, ids_ref, *refs):
    count = len(places)
    received, outs, total = refs[:count], refs[count:-1], refs[-1]
    total[...] = jnp.zeros_like(total)
    for source in range(received[0].shape[0]):
        adapter, spot = ids_ref[source], 0
        for member in received:
            width = member.shape[2]
            at = (adapter, slice(None), slice(spot, spot + width))
            total[at] = total[at] + member[source].astype(wide)
            spot += width
    base = 0
    for member, orders in zip(received, places):
        for layer_index, order in orders:
            for kind, _ in order:
                size = outs[kind].shape[3]
                outs[kind][layer_index] = total[:, :, base : base + size]
                base += size


def combine(ids, received, places, sizes):
    local_spec = pl.BlockSpec(memory_space=pltpu.VMEM)
    width = sum(member.shape[2] for member in received)
    return pl.pallas_call(
        functools.partial(combine_kernel, places),
        out_shape=tuple(jax.ShapeDtypeStruct((LAYERS, ADAPTERS, RANK, size), wide) for size in sizes),
        in_specs=[pl.BlockSpec(memory_space=pltpu.SMEM)] + [local_spec] * len(received),
        out_specs=(local_spec,) * len(sizes),
        scratch_shapes=[pltpu.VMEM((ADAPTERS, RANK, width), wide)],
        compiler_params=pltpu.CompilerParams(vmem_limit_bytes=32 * 2**20),
        cost_estimate=pl.CostEstimate(flops=3 * MICROSECOND, bytes_accessed=0, transcendentals=0),
        name="combine",
    )(ids, *received)


class Bag:
    pass


def open_bag(bag):
    names = tuple(sorted(vars(bag)))
    return tuple(getattr(bag, name) for name in names), names


def close_bag(names, members):
    bag = Bag()
    for name, member in zip(names, members):
        setattr(bag, name, member)
    return bag


jax.tree_util.register_pytree_node(Bag, open_bag, close_bag)


def sync(values):
    leaves, shape = jax.tree.flatten(values)
    return jax.tree.unflatten(shape, lax.optimization_barrier(tuple(leaves)))


def local(
    tokens, cotangent, adapter_ids, attend_weight, output_weight, expand_weight, reduce_weight,
    attend_bias, output_bias, expand_bias, reduce_bias, first_gain, first_shift, second_gain, second_shift,
    *adapters,
):
    data_count, chips = lax.axis_size("dp"), lax.axis_size("chip")
    count = chips * lax.axis_size("core")
    half = count // 2
    devices = data_count * count
    data_rank, core = lax.axis_index("dp"), lax.axis_index("core")
    rank = lax.axis_index("chip") * 2 + core
    below = rank < half
    place = jnp.reshape(lax.rem(rank, half), (1,)).astype(jnp.int32)
    columns = tokens.shape[2]
    linked = (data_count, chips, columns) == (8, 2, 1024)

    lane_chip = jnp.arange(data_count * chips, dtype=jnp.int32)
    lane_sequence = (lane_chip // chips) * 2 + (lane_chip % chips) // (chips // 2)
    lane_adapter = jnp.take(adapter_ids, lane_sequence)

    sizes = [member.shape[2] for member in adapters]
    packed = jnp.concatenate([jnp.swapaxes(adapters[kind], 2, 3) for kind, _ in PACKED], axis=3)
    chosen = jnp.moveaxis(jnp.take(packed, lane_adapter, axis=1), 1, 0)

    def shards(layer_index):
        lists = [attend_weight[layer_index], output_weight[layer_index], expand_weight[layer_index]]
        blocks = [
            member[:, first : first + columns]
            for member in lists
            for first in range(0, member.shape[1], columns)
        ]
        return jnp.concatenate(blocks + [reduce_weight[layer_index]], axis=0)

    extras = [
        tuple(
            member[layer_index]
            for member in (
                attend_bias, output_bias, expand_bias, reduce_bias,
                first_gain, first_shift, second_gain, second_shift,
            )
        )
        for layer_index in range(LAYERS)
    ]
    position = ring_position(data_rank // 2)
    at = jnp.stack([position, data_rank % 2, lax.axis_index("chip"), core]).astype(jnp.int32)
    kept = [Bag(), Bag()]

    def attention_step(current, weights, picked, layer_index):
        keep = kept[layer_index]
        (
            keep.normed_one, keep.unit_one, keep.scale_one, keep.rank_attend,
            keep.queries, keys, values,
        ) = forward_qkv(current, weights, picked, extras[layer_index], at)
        keep.keys, keep.values = ring_gather(keys, count), ring_gather(values, count)
        keep.attended, keep.stat = attend_forward(place, keep.queries, keep.keys, keep.values)

    def output_step(current, weights, picked, layer_index):
        keep = kept[layer_index]
        (
            keep.attended_low, middle, keep.normed_two, keep.unit_two, keep.scale_two,
            keep.rank_output,
        ) = forward_output(current, keep.attended, weights, picked, extras[layer_index], at)
        return middle

    def feed_step(middle, weights, picked, layer_index):
        keep = kept[layer_index]
        result, keep.slope, keep.active, keep.rank_expand, keep.rank_reduce = forward_feed(
            keep.normed_two, middle, weights, picked, extras[layer_index], at
        )
        return result

    if linked:
        first, second = shards(0), shards(1)
        current, grad_current, picked, frozen = linked_forward(
            first, second, chosen, tokens, cotangent, sizes, at, below, count, kept,
            attention_step, output_step, feed_step,
        )
    else:
        current = spread_tokens(tokens, below, count).astype(wide)
        grad_current = spread_tokens(cotangent, below, count).astype(wide)
        mine = lax.all_to_all(chosen, LANE, split_axis=0, concat_axis=0, tiled=True)
        theirs = lax.ppermute(mine, "core", SWAP)
        both = jnp.stack(
            [jnp.where(core == 0, mine, theirs), jnp.where(core == 0, theirs, mine)], axis=1
        )
        places, spot = {}, 0
        for kind, _ in PACKED:
            places[kind] = spot
            spot += sizes[kind]
        picked = [
            tuple(
                jnp.transpose(
                    both[:, :, layer_index, :, places[kind] : places[kind] + size], (2, 0, 1, 3)
                ).reshape(RANK, devices * size)
                for kind, size in enumerate(sizes)
            )
            for layer_index in range(LAYERS)
        ]
        frozen = []
        for layer_index in range(LAYERS):
            whole = lax.all_gather(shards(layer_index), EVERY, axis=0)
            size = columns // devices
            squares = [whole[:, part * size : (part + 1) * size, :].reshape(SQUARE) for part in range(8)]
            tall = whole[:, 8 * size :, :].reshape(TALL)
            frozen.append(((WHOLE, tuple(squares[:4])), (WHOLE, (*squares[4:], tall))))
            first_weights, second_weights = frozen[layer_index]
            attention_step(current, first_weights, picked[layer_index], layer_index)
            middle = output_step(current, first_weights, picked[layer_index], layer_index)
            current = feed_step(middle, second_weights, picked[layer_index], layer_index)

    result = current.astype(low_type)
    result_got, result_other = send_across(result, below, count), send_inside(result, count)
    lanes = data_count * chips

    def to_owners(groups):
        if linked:
            both = pack_gradients(at, groups, lanes)
            own, sent = both[0], both[1]
        else:
            both = jnp.concatenate(
                [
                    jnp.transpose(
                        terms[kind].reshape(RANK, lanes, 2, sizes[kind]), (2, 1, 0, 3)
                    )
                    for order, terms in groups
                    for kind, _ in order
                ],
                axis=3,
            )
            own, sent = jnp.where(core == 0, both[0], both[1]), jnp.where(core == 0, both[1], both[0])
        total = add_up([own, lax.ppermute(sent, "core", SWAP)])
        return lax.all_to_all(total, LANE, split_axis=0, concat_axis=0, tiled=True)

    terms = [None] * LAYERS
    for layer_index in reversed(range(LAYERS)):
        keep, extra, factors = kept[layer_index], extras[layer_index], picked[layer_index]
        first_weights, second_weights = frozen[layer_index]
        middle_grad, *feed_terms = backward_feed(grad_current, keep, second_weights, factors, extra, at)
        if layer_index == LAYERS - 1:
            middle_grad, feed_terms, result_got = sync((middle_grad, feed_terms, result_got))
        attended_grad, *output_terms = backward_output(middle_grad, keep, first_weights, factors, at)
        query_grad, key_grads, value_grads = attend_backward(
            place, keep.queries, keep.keys, keep.values, attended_grad, keep.attended, keep.stat
        )
        if layer_index == LAYERS - 1:
            query_grad, key_grads, value_grads, result_other = sync(
                (query_grad, key_grads, value_grads, result_other)
            )
        grads = (
            query_grad,
            [key_grads[0], *ring_scatter(key_grads, count)],
            [value_grads[0], *ring_scatter(value_grads, count)],
        )
        if layer_index > 0:
            grad_current, *attend_terms = backward_qkv_whole(
                middle_grad, grads, keep, first_weights, factors, extra, at
            )
            terms[layer_index] = [*attend_terms, *output_terms, *feed_terms]
            continue
        key_grad, value_grad, turned, *attend_terms = backward_turn(grads, keep, factors, at)
        terms[layer_index] = [*attend_terms, *output_terms, *feed_terms]
        received = to_owners([(PACKED, terms[1]), (PACKED, terms[0])])
        grad_current = backward_qkv(
            middle_grad, (query_grad, key_grad, value_grad), turned, keep, first_weights, factors, extra, at
        )
        received, grad_current = sync((received, grad_current))
    low_grad = grad_current.astype(low_type)
    moved = collect_tokens(low_grad, send_across(low_grad, below, count), send_inside(low_grad, count), below)
    kept_part = collect_own(grad_current, below)
    received = [received]
    places = (((1, PACKED), (0, PACKED)),)
    if linked:
        results = combine(lane_adapter, received, places, sizes)
    else:
        owner_adapter = (lane_adapter[:, None] == jnp.arange(ADAPTERS)[None, :]).astype(wide)
        found = [[None] * len(sizes) for _ in range(LAYERS)]
        for held, orders in zip(received, places):
            summed = jnp.einsum(
                "sa,srp->arp", owner_adapter, held.astype(wide), precision=lax.Precision.HIGHEST
            )
            spot = 0
            for layer_index, order in orders:
                for kind, _ in order:
                    found[layer_index][kind] = summed[:, :, spot : spot + sizes[kind]]
                    spot += sizes[kind]
        results = [
            jnp.stack([found[layer_index][kind] for layer_index in range(LAYERS)])
            for kind in range(len(sizes))
        ]
    return (
        collect_tokens(result, result_got, result_other, below),
        jnp.where(kept_part[0], kept_part[1], moved.astype(wide)),
        *[jnp.swapaxes(member, 2, 3) for member in results],
    )


def solution(mesh):
    count = mesh.shape["ctx"]
    inner = Mesh(mesh.devices.reshape(mesh.shape["dp"], count // 2, 2), EVERY)
    token_spec, factor_spec = P("dp", CTX, None), P(None, None, EVERY, None)
    in_specs = (
        (token_spec,) * 2 + (P(),) + (P(None, EVERY, None),) * 4 + (P(),) * 8 + (factor_spec,) * 8
    )
    out_specs = (token_spec,) * 2 + (factor_spec,) * 8
    return jax.shard_map(local, mesh=inner, in_specs=in_specs, out_specs=out_specs, check_vma=False)
```

```python
import functools

import jax
import jax.numpy as jnp
from jax import lax
from jax.experimental import pallas as pl
from jax.experimental.pallas import tpu as pltpu
from jax.sharding import Mesh
from jax.sharding import PartitionSpec as P

HEADS = 16
HEAD_DIM = 64
RANK = 16
ADAPTERS = 8
LAYERS = 2

WHOLE, PIECES, GATHERED, MIXED = range(4)
MICROSECOND = 10**8
BLK = 256

epsilon = 1e-05
root_factor = 0.7978845608028654
low_type = jnp.bfloat16
wide = jnp.float32

ROWS_BY_ROWS = (((1,), (1,)), ((), ()))
COLS_BY_COLS = (((0,), (0,)), ((), ()))
PLAIN = (((1,), (0,)), ((), ()))
EVERY = ("dp", "chip", "core")
LANE = ("dp", "chip")
CTX = ("chip", "core")


def times(left_side, right_side, dims=PLAIN):
    return lax.dot_general(left_side, right_side, dims, preferred_element_type=wide)


def block_steps(place, pieces):
    steps = [(0, 0, 0), (0, 1, 0), (0, 1, 1)]
    for piece in range(1, pieces):
        slot = jnp.where(place >= piece, 0, 1)
        steps += [(piece, slot, 0), (piece, 1, slot)]
    return steps


def block_rows(slot):
    return pl.ds(slot * BLK if isinstance(slot, int) else pl.multiple_of(slot * BLK, BLK), BLK)


def stack_heads(rows, mask):
    zero = jnp.zeros_like(rows)
    return jnp.concatenate([jnp.where(mask, rows, zero), jnp.where(mask, zero, rows)], axis=0)


def update_slot(held, slot, change):
    if isinstance(slot, int):
        return [change(member) if which == slot else member for which, member in enumerate(held)]
    return [jnp.where(slot == which, change(member), member) for which, member in enumerate(held)]


def pick_slot(held, slot):
    return held[slot] if isinstance(slot, int) else jnp.where(slot == 0, held[0], held[1])


def attend_forward_kernel(pieces, place_ref, q_ref, *refs):
    k_refs, v_refs = refs[:pieces], refs[pieces : 2 * pieces]
    o_ref, stat_ref, queries, scores, total = refs[2 * pieces :]
    mask = lax.broadcasted_iota(jnp.int32, (BLK, 2 * HEAD_DIM), 1) < HEAD_DIM
    for slot in range(2):
        queries[slot] = stack_heads(q_ref[block_rows(slot), :] * HEAD_DIM**-0.5, mask)
    steps = block_steps(place_ref[0], pieces)
    peaks = [jnp.full((1, 2 * BLK), -1e30, wide)] * 2
    for step, (piece, slot, key_slot) in enumerate(steps):
        block = times(k_refs[piece][block_rows(key_slot), :], queries[slot], ROWS_BY_ROWS)
        scores[step] = block
        top = jnp.max(block, axis=0, keepdims=True)
        peaks = update_slot(peaks, slot, lambda held, top=top: jnp.maximum(held, top))
    total[...] = jnp.zeros_like(total)
    sums = [jnp.zeros((1, 2 * BLK), wide)] * 2
    for step, (piece, slot, key_slot) in enumerate(steps):
        weights = jnp.exp(scores[step] - pick_slot(peaks, slot))
        part = jnp.sum(weights, axis=0, keepdims=True)
        sums = update_slot(sums, slot, lambda held, part=part: held + part)
        weights = weights.astype(low_type)
        turned = v_refs[piece][block_rows(key_slot), :].T
        total[slot] = total[slot] + jnp.concatenate(
            [
                times(turned[:HEAD_DIM], weights[:, :BLK]),
                times(turned[HEAD_DIM:], weights[:, BLK:]),
            ],
            axis=0,
        )
    for slot in range(2):
        share = 1.0 / sums[slot]
        held = total[slot]
        held = jnp.concatenate(
            [held[:HEAD_DIM] * share[:, :BLK], held[HEAD_DIM:] * share[:, BLK:]], axis=0
        )
        o_ref[block_rows(slot), :] = held.T
        stat_ref[0, slot : slot + 1, :] = peaks[slot] + jnp.log(sums[slot])


def attend_backward_kernel(pieces, place_ref, q_ref, g_ref, o_ref, stat_ref, *refs):
    k_refs, v_refs = refs[:pieces], refs[pieces : 2 * pieces]
    dq_ref, dk_refs, dv_refs = refs[2 * pieces], refs[2 * pieces + 1 : 3 * pieces + 1], refs[3 * pieces + 1 : 4 * pieces + 1]
    queries, grads, key_sum, value_sum, query_sum, inner = refs[4 * pieces + 1 :]
    mask = lax.broadcasted_iota(jnp.int32, (BLK, 2 * HEAD_DIM), 1) < HEAD_DIM
    for slot in range(2):
        rows = block_rows(slot)
        queries[slot] = stack_heads(q_ref[rows, :] * HEAD_DIM**-0.5, mask)
        grad = g_ref[rows, :]
        grads[slot] = stack_heads(grad, mask)
        both = (grad.astype(wide) * o_ref[rows, :]).T
        inner[slot] = jnp.concatenate(
            [
                jnp.sum(both[:HEAD_DIM], axis=0, keepdims=True),
                jnp.sum(both[HEAD_DIM:], axis=0, keepdims=True),
            ],
            axis=1,
        )
    key_sum[...] = jnp.zeros_like(key_sum)
    value_sum[...] = jnp.zeros_like(value_sum)
    query_sum[...] = jnp.zeros_like(query_sum)
    for piece, slot, key_slot in block_steps(place_ref[0], pieces):
        at = block_rows(key_slot)
        keys, values = k_refs[piece][at, :], v_refs[piece][at, :]
        own, grad = queries[slot], grads[slot]
        probs = jnp.exp(times(keys, own, ROWS_BY_ROWS) - stat_ref[0, pl.ds(slot, 1), :])
        dscores = probs * (times(values, grad, ROWS_BY_ROWS) - inner[slot])
        dscores = dscores.astype(low_type)
        value_sum[piece, at, :] = value_sum[piece, at, :] + times(probs.astype(low_type), grad)
        key_sum[piece, at, :] = key_sum[piece, at, :] + times(dscores, own)
        turned = keys.T
        query_sum[slot] = query_sum[slot] + jnp.concatenate(
            [
                times(turned[:HEAD_DIM], dscores[:, :BLK]),
                times(turned[HEAD_DIM:], dscores[:, BLK:]),
            ],
            axis=0,
        )
    for slot in range(2):
        dq_ref[block_rows(slot), :] = (query_sum[slot].T * HEAD_DIM**-0.5).astype(low_type)
    for piece in range(pieces):
        dk_refs[piece][...] = key_sum[piece].astype(low_type)
        dv_refs[piece][...] = value_sum[piece].astype(low_type)


def attention_specs():
    own = pl.BlockSpec((2 * BLK, 2 * HEAD_DIM), lambda pair, place: (0, pair))
    stats = pl.BlockSpec((1, 2, 2 * BLK), lambda pair, place: (pair, 0, 0))
    return own, stats


def attend_forward(place, queries, keys, values):
    pieces, pairs = len(keys), queries.shape[1] // (2 * HEAD_DIM)
    own, stats = attention_specs()
    return pl.pallas_call(
        functools.partial(attend_forward_kernel, pieces),
        out_shape=(
            jax.ShapeDtypeStruct(queries.shape, wide),
            jax.ShapeDtypeStruct((pairs, 2, 2 * BLK), wide),
        ),
        grid_spec=pltpu.PrefetchScalarGridSpec(
            num_scalar_prefetch=1,
            grid=(pairs,),
            in_specs=[own] * (1 + 2 * pieces),
            out_specs=[own, stats],
            scratch_shapes=[
                pltpu.VMEM((2, 2 * BLK, 2 * HEAD_DIM), low_type),
                pltpu.VMEM((2 * pieces + 1, BLK, 2 * BLK), wide),
                pltpu.VMEM((2, 2 * HEAD_DIM, BLK), wide),
            ],
        ),
        compiler_params=pltpu.CompilerParams(vmem_limit_bytes=48 * 2**20),
        cost_estimate=pl.CostEstimate(flops=13 * MICROSECOND, bytes_accessed=0, transcendentals=0),
        name="attend_forward",
    )(place, queries, *keys, *values)


def attend_backward(place, queries, keys, values, grads, attended, stat):
    pieces, pairs = len(keys), queries.shape[1] // (2 * HEAD_DIM)
    own, stats = attention_specs()
    query_grad, *others = pl.pallas_call(
        functools.partial(attend_backward_kernel, pieces),
        out_shape=(jax.ShapeDtypeStruct(queries.shape, low_type),) * (1 + 2 * pieces),
        grid_spec=pltpu.PrefetchScalarGridSpec(
            num_scalar_prefetch=1,
            grid=(pairs,),
            in_specs=[own, own, own, stats] + [own] * (2 * pieces),
            out_specs=[own] * (1 + 2 * pieces),
            scratch_shapes=[
                pltpu.VMEM((2, 2 * BLK, 2 * HEAD_DIM), low_type),
                pltpu.VMEM((2, 2 * BLK, 2 * HEAD_DIM), low_type),
                pltpu.VMEM((pieces, 2 * BLK, 2 * HEAD_DIM), wide),
                pltpu.VMEM((pieces, 2 * BLK, 2 * HEAD_DIM), wide),
                pltpu.VMEM((2, 2 * HEAD_DIM, BLK), wide),
                pltpu.VMEM((2, 1, 2 * BLK), wide),
            ],
        ),
        compiler_params=pltpu.CompilerParams(vmem_limit_bytes=48 * 2**20),
        cost_estimate=pl.CostEstimate(flops=21 * MICROSECOND, bytes_accessed=0, transcendentals=0),
        name="attend_backward",
    )(place, queries, grads, attended, stat, *keys, *values)
    return query_grad, others[:pieces], others[pieces:]


def spread_across(pair, below, count):
    half = count // 2
    across = [(b, half + b if b < half else count - 1 - b) for b in range(count)]
    return lax.ppermute(jnp.where(below, pair[1], pair[0]), CTX, across)


def spread_inside(pair, count):
    half = count // 2
    return lax.ppermute(pair[1], CTX, [(b, half + count - 1 - b) for b in range(half, count)])


def joined_tokens(pair, got, other, below):
    return jnp.concatenate(
        [jnp.where(below, pair[0], got), jnp.where(below, got, other)], axis=0
    )


def spread_tokens(pair, below, count):
    return joined_tokens(pair, spread_across(pair, below, count), spread_inside(pair, count), below)


def send_across(rows, below, count):
    half = count // 2
    across = [(half + b if b < half else count - 1 - b, b) for b in range(count)]
    return lax.ppermute(jnp.where(below, rows[BLK:], rows[:BLK]), CTX, across)


def send_inside(rows, count):
    half = count // 2
    inside = [(half + count - 1 - b, b) for b in range(half, count)]
    return lax.ppermute(rows[BLK:], CTX, inside)


def collect_tokens(rows, got, other, below):
    return jnp.stack([jnp.where(below, rows[:BLK], got), jnp.where(below, got, other)])


def collect_own(rows, below):
    mask = jnp.stack([below, jnp.zeros_like(below)])[:, None, None]
    return mask, jnp.stack([rows[:BLK], rows[:BLK]])


def ring_gather(rows, count):
    half = count // 2
    pieces = [rows]
    for step in range(1, half):
        pairs = [
            (side * half + b, side * half + (b + step) % half)
            for side in range(2)
            for b in range(half)
        ]
        pieces.append(lax.ppermute(rows, CTX, pairs))
    return pieces


def ring_scatter(pieces, count):
    half = count // 2
    arrived = []
    for step in range(1, half):
        pairs = [
            (side * half + b, side * half + (b - step) % half)
            for side in range(2)
            for b in range(half)
        ]
        arrived.append(lax.ppermute(pieces[step], CTX, pairs))
    return arrived


def add_up(members):
    return sum(member.astype(wide) for member in members).astype(low_type)


def ring_position(z):
    return jnp.where(z == 2, 3, jnp.where(z == 3, 2, z))


SWAP = [(0, 1), (1, 0)]
RING = [(z * 2 + x, after * 2 + x) for z, after in enumerate((1, 3, 0, 2)) for x in range(2)]
ACROSS_X = [(d, d ^ 1) for d in range(8)]


def along_z(rows):
    return lax.ppermute(rows, "dp", RING)


def along_x(rows):
    return lax.ppermute(rows, "dp", ACROSS_X)


def along_y(rows):
    return lax.ppermute(rows, "chip", SWAP)


def on_chip(rows):
    return lax.ppermute(rows, "core", SWAP)


def join(*members):
    return jnp.concatenate(members, axis=0)


def by_z(ring, first, rows, position):
    parts = [member[first : first + rows] for member in ring]
    placed = []
    for spot in (0, 1, 3, 2):
        step = lax.rem(position + 4 - spot, 4)
        chosen = parts[3]
        for index in (2, 1, 0):
            chosen = jnp.where(step == index, parts[index], chosen)
        placed.append(chosen)
    return jnp.stack(placed)


def z_halves(ring, position):
    size = ring[0].shape[0] // 2
    return [by_z(ring, part * size, size, position) for part in range(2)]


def cross(halves):
    return [along_x(halves[0]), along_y(halves[1])]


def cross_other(halves):
    return [along_y(halves[0]), along_x(halves[1])]


def paired(halves, crossed):
    return [jnp.stack([halves[part], crossed[part]]) for part in range(2)]


def swapped(members):
    return [on_chip(member) for member in members]


def linked_forward(
    first, second, chosen, tokens, cotangent, sizes, at, below, count, kept, attention_step, output_step, feed_step
):
    position = at[0]

    def gather(rows):
        whole = lax.all_gather(rows, EVERY, axis=0)
        return whole.reshape(4, 2, 2, 2, *rows.shape)

    v = Bag()
    v.f, v.g, v.h = [first[:128]], [second[:128]], [second[128:256]]
    first_feed, second_reduce = gather(first[128:]), gather(second[256:])

    def advance(ring):
        ring.append(along_z(ring[-1]))

    def mix(near, far):
        return near[0], far[0], near[1], far[1]

    def weights_f():
        return mix(v.f_near, v.f_far) + mix(v.f_near_other, v.f_far_other)

    def weights_g():
        return mix(v.g_near, v.g_far) + mix(v.g_near_other, v.g_far_other)

    def weights_h():
        return mix(v.h_near, v.h_far) + mix(v.h_near_other, v.h_far_other)

    for _ in range(3):
        advance(v.f)
    v.tokens = spread_tokens(tokens, below, count)
    v.chosen = chosen
    v = sync(v)
    v.f_half = z_halves(v.f, position)
    del v.f
    v.f_cross = cross(v.f_half)
    v.factors = lax.all_to_all(v.chosen, LANE, split_axis=0, concat_axis=0, tiled=True)
    del v.chosen
    advance(v.g)
    v = sync(v)
    v.f_near = paired(v.f_half, v.f_cross)
    del v.f_half, v.f_cross
    v.f_far = cross_other(v.f_near)
    v.f_near_other = swapped(v.f_near)
    v.factors_other = on_chip(v.factors)
    advance(v.g)
    advance(v.g)
    v = sync(v)
    v.g_half = z_halves(v.g, position)
    del v.g
    v.g_cross = cross(v.g_half)
    v.f_far_other = swapped(v.f_far)
    v.picked = unpack_factors(at, v.factors, v.factors_other, sizes)
    del v.factors, v.factors_other
    advance(v.h)
    v = sync(v)
    v.g_near = paired(v.g_half, v.g_cross)
    del v.g_half, v.g_cross
    v.g_far = cross_other(v.g_near)
    v.g_near_other = swapped(v.g_near)
    advance(v.h)
    advance(v.h)
    v.current = v.tokens.astype(wide)
    del v.tokens
    attention_step(v.current, (PIECES, weights_f()), v.picked[0], 0)
    v.middle = output_step(v.current, (PIECES, weights_f()), v.picked[0], 0)
    del v.current
    v.kept = kept
    v = sync(v)
    kept[:] = v.kept
    v.h_half = z_halves(v.h, position)
    del v.h
    v.h_cross = cross(v.h_half)
    v.g_far_other = swapped(v.g_far)
    v.current = feed_step(v.middle, (GATHERED, (first_feed,)), v.picked[0], 0)
    v.kept = kept
    v = sync(v)
    kept[:] = v.kept
    v.h_near = paired(v.h_half, v.h_cross)
    del v.h_half, v.h_cross
    v.h_far = cross_other(v.h_near)
    v.h_near_other = swapped(v.h_near)
    v.cotangent_other = spread_inside(cotangent, count)
    attention_step(v.current, (PIECES, weights_g()), v.picked[1], 1)
    v.middle = output_step(v.current, (PIECES, weights_g()), v.picked[1], 1)
    del v.current
    v.kept = kept
    v = sync(v)
    kept[:] = v.kept
    v.h_far_other = swapped(v.h_far)
    cotangent_got = spread_across(cotangent, below, count)
    frozen = [
        ((PIECES, weights_f()), (GATHERED, (first_feed,))),
        ((PIECES, weights_g()), (MIXED, (*weights_h(), second_reduce))),
    ]
    current = feed_step(v.middle, frozen[1][1], v.picked[1], 1)
    current, cotangent_got = sync((current, cotangent_got))
    cotangent = joined_tokens(cotangent, cotangent_got, v.cotangent_other, below)
    return current, cotangent.astype(wide), v.picked, frozen


SQUARE = (4, 2, 2, 2, 32, 1024)
TALL = (4, 2, 2, 2, 128, 1024)


def square_unit(form, part):
    return part if form == WHOLE else (part // 2, part % 2 * 32)


def expand_unit(form, part):
    return {WHOLE: part, GATHERED: 32 * part}.get(form, (part // 2, part % 2 * 32))


def fetch(form, at_ref, sources, unit, rows, held, arrived, by_quarter=None):
    spread_z = slice(None) if by_quarter is None else by_quarter
    if not isinstance(unit, tuple):
        if form == WHOLE:
            source = sources[unit].at[spread_z]
        else:
            source = sources[-1].at[(spread_z, *[slice(None)] * 3, pl.ds(unit, rows), slice(None))]
        pltpu.make_async_copy(source, held.at[spread_z], arrived).start()
        return
    part, first = unit
    x, y, core = at_ref[1], at_ref[2], at_ref[3]
    for other in range(2):
        for far in range(2):
            source = sources[other * 4 + part * 2 + far]
            for over in range(2):
                over_x, over_y = (over, far) if part == 0 else (far, over)
                pltpu.make_async_copy(
                    source.at[over, spread_z, pl.ds(first, rows), :],
                    held.at[
                        spread_z,
                        lax.rem(x + over_x, 2),
                        lax.rem(y + over_y, 2),
                        lax.rem(core + other, 2),
                    ],
                    arrived,
                ).start()


def wait_for(held, arrived):
    pltpu.make_async_copy(held, held, arrived).wait()


def square(held):
    return held[...].reshape(1024, 1024)


QKV_TILE, OUTPUT_TILE, FEED_TILE, TURN_TILE, QKV_BACK_TILE = 0, 0, 512, 512, 512
STRIP = 64
QKV_ROWS, OUTPUT_ROWS, QKV_BACK_ROWS, FEED_BACK_ROWS = 256, 256, 256, 256
COLUMNS = 1024


def strips(count, body):
    def step(index, carry):
        body(pl.ds(pl.multiple_of(index * STRIP, STRIP), STRIP))
        return carry

    lax.fori_loop(0, count // STRIP, step, 0, unroll=True)


def normalize_rows(values, gain, shift):
    center = jnp.mean(values, axis=-1, keepdims=True)
    spread = values - center
    scale = lax.rsqrt(jnp.mean(spread * spread, axis=-1, keepdims=True) + epsilon)
    unit = spread * scale
    return unit, scale, unit * gain + shift


def normalize_pull(grad, unit, scale, gain):
    scaled = grad * gain
    first = jnp.mean(scaled, axis=-1, keepdims=True)
    second = jnp.mean(scaled * unit, axis=-1, keepdims=True)
    return scale * (scaled - first - unit * second)


def store_norm(values_ref, gain_ref, shift_ref, normed_ref, unit_ref, scale_ref):
    def norm(rows):
        unit, scale, normed = normalize_rows(values_ref[rows, :], gain_ref[...], shift_ref[...])
        normed_ref[rows, :] = normed.astype(low_type)
        unit_ref[rows, :] = unit.astype(low_type)
        scale_ref[rows, :] = jnp.broadcast_to(scale, (STRIP, 128))

    strips(values_ref.shape[0], norm)


def store_pull(out_ref, grad_ref, inner_ref, unit_ref, scale_ref, gain_ref):
    def pull(rows):
        out_ref[rows, :] = grad_ref[rows, :] + normalize_pull(
            inner_ref[rows, :], unit_ref[rows, :].astype(wide), scale_ref[rows, :1], gain_ref[...]
        )

    strips(out_ref.shape[0], pull)


def row_tiles(count, size):
    return [slice(first, first + size) for first in range(0, count, size)]


def span(part):
    return slice(part * COLUMNS, (part + 1) * COLUMNS)


TILED = [False]


def at_first(body):
    if TILED[0]:
        pl.when(pl.program_id(0) == 0)(body)
    else:
        body()


def at_last(body):
    if TILED[0]:
        pl.when(pl.program_id(0) == pl.num_programs(0) - 1)(body)
    else:
        body()


def await_first(held, arrived):
    at_first(lambda: wait_for(held, arrived))


def gather_sum(total, step_value):
    @at_first
    def _():
        total[...] = step_value

    if TILED[0]:

        @pl.when(pl.program_id(0) > 0)
        def _():
            total[...] = total[...] + step_value


def qkv_kernel(form, at_ref, x_ref, gain_ref, shift_ref, left_ref, right_ref, bias_ref, *refs):
    sources, (normed_ref, unit_ref, scale_ref, rank_ref, *outs) = refs[:-9], refs[-9:-2]
    held, arrived = refs[-2:]

    @at_first
    def _():
        for part in range(3):
            fetch(form, at_ref, sources, square_unit(form, part), 32, held.at[part], arrived.at[part])

    store_norm(x_ref, gain_ref, shift_ref, normed_ref, unit_ref, scale_ref)
    rank_ref[...] = times(normed_ref[...], left_ref[...], ROWS_BY_ROWS).astype(low_type)
    for part, out in enumerate(outs):
        await_first(held.at[part], arrived.at[part])
        for rows in row_tiles(out.shape[0], QKV_ROWS):
            out[rows, :] = (
                times(normed_ref[rows, :], square(held.at[part]))
                + times(rank_ref[rows, :], right_ref[:, span(part)])
                + bias_ref[:, span(part)]
            ).astype(low_type)


def output_kernel(form, at_ref, x_ref, attended_ref, left_ref, right_ref, bias_ref, gain_ref, shift_ref, *refs):
    sources, (low_ref, middle_ref, normed_ref, unit_ref, scale_ref, rank_ref) = refs[:-8], refs[-8:-2]
    held, arrived = refs[-2:]
    at_first(lambda: fetch(form, at_ref, sources, square_unit(form, 3), 32, held, arrived))
    low_ref[...] = attended_ref[...].astype(low_type)
    rank_ref[...] = times(low_ref[...], left_ref[...], ROWS_BY_ROWS).astype(low_type)
    await_first(held, arrived)
    for rows in row_tiles(x_ref.shape[0], OUTPUT_ROWS):
        middle_ref[rows, :] = (
            x_ref[rows, :]
            + times(low_ref[rows, :], square(held))
            + times(rank_ref[rows, :], right_ref[...])
            + bias_ref[...]
        )
    store_norm(middle_ref, gain_ref, shift_ref, normed_ref, unit_ref, scale_ref)


def fetch_feed_part(form, at_ref, sources, part, expand, reduce, arrived, reduce_first):
    jobs = [
        (expand_unit(form, part), 32, expand.at[part], arrived.at[0, part], None),
        ({WHOLE: 4, GATHERED: 128, MIXED: 0}[form], 128, reduce, arrived.at[1, part], part),
    ]
    for unit, rows, held, semaphore, quarter in jobs[::-1] if reduce_first else jobs:
        fetch(form, at_ref, sources, unit, rows, held, semaphore, quarter)


def fetch_feed_forward(form, at_ref, sources, expand, reduce, arrived, reduce_first):
    for part in range(4):
        fetch_feed_part(form, at_ref, sources, part, expand, reduce, arrived, reduce_first)


def feed_forward_kernel(
    form, at_ref, normed_ref, middle_ref, expand_left_ref, expand_right_ref, expand_bias_ref,
    reduce_left_ref, reduce_right_ref, reduce_bias_ref, *refs,
):
    sources, (result_ref, slope_ref, active_ref, rank_expand_ref, rank_reduce_ref) = refs[:-9], refs[-9:-4]
    expand, reduce, rank_sum, arrived = refs[-4:]
    at_first(lambda: fetch_feed_forward(form, at_ref, sources, expand, reduce, arrived, False))
    rank_expand_ref[...] = times(normed_ref[...], expand_left_ref[...], ROWS_BY_ROWS).astype(low_type)
    result_ref[...] = middle_ref[...] + reduce_bias_ref[...]
    rank_sum[...] = jnp.zeros_like(rank_sum)

    def part_step(part, carry):
        columns = pl.ds(pl.multiple_of(part * COLUMNS, COLUMNS), COLUMNS)
        await_first(expand.at[part], arrived.at[0, part])
        await_first(reduce.at[part], arrived.at[1, part])
        value = (
            times(normed_ref[...], square(expand.at[part]))
            + times(rank_expand_ref[...], expand_right_ref[:, columns])
            + expand_bias_ref[:, columns]
        )
        squared = value * value
        bent = jnp.tanh(value * (root_factor + 0.044715 * root_factor * squared))
        half = 0.5 + 0.5 * bent
        slope_ref[:, columns] = (
            half
            + value * (0.5 - 0.5 * bent * bent) * (root_factor + 3 * 0.044715 * root_factor * squared)
        ).astype(low_type)
        active = (value * half).astype(low_type)
        active_ref[:, columns] = active
        result_ref[...] = result_ref[...] + times(active, square(reduce.at[part]))
        rank_sum[...] = rank_sum[...] + times(active, reduce_left_ref[:, columns], ROWS_BY_ROWS)
        return carry

    lax.fori_loop(0, 4, part_step, 0)
    rank_reduce_ref[...] = rank_sum[...].astype(low_type)
    result_ref[...] = result_ref[...] + times(rank_reduce_ref[...], reduce_right_ref[...])


def feed_output_backward_kernel(
    form, output_form, members, at_ref, grad_ref, normed_ref, unit_ref, scale_ref, rank_expand_ref, rank_reduce_ref,
    attended_ref, rank_output_ref, gain_ref, output_left_ref, output_right_ref, expand_left_ref, expand_right_ref,
    reduce_left_ref, reduce_right_ref, slope_ref, active_ref, *refs,
):
    sources, output_sources, outs, scratch = refs[:members], refs[members:-23], refs[-23:-15], refs[-15:]
    middle_ref, out_ref, output_left_g, output_right_g, expand_left_g, expand_right_g, reduce_left_g, reduce_right_g = outs
    (
        expand, reduce, arrived, held, held_arrived, slope, active, side_arrived,
        low_grad, turned, bent, total, turn_sum, low_middle, output_turned,
    ) = scratch
    for part in range(4):
        for which, (source, kept) in enumerate(((slope_ref, slope), (active_ref, active))):
            pltpu.make_async_copy(
                source.at[:, span(part)], kept.at[part], side_arrived.at[which, part]
            ).start()
        fetch_feed_part(form, at_ref, sources, part, expand, reduce, arrived, True)
    fetch(output_form, at_ref, output_sources, square_unit(output_form, 3), 32, held, held_arrived)
    low_grad[...] = grad_ref[...].astype(low_type)
    turned[...] = times(low_grad[...], reduce_right_ref[...], ROWS_BY_ROWS).astype(low_type)
    reduce_right_g[...] = times(rank_reduce_ref[...], low_grad[...], COLS_BY_COLS).astype(low_type)
    total[...] = jnp.zeros_like(total)
    turn_sum[...] = jnp.zeros_like(turn_sum)

    def part_step(part, carry):
        columns = pl.ds(pl.multiple_of(part * COLUMNS, COLUMNS), COLUMNS)
        wait_for(slope.at[part], side_arrived.at[0, part])
        wait_for(active.at[part], side_arrived.at[1, part])
        wait_for(reduce.at[part], arrived.at[1, part])
        wait_for(expand.at[part], arrived.at[0, part])
        for rows in row_tiles(grad_ref.shape[0], FEED_BACK_ROWS):
            grad_active = times(low_grad[rows, :], square(reduce.at[part]), ROWS_BY_ROWS) + times(
                turned[rows, :], reduce_left_ref[:, columns]
            )
            bent[rows, :] = (grad_active * slope[part, rows, :].astype(wide)).astype(low_type)
            total[rows, :] = total[rows, :] + times(bent[rows, :], square(expand.at[part]), ROWS_BY_ROWS)
        turn_sum[...] = turn_sum[...] + times(bent[...], expand_right_ref[:, columns], ROWS_BY_ROWS)
        reduce_left_g[:, columns] = times(turned[...], active[part], COLS_BY_COLS).astype(low_type)
        expand_right_g[:, columns] = times(rank_expand_ref[...], bent[...], COLS_BY_COLS).astype(low_type)
        return carry

    lax.fori_loop(0, 4, part_step, 0)
    turned[...] = turn_sum[...].astype(low_type)
    expand_left_g[...] = times(turned[...], normed_ref[...], COLS_BY_COLS).astype(low_type)
    total[...] = total[...] + times(turned[...], expand_left_ref[...])
    store_pull(middle_ref, grad_ref, total, unit_ref, scale_ref, gain_ref)
    low_middle[...] = middle_ref[...].astype(low_type)
    output_turned[...] = times(low_middle[...], output_right_ref[...], ROWS_BY_ROWS).astype(low_type)
    output_right_g[...] = times(rank_output_ref[...], low_middle[...], COLS_BY_COLS).astype(low_type)
    output_left_g[...] = times(output_turned[...], attended_ref[...], COLS_BY_COLS).astype(low_type)
    wait_for(held, held_arrived)
    out_ref[...] = (
        times(low_middle[...], square(held), ROWS_BY_ROWS) + times(output_turned[...], output_left_ref[...])
    ).astype(low_type)


def qkv_turn_kernel(pieces, form, at_ref, normed_ref, rank_ref, dq_ref, *refs):
    dk_refs, dv_refs, (right_ref, *refs) = refs[:pieces], refs[pieces : 2 * pieces], refs[2 * pieces :]
    dk_ref, dv_ref, turned_ref, left_g, right_g, left_sum, right_sum = refs
    dk_ref[...] = add_up([member[...] for member in dk_refs])
    dv_ref[...] = add_up([member[...] for member in dv_refs])
    grads = (dq_ref, dk_ref, dv_ref)
    turned = sum(
        times(grads[part][...], right_ref[:, span(part)], ROWS_BY_ROWS) for part in range(3)
    ).astype(low_type)
    turned_ref[...] = turned
    gather_sum(left_sum, times(turned, normed_ref[...], COLS_BY_COLS))
    for part in range(3):
        gather_sum(right_sum.at[part], times(rank_ref[...], grads[part][...], COLS_BY_COLS))

    @at_last
    def _():
        left_g[...] = left_sum[...].astype(low_type)
        for part in range(3):
            right_g[:, span(part)] = right_sum[part].astype(low_type)


def qkv_backward_kernel(
    form, at_ref, grad_ref, unit_ref, scale_ref, turned_ref, dq_ref, dk_ref, dv_ref, gain_ref, left_ref, *refs
):
    sources, (out_ref, low_ref), (held, arrived, total) = refs[:-5], refs[-5:-3], refs[-3:]

    @at_first
    def _():
        for part in range(3):
            fetch(form, at_ref, sources, square_unit(form, part), 32, held.at[part], arrived.at[part])

    total[...] = times(turned_ref[...], left_ref[...])
    for part, member in enumerate((dq_ref, dk_ref, dv_ref)):
        await_first(held.at[part], arrived.at[part])
        for rows in row_tiles(out_ref.shape[0], QKV_BACK_ROWS):
            total[rows, :] = total[rows, :] + times(member[rows, :], square(held.at[part]), ROWS_BY_ROWS)
    store_pull(out_ref, grad_ref, total, unit_ref, scale_ref, gain_ref)
    low_ref[...] = out_ref[...].astype(low_type)


def qkv_whole_kernel(
    pieces, form, at_ref, grad_ref, unit_ref, scale_ref, normed_ref, rank_ref, dq_ref, *refs
):
    dk_refs, dv_refs, (gain_ref, left_ref, right_ref, *refs) = refs[:pieces], refs[pieces : 2 * pieces], refs[2 * pieces :]
    sources, (out_ref, left_g, right_g) = refs[:-9], refs[-9:-6]
    held, arrived, turned, total, dk_ref, dv_ref = refs[-6:]
    for part in range(3):
        fetch(form, at_ref, sources, square_unit(form, part), 32, held.at[part], arrived.at[part])
    dk_ref[...] = add_up([member[...] for member in dk_refs])
    dv_ref[...] = add_up([member[...] for member in dv_refs])
    grads = (dq_ref, dk_ref, dv_ref)
    turned[...] = sum(
        times(grads[part][...], right_ref[:, span(part)], ROWS_BY_ROWS) for part in range(3)
    ).astype(low_type)
    for part in range(3):
        right_g[:, span(part)] = times(rank_ref[...], grads[part][...], COLS_BY_COLS).astype(low_type)
    left_g[...] = times(turned[...], normed_ref[...], COLS_BY_COLS).astype(low_type)
    for part, member in enumerate(grads):
        wait_for(held.at[part], arrived.at[part])
        for rows in row_tiles(out_ref.shape[0], QKV_BACK_ROWS):
            value = times(member[rows, :], square(held.at[part]), ROWS_BY_ROWS)
            before = total[rows, :] if part else times(turned[rows, :], left_ref[...])
            total[rows, :] = before + value
    store_pull(out_ref, grad_ref, total, unit_ref, scale_ref, gain_ref)


def frozen_call(kernel, name, at, weights, tile, tiled, fixed, outs, fixed_outs, scratch, cost):
    form, sources = weights
    count = tiled[0].shape[0]
    TILED[0] = tile > 0

    def by_rows(shape):
        if tile == 0:
            return pl.BlockSpec(memory_space=pltpu.VMEM)
        return pl.BlockSpec((tile, shape[1]), lambda step: (step, 0))

    def every(shape):
        if tile == 0:
            return pl.BlockSpec(memory_space=pltpu.VMEM)
        return pl.BlockSpec(shape, lambda step: (0, 0))

    return pl.pallas_call(
        functools.partial(kernel, form),
        grid=(count // tile,) if tile else (),
        out_shape=tuple(jax.ShapeDtypeStruct(shape, kind) for shape, kind in (*outs, *fixed_outs)),
        in_specs=[pl.BlockSpec(memory_space=pltpu.SMEM)]
        + [by_rows(member.shape) for member in tiled]
        + [every(member.shape) for member in fixed]
        + [pl.BlockSpec(memory_space=pl.ANY)] * len(sources),
        out_specs=tuple(by_rows(shape) for shape, _ in outs) + tuple(every(shape) for shape, _ in fixed_outs),
        scratch_shapes=scratch,
        compiler_params=pltpu.CompilerParams(vmem_limit_bytes=60 * 2**20),
        cost_estimate=pl.CostEstimate(flops=cost * MICROSECOND, bytes_accessed=0, transcendentals=0),
        name=name,
    )(at, *tiled, *fixed, *sources)


def row(vector):
    return vector.reshape(1, -1)


DMA = pltpu.SemaphoreType.DMA


PACKED = ((5, 0), (6, 128), (1, 256), (0, 352), (2, 384), (3, 416), (4, 448), (7, 480))


def unpack_kernel(order, at_ref, own_ref, other_ref, *outs):
    layers, groups = own_ref.shape[1], own_ref.shape[0] // 2
    swapped = at_ref[3] == 1
    for layer_index in range(layers):
        for group in range(groups):
            lanes = []
            for chip in range(2):
                own = own_ref[group * 2 + chip, layer_index]
                other = other_ref[group * 2 + chip, layer_index]
                lanes += [jnp.where(swapped, other, own), jnp.where(swapped, own, other)]
            for kind, first in order:
                out = outs[layer_index * len(order) + kind]
                size = out.shape[1] // (4 * groups)
                out[:, group * 4 * size : (group + 1) * 4 * size] = jnp.concatenate(
                    [lane[:, first : first + size] for lane in lanes], axis=1
                )


def unpack_factors(at, own, other, sizes):
    lanes, layers = own.shape[:2]
    local_spec = pl.BlockSpec(memory_space=pltpu.VMEM)
    found = pl.pallas_call(
        functools.partial(unpack_kernel, PACKED),
        out_shape=tuple(
            jax.ShapeDtypeStruct((RANK, size * lanes * 2), low_type) for _ in range(layers) for size in sizes
        ),
        in_specs=[pl.BlockSpec(memory_space=pltpu.SMEM), local_spec, local_spec],
        out_specs=(local_spec,) * (layers * len(sizes)),
        compiler_params=pltpu.CompilerParams(vmem_limit_bytes=32 * 2**20),
        cost_estimate=pl.CostEstimate(flops=4 * MICROSECOND, bytes_accessed=0, transcendentals=0),
        name="unpack_factors",
    )(at, own, other)
    return [found[layer * len(sizes) : (layer + 1) * len(sizes)] for layer in range(layers)]


def pack_kernel(orders, at_ref, *refs):
    members, out_ref = refs[:-1], refs[-1]
    core, base, offset = at_ref[3], 0, 0
    for order in orders:
        for lane_chip in range(out_ref.shape[1]):
            for owner_core in range(2):
                owner = lane_chip * 2 + owner_core
                parts = []
                for index, _ in enumerate(order):
                    member = members[base + index]
                    size = member.shape[1] // (2 * out_ref.shape[1])
                    parts.append(member[:, owner * size : (owner + 1) * size])
                joined = jnp.concatenate(parts, axis=1)
                out_ref[lax.rem(owner_core + core, 2), lane_chip, :, offset : offset + joined.shape[1]] = joined
        base += len(order)
        offset += joined.shape[1]


def pack_gradients(at, groups, lanes):
    members, width = [], 0
    for order, terms in groups:
        members += [terms[kind] for kind, _ in order]
        width += sum(terms[kind].shape[1] for kind, _ in order) // (2 * lanes)
    local_spec = pl.BlockSpec(memory_space=pltpu.VMEM)
    return pl.pallas_call(
        functools.partial(pack_kernel, [order for order, _ in groups]),
        out_shape=jax.ShapeDtypeStruct((2, lanes, RANK, width), low_type),
        in_specs=[pl.BlockSpec(memory_space=pltpu.SMEM)] + [local_spec] * len(members),
        out_specs=local_spec,
        compiler_params=pltpu.CompilerParams(vmem_limit_bytes=32 * 2**20),
        cost_estimate=pl.CostEstimate(flops=4 * MICROSECOND, bytes_accessed=0, transcendentals=0),
        name="pack_gradients",
    )(at, *members)


LOW, WIDE = low_type, wide


def forward_qkv(current, weights, picked, extras, at):
    rows, columns = current.shape
    full_low = ((rows, columns), LOW)
    bias = jnp.concatenate([extras[0][:columns], jnp.zeros((columns,), WIDE), extras[0][columns:]])
    return frozen_call(
        qkv_kernel, "qkv_forward", at, weights, QKV_TILE, (current,),
        (row(extras[4]), row(extras[5]), picked[0], picked[1], row(bias)),
        (full_low, full_low, ((rows, 128), WIDE), ((rows, RANK), LOW), full_low, full_low, full_low), (),
        [pltpu.VMEM((3, *SQUARE), LOW), DMA((3,))], 9,
    )


def forward_output(current, attended, weights, picked, extras, at):
    rows, columns = current.shape
    full, full_low = ((rows, columns), WIDE), ((rows, columns), LOW)
    return frozen_call(
        output_kernel, "output_forward", at, weights, OUTPUT_TILE, (current, attended),
        (picked[2], picked[3], row(extras[1]), row(extras[6]), row(extras[7])),
        (full_low, full, full_low, full_low, ((rows, 128), WIDE), ((rows, RANK), LOW)), (),
        [pltpu.VMEM(SQUARE, LOW), DMA], 8,
    )


def forward_feed(normed, middle, weights, picked, extras, at):
    rows, columns = middle.shape
    tall, ranks = ((rows, picked[5].shape[1]), LOW), ((rows, RANK), LOW)
    return frozen_call(
        feed_forward_kernel, "feed_forward", at, weights, FEED_TILE, (normed, middle),
        (picked[4], picked[5], row(extras[2]), picked[6], picked[7], row(extras[3])),
        (((rows, columns), WIDE), tall, tall, ranks, ranks), (),
        [
            pltpu.VMEM((4, *SQUARE), LOW), pltpu.VMEM(TALL, LOW), pltpu.VMEM((FEED_TILE or rows, RANK), WIDE),
            DMA((2, 4)),
        ], 20,
    )


def like(member):
    return (member.shape, LOW)


def backward_feed_output(grad, kept, weights, output_weights, picked, extras, at):
    rows, columns = grad.shape
    form, sources = weights
    output_form, output_sources = output_weights
    full, full_low, ranks = ((rows, columns), WIDE), ((rows, columns), LOW), ((rows, RANK), LOW)
    tall = ((4, rows, columns), LOW)
    members = (
        grad, kept.normed_two, kept.unit_two, kept.scale_two, kept.rank_expand, kept.rank_reduce,
        kept.attended_low, kept.rank_output, row(extras[6]), *picked[2:],
    )
    local_spec, anywhere = pl.BlockSpec(memory_space=pltpu.VMEM), pl.BlockSpec(memory_space=pl.ANY)
    outs = (full, full_low, *map(like, picked[2:]))
    return pl.pallas_call(
        functools.partial(feed_output_backward_kernel, form, output_form, len(sources)),
        out_shape=tuple(jax.ShapeDtypeStruct(shape, kind) for shape, kind in outs),
        in_specs=[pl.BlockSpec(memory_space=pltpu.SMEM)]
        + [local_spec] * len(members)
        + [anywhere] * (2 + len(sources) + len(output_sources)),
        out_specs=(local_spec,) * len(outs),
        scratch_shapes=[
            pltpu.VMEM((4, *SQUARE), LOW), pltpu.VMEM(TALL, LOW), DMA((2, 4)), pltpu.VMEM(SQUARE, LOW), DMA,
            pltpu.VMEM(*tall), pltpu.VMEM(*tall), DMA((2, 4)), pltpu.VMEM(*full_low), pltpu.VMEM(*ranks),
            pltpu.VMEM(*full_low), pltpu.VMEM(*full), pltpu.VMEM((rows, RANK), WIDE), pltpu.VMEM(*full_low),
            pltpu.VMEM(*ranks),
        ],
        compiler_params=pltpu.CompilerParams(vmem_limit_bytes=60 * 2**20),
        cost_estimate=pl.CostEstimate(flops=25 * MICROSECOND, bytes_accessed=0, transcendentals=0),
        name="feed_output_backward",
    )(at, *members, kept.slope, kept.active, *sources, *output_sources)


def backward_turn(grads, kept, picked, at):
    query_grad, key_grads, value_grads = grads
    full_low = (query_grad.shape, LOW)
    return frozen_call(
        functools.partial(qkv_turn_kernel, len(key_grads)), "qkv_turn", at, (WHOLE, ()), TURN_TILE,
        (kept.normed_one, kept.rank_attend, query_grad, *key_grads, *value_grads), (picked[1],),
        (full_low, full_low, like(kept.rank_attend)), (like(picked[0]), like(picked[1])),
        [pltpu.VMEM(picked[0].shape, WIDE), pltpu.VMEM((3, *picked[0].shape), WIDE)], 3,
    )


def backward_qkv_whole(grad, grads, kept, weights, picked, extras, at):
    rows, columns = grad.shape
    query_grad, key_grads, value_grads = grads
    return frozen_call(
        functools.partial(qkv_whole_kernel, len(key_grads)), "qkv_whole", at, weights, QKV_BACK_TILE,
        (
            grad, kept.unit_one, kept.scale_one, kept.normed_one, kept.rank_attend, query_grad, *key_grads,
            *value_grads,
        ),
        (row(extras[4]), picked[0], picked[1]),
        (((rows, columns), WIDE),), (like(picked[0]), like(picked[1])),
        [
            pltpu.VMEM((3, *SQUARE), LOW), DMA((3,)), pltpu.VMEM((rows, RANK), LOW),
            pltpu.VMEM((rows, columns), WIDE), pltpu.VMEM((rows, columns), LOW), pltpu.VMEM((rows, columns), LOW),
        ], 11,
    )


def backward_qkv(grad, joined, turned, kept, weights, picked, extras, at):
    rows, columns = grad.shape
    return frozen_call(
        qkv_backward_kernel, "qkv_backward", at, weights, QKV_BACK_TILE,
        (grad, kept.unit_one, kept.scale_one, turned, *joined), (row(extras[4]), picked[0]),
        (((rows, columns), WIDE), ((rows, columns), LOW)), (),
        [pltpu.VMEM((3, *SQUARE), LOW), DMA((3,)), pltpu.VMEM((QKV_BACK_TILE or rows, columns), WIDE)], 9,
    )


def combine_kernel(places, ids_ref, *refs):
    count = len(places)
    received, outs, total = refs[:count], refs[count:-1], refs[-1]
    total[...] = jnp.zeros_like(total)
    for source in range(received[0].shape[0]):
        adapter, spot = ids_ref[source], 0
        for member in received:
            width = member.shape[2]
            at = (adapter, slice(None), slice(spot, spot + width))
            total[at] = total[at] + member[source].astype(wide)
            spot += width
    base = 0
    for member, orders in zip(received, places):
        for layer_index, order in orders:
            for kind, _ in order:
                size = outs[kind].shape[3]
                outs[kind][layer_index] = total[:, :, base : base + size]
                base += size


def combine(ids, received, places, sizes):
    local_spec = pl.BlockSpec(memory_space=pltpu.VMEM)
    width = sum(member.shape[2] for member in received)
    return pl.pallas_call(
        functools.partial(combine_kernel, places),
        out_shape=tuple(jax.ShapeDtypeStruct((LAYERS, ADAPTERS, RANK, size), wide) for size in sizes),
        in_specs=[pl.BlockSpec(memory_space=pltpu.SMEM)] + [local_spec] * len(received),
        out_specs=(local_spec,) * len(sizes),
        scratch_shapes=[pltpu.VMEM((ADAPTERS, RANK, width), wide)],
        compiler_params=pltpu.CompilerParams(vmem_limit_bytes=32 * 2**20),
        cost_estimate=pl.CostEstimate(flops=3 * MICROSECOND, bytes_accessed=0, transcendentals=0),
        name="combine",
    )(ids, *received)


class Bag:
    pass


def open_bag(bag):
    names = tuple(sorted(vars(bag)))
    return tuple(getattr(bag, name) for name in names), names


def close_bag(names, members):
    bag = Bag()
    for name, member in zip(names, members):
        setattr(bag, name, member)
    return bag


jax.tree_util.register_pytree_node(Bag, open_bag, close_bag)


def sync(values):
    leaves, shape = jax.tree.flatten(values)
    return jax.tree.unflatten(shape, lax.optimization_barrier(tuple(leaves)))


def local(
    tokens, cotangent, adapter_ids, attend_weight, output_weight, expand_weight, reduce_weight,
    attend_bias, output_bias, expand_bias, reduce_bias, first_gain, first_shift, second_gain, second_shift,
    *adapters,
):
    data_count, chips = lax.axis_size("dp"), lax.axis_size("chip")
    count = chips * lax.axis_size("core")
    half = count // 2
    devices = data_count * count
    data_rank, core = lax.axis_index("dp"), lax.axis_index("core")
    rank = lax.axis_index("chip") * 2 + core
    below = rank < half
    place = jnp.reshape(lax.rem(rank, half), (1,)).astype(jnp.int32)
    columns = tokens.shape[2]
    linked = (data_count, chips, columns) == (8, 2, 1024)

    lane_chip = jnp.arange(data_count * chips, dtype=jnp.int32)
    lane_sequence = (lane_chip // chips) * 2 + (lane_chip % chips) // (chips // 2)
    lane_adapter = jnp.take(adapter_ids, lane_sequence)

    sizes = [member.shape[2] for member in adapters]
    packed = jnp.concatenate([jnp.swapaxes(adapters[kind], 2, 3) for kind, _ in PACKED], axis=3)
    chosen = jnp.moveaxis(jnp.take(packed, lane_adapter, axis=1), 1, 0)

    def shards(layer_index):
        lists = [attend_weight[layer_index], output_weight[layer_index], expand_weight[layer_index]]
        blocks = [
            member[:, first : first + columns]
            for member in lists
            for first in range(0, member.shape[1], columns)
        ]
        return jnp.concatenate(blocks + [reduce_weight[layer_index]], axis=0)

    extras = [
        tuple(
            member[layer_index]
            for member in (
                attend_bias, output_bias, expand_bias, reduce_bias,
                first_gain, first_shift, second_gain, second_shift,
            )
        )
        for layer_index in range(LAYERS)
    ]
    position = ring_position(data_rank // 2)
    at = jnp.stack([position, data_rank % 2, lax.axis_index("chip"), core]).astype(jnp.int32)
    kept = [Bag(), Bag()]

    def attention_step(current, weights, picked, layer_index):
        keep = kept[layer_index]
        (
            keep.normed_one, keep.unit_one, keep.scale_one, keep.rank_attend,
            keep.queries, keys, values,
        ) = forward_qkv(current, weights, picked, extras[layer_index], at)
        keep.keys, keep.values = ring_gather(keys, count), ring_gather(values, count)
        keep.attended, keep.stat = attend_forward(place, keep.queries, keep.keys, keep.values)

    def output_step(current, weights, picked, layer_index):
        keep = kept[layer_index]
        (
            keep.attended_low, middle, keep.normed_two, keep.unit_two, keep.scale_two,
            keep.rank_output,
        ) = forward_output(current, keep.attended, weights, picked, extras[layer_index], at)
        return middle

    def feed_step(middle, weights, picked, layer_index):
        keep = kept[layer_index]
        result, keep.slope, keep.active, keep.rank_expand, keep.rank_reduce = forward_feed(
            keep.normed_two, middle, weights, picked, extras[layer_index], at
        )
        return result

    if linked:
        first, second = shards(0), shards(1)
        current, grad_current, picked, frozen = linked_forward(
            first, second, chosen, tokens, cotangent, sizes, at, below, count, kept,
            attention_step, output_step, feed_step,
        )
    else:
        current = spread_tokens(tokens, below, count).astype(wide)
        grad_current = spread_tokens(cotangent, below, count).astype(wide)
        mine = lax.all_to_all(chosen, LANE, split_axis=0, concat_axis=0, tiled=True)
        theirs = lax.ppermute(mine, "core", SWAP)
        both = jnp.stack(
            [jnp.where(core == 0, mine, theirs), jnp.where(core == 0, theirs, mine)], axis=1
        )
        places, spot = {}, 0
        for kind, _ in PACKED:
            places[kind] = spot
            spot += sizes[kind]
        picked = [
            tuple(
                jnp.transpose(
                    both[:, :, layer_index, :, places[kind] : places[kind] + size], (2, 0, 1, 3)
                ).reshape(RANK, devices * size)
                for kind, size in enumerate(sizes)
            )
            for layer_index in range(LAYERS)
        ]
        frozen = []
        for layer_index in range(LAYERS):
            whole = lax.all_gather(shards(layer_index), EVERY, axis=0)
            size = columns // devices
            squares = [whole[:, part * size : (part + 1) * size, :].reshape(SQUARE) for part in range(8)]
            tall = whole[:, 8 * size :, :].reshape(TALL)
            frozen.append(((WHOLE, tuple(squares[:4])), (WHOLE, (*squares[4:], tall))))
            first_weights, second_weights = frozen[layer_index]
            attention_step(current, first_weights, picked[layer_index], layer_index)
            middle = output_step(current, first_weights, picked[layer_index], layer_index)
            current = feed_step(middle, second_weights, picked[layer_index], layer_index)

    result = current.astype(low_type)
    result_got, result_other = send_across(result, below, count), send_inside(result, count)
    lanes = data_count * chips

    def to_owners(groups):
        if linked:
            both = pack_gradients(at, groups, lanes)
            own, sent = both[0], both[1]
        else:
            both = jnp.concatenate(
                [
                    jnp.transpose(
                        terms[kind].reshape(RANK, lanes, 2, sizes[kind]), (2, 1, 0, 3)
                    )
                    for order, terms in groups
                    for kind, _ in order
                ],
                axis=3,
            )
            own, sent = jnp.where(core == 0, both[0], both[1]), jnp.where(core == 0, both[1], both[0])
        total = add_up([own, lax.ppermute(sent, "core", SWAP)])
        return lax.all_to_all(total, LANE, split_axis=0, concat_axis=0, tiled=True)

    terms = [None] * LAYERS
    for layer_index in reversed(range(LAYERS)):
        keep, extra, factors = kept[layer_index], extras[layer_index], picked[layer_index]
        first_weights, second_weights = frozen[layer_index]
        middle_grad, attended_grad, *some_terms = backward_feed_output(
            grad_current, keep, second_weights, first_weights, factors, extra, at
        )
        if layer_index == LAYERS - 1:
            middle_grad, attended_grad, some_terms, result_got = sync(
                (middle_grad, attended_grad, some_terms, result_got)
            )
        query_grad, key_grads, value_grads = attend_backward(
            place, keep.queries, keep.keys, keep.values, attended_grad, keep.attended, keep.stat
        )
        if layer_index == LAYERS - 1:
            query_grad, key_grads, value_grads, result_other = sync(
                (query_grad, key_grads, value_grads, result_other)
            )
        grads = (
            query_grad,
            [key_grads[0], *ring_scatter(key_grads, count)],
            [value_grads[0], *ring_scatter(value_grads, count)],
        )
        if layer_index > 0:
            grad_current, *attend_terms = backward_qkv_whole(
                middle_grad, grads, keep, first_weights, factors, extra, at
            )
            terms[layer_index] = [*attend_terms, *some_terms]
            continue
        key_grad, value_grad, turned, *attend_terms = backward_turn(grads, keep, factors, at)
        terms[layer_index] = [*attend_terms, *some_terms]
        received = to_owners([(PACKED, terms[1]), (PACKED, terms[0])])
        grad_current, low_grad = backward_qkv(
            middle_grad, (query_grad, key_grad, value_grad), turned, keep, first_weights, factors, extra, at
        )
    got, other = send_across(low_grad, below, count), send_inside(low_grad, count)
    received, got = sync((received, got))
    moved = collect_tokens(low_grad, got, other, below)
    kept_part = collect_own(grad_current, below)
    received = [received]
    places = (((1, PACKED), (0, PACKED)),)
    if linked:
        results = combine(lane_adapter, received, places, sizes)
    else:
        owner_adapter = (lane_adapter[:, None] == jnp.arange(ADAPTERS)[None, :]).astype(wide)
        found = [[None] * len(sizes) for _ in range(LAYERS)]
        for held, orders in zip(received, places):
            summed = jnp.einsum(
                "sa,srp->arp", owner_adapter, held.astype(wide), precision=lax.Precision.HIGHEST
            )
            spot = 0
            for layer_index, order in orders:
                for kind, _ in order:
                    found[layer_index][kind] = summed[:, :, spot : spot + sizes[kind]]
                    spot += sizes[kind]
        results = [
            jnp.stack([found[layer_index][kind] for layer_index in range(LAYERS)])
            for kind in range(len(sizes))
        ]
    return (
        collect_tokens(result, result_got, result_other, below),
        jnp.where(kept_part[0], kept_part[1], moved.astype(wide)),
        *[jnp.swapaxes(member, 2, 3) for member in results],
    )


def solution(mesh):
    count = mesh.shape["ctx"]
    inner = Mesh(mesh.devices.reshape(mesh.shape["dp"], count // 2, 2), EVERY)
    token_spec, factor_spec = P("dp", CTX, None), P(None, None, EVERY, None)
    in_specs = (
        (token_spec,) * 2 + (P(),) + (P(None, EVERY, None),) * 4 + (P(),) * 8 + (factor_spec,) * 8
    )
    out_specs = (token_spec,) * 2 + (factor_spec,) * 8
    return jax.shard_map(local, mesh=inner, in_specs=in_specs, out_specs=out_specs, check_vma=False)
```

```python
import functools

import jax
import jax.numpy as jnp
from jax import lax
from jax.experimental import pallas as pl
from jax.experimental.pallas import tpu as pltpu
from jax.sharding import Mesh
from jax.sharding import PartitionSpec as P

HEADS = 16
HEAD_DIM = 64
RANK = 16
ADAPTERS = 8
LAYERS = 2

WHOLE, PIECES, GATHERED, MIXED = range(4)
MICROSECOND = 10**8
BLK = 256

epsilon = 1e-05
root_factor = 0.7978845608028654
low_type = jnp.bfloat16
wide = jnp.float32

ROWS_BY_ROWS = (((1,), (1,)), ((), ()))
COLS_BY_COLS = (((0,), (0,)), ((), ()))
PLAIN = (((1,), (0,)), ((), ()))
EVERY = ("dp", "chip", "core")
LANE = ("dp", "chip")
CTX = ("chip", "core")


def times(left_side, right_side, dims=PLAIN):
    return lax.dot_general(left_side, right_side, dims, preferred_element_type=wide)


def block_steps(place, pieces):
    steps = [(0, 0, 0), (0, 1, 0), (0, 1, 1)]
    for piece in range(1, pieces):
        slot = jnp.where(place >= piece, 0, 1)
        steps += [(piece, slot, 0), (piece, 1, slot)]
    return steps


def block_rows(slot):
    return pl.ds(slot * BLK if isinstance(slot, int) else pl.multiple_of(slot * BLK, BLK), BLK)


def stack_heads(rows, mask):
    zero = jnp.zeros_like(rows)
    return jnp.concatenate([jnp.where(mask, rows, zero), jnp.where(mask, zero, rows)], axis=0)


def update_slot(held, slot, change):
    if isinstance(slot, int):
        return [change(member) if which == slot else member for which, member in enumerate(held)]
    return [jnp.where(slot == which, change(member), member) for which, member in enumerate(held)]


def pick_slot(held, slot):
    return held[slot] if isinstance(slot, int) else jnp.where(slot == 0, held[0], held[1])


def attend_forward_kernel(pieces, place_ref, q_ref, *refs):
    k_refs, v_refs = refs[:pieces], refs[pieces : 2 * pieces]
    o_ref, stat_ref, queries, scores, total = refs[2 * pieces :]
    mask = lax.broadcasted_iota(jnp.int32, (BLK, 2 * HEAD_DIM), 1) < HEAD_DIM
    for slot in range(2):
        queries[slot] = stack_heads(q_ref[block_rows(slot), :] * HEAD_DIM**-0.5, mask)
    steps = block_steps(place_ref[0], pieces)
    peaks = [jnp.full((1, 2 * BLK), -1e30, wide)] * 2
    for step, (piece, slot, key_slot) in enumerate(steps):
        block = times(k_refs[piece][block_rows(key_slot), :], queries[slot], ROWS_BY_ROWS)
        scores[step] = block
        top = jnp.max(block, axis=0, keepdims=True)
        peaks = update_slot(peaks, slot, lambda held, top=top: jnp.maximum(held, top))
    total[...] = jnp.zeros_like(total)
    sums = [jnp.zeros((1, 2 * BLK), wide)] * 2
    for step, (piece, slot, key_slot) in enumerate(steps):
        weights = jnp.exp(scores[step] - pick_slot(peaks, slot))
        part = jnp.sum(weights, axis=0, keepdims=True)
        sums = update_slot(sums, slot, lambda held, part=part: held + part)
        weights = weights.astype(low_type)
        turned = v_refs[piece][block_rows(key_slot), :].T
        total[slot] = total[slot] + jnp.concatenate(
            [
                times(turned[:HEAD_DIM], weights[:, :BLK]),
                times(turned[HEAD_DIM:], weights[:, BLK:]),
            ],
            axis=0,
        )
    for slot in range(2):
        share = 1.0 / sums[slot]
        held = total[slot]
        held = jnp.concatenate(
            [held[:HEAD_DIM] * share[:, :BLK], held[HEAD_DIM:] * share[:, BLK:]], axis=0
        )
        o_ref[block_rows(slot), :] = held.T
        stat_ref[0, slot : slot + 1, :] = peaks[slot] + jnp.log(sums[slot])


def attend_backward_kernel(pieces, place_ref, q_ref, g_ref, o_ref, stat_ref, *refs):
    k_refs, v_refs = refs[:pieces], refs[pieces : 2 * pieces]
    dq_ref, dk_refs, dv_refs = refs[2 * pieces], refs[2 * pieces + 1 : 3 * pieces + 1], refs[3 * pieces + 1 : 4 * pieces + 1]
    queries, grads, key_sum, value_sum, query_sum, inner = refs[4 * pieces + 1 :]
    mask = lax.broadcasted_iota(jnp.int32, (BLK, 2 * HEAD_DIM), 1) < HEAD_DIM
    for slot in range(2):
        rows = block_rows(slot)
        queries[slot] = stack_heads(q_ref[rows, :] * HEAD_DIM**-0.5, mask)
        grad = g_ref[rows, :]
        grads[slot] = stack_heads(grad, mask)
        both = (grad.astype(wide) * o_ref[rows, :]).T
        inner[slot] = jnp.concatenate(
            [
                jnp.sum(both[:HEAD_DIM], axis=0, keepdims=True),
                jnp.sum(both[HEAD_DIM:], axis=0, keepdims=True),
            ],
            axis=1,
        )
    key_sum[...] = jnp.zeros_like(key_sum)
    value_sum[...] = jnp.zeros_like(value_sum)
    query_sum[...] = jnp.zeros_like(query_sum)
    for piece, slot, key_slot in block_steps(place_ref[0], pieces):
        at = block_rows(key_slot)
        keys, values = k_refs[piece][at, :], v_refs[piece][at, :]
        own, grad = queries[slot], grads[slot]
        probs = jnp.exp(times(keys, own, ROWS_BY_ROWS) - stat_ref[0, pl.ds(slot, 1), :])
        dscores = probs * (times(values, grad, ROWS_BY_ROWS) - inner[slot])
        dscores = dscores.astype(low_type)
        value_sum[piece, at, :] = value_sum[piece, at, :] + times(probs.astype(low_type), grad)
        key_sum[piece, at, :] = key_sum[piece, at, :] + times(dscores, own)
        turned = keys.T
        query_sum[slot] = query_sum[slot] + jnp.concatenate(
            [
                times(turned[:HEAD_DIM], dscores[:, :BLK]),
                times(turned[HEAD_DIM:], dscores[:, BLK:]),
            ],
            axis=0,
        )
    for slot in range(2):
        dq_ref[block_rows(slot), :] = (query_sum[slot].T * HEAD_DIM**-0.5).astype(low_type)
    for piece in range(pieces):
        dk_refs[piece][...] = key_sum[piece].astype(low_type)
        dv_refs[piece][...] = value_sum[piece].astype(low_type)


def attention_specs():
    own = pl.BlockSpec((2 * BLK, 2 * HEAD_DIM), lambda pair, place: (0, pair))
    stats = pl.BlockSpec((1, 2, 2 * BLK), lambda pair, place: (pair, 0, 0))
    return own, stats


def attend_forward(place, queries, keys, values):
    pieces, pairs = len(keys), queries.shape[1] // (2 * HEAD_DIM)
    own, stats = attention_specs()
    return pl.pallas_call(
        functools.partial(attend_forward_kernel, pieces),
        out_shape=(
            jax.ShapeDtypeStruct(queries.shape, wide),
            jax.ShapeDtypeStruct((pairs, 2, 2 * BLK), wide),
        ),
        grid_spec=pltpu.PrefetchScalarGridSpec(
            num_scalar_prefetch=1,
            grid=(pairs,),
            in_specs=[own] * (1 + 2 * pieces),
            out_specs=[own, stats],
            scratch_shapes=[
                pltpu.VMEM((2, 2 * BLK, 2 * HEAD_DIM), low_type),
                pltpu.VMEM((2 * pieces + 1, BLK, 2 * BLK), wide),
                pltpu.VMEM((2, 2 * HEAD_DIM, BLK), wide),
            ],
        ),
        compiler_params=pltpu.CompilerParams(vmem_limit_bytes=62 * 2**20),
        cost_estimate=pl.CostEstimate(flops=13 * MICROSECOND, bytes_accessed=0, transcendentals=0),
        name="attend_forward",
    )(place, queries, *keys, *values)


def attend_backward(place, queries, keys, values, grads, attended, stat):
    pieces, pairs = len(keys), queries.shape[1] // (2 * HEAD_DIM)
    own, stats = attention_specs()
    query_grad, *others = pl.pallas_call(
        functools.partial(attend_backward_kernel, pieces),
        out_shape=(jax.ShapeDtypeStruct(queries.shape, low_type),) * (1 + 2 * pieces),
        grid_spec=pltpu.PrefetchScalarGridSpec(
            num_scalar_prefetch=1,
            grid=(pairs,),
            in_specs=[own, own, own, stats] + [own] * (2 * pieces),
            out_specs=[own] * (1 + 2 * pieces),
            scratch_shapes=[
                pltpu.VMEM((2, 2 * BLK, 2 * HEAD_DIM), low_type),
                pltpu.VMEM((2, 2 * BLK, 2 * HEAD_DIM), low_type),
                pltpu.VMEM((pieces, 2 * BLK, 2 * HEAD_DIM), wide),
                pltpu.VMEM((pieces, 2 * BLK, 2 * HEAD_DIM), wide),
                pltpu.VMEM((2, 2 * HEAD_DIM, BLK), wide),
                pltpu.VMEM((2, 1, 2 * BLK), wide),
            ],
        ),
        compiler_params=pltpu.CompilerParams(vmem_limit_bytes=62 * 2**20),
        cost_estimate=pl.CostEstimate(flops=21 * MICROSECOND, bytes_accessed=0, transcendentals=0),
        name="attend_backward",
    )(place, queries, grads, attended, stat, *keys, *values)
    return query_grad, others[:pieces], others[pieces:]


def spread_across(pair, below, count):
    half = count // 2
    across = [(b, half + b if b < half else count - 1 - b) for b in range(count)]
    return lax.ppermute(jnp.where(below, pair[1], pair[0]), CTX, across)


def spread_inside(pair, count):
    half = count // 2
    return lax.ppermute(pair[1], CTX, [(b, half + count - 1 - b) for b in range(half, count)])


def joined_tokens(pair, got, other, below):
    return jnp.concatenate(
        [jnp.where(below, pair[0], got), jnp.where(below, got, other)], axis=0
    )


def spread_tokens(pair, below, count):
    return joined_tokens(pair, spread_across(pair, below, count), spread_inside(pair, count), below)


def send_across(rows, below, count):
    half = count // 2
    across = [(half + b if b < half else count - 1 - b, b) for b in range(count)]
    return lax.ppermute(jnp.where(below, rows[BLK:], rows[:BLK]), CTX, across)


def send_inside(rows, count):
    half = count // 2
    inside = [(half + count - 1 - b, b) for b in range(half, count)]
    return lax.ppermute(rows[BLK:], CTX, inside)


def collect_tokens(rows, got, other, below):
    return jnp.stack([jnp.where(below, rows[:BLK], got), jnp.where(below, got, other)])


def collect_own(rows, below):
    mask = jnp.stack([below, jnp.zeros_like(below)])[:, None, None]
    return mask, jnp.stack([rows[:BLK], rows[:BLK]])


def ring_gather(rows, count):
    half = count // 2
    pieces = [rows]
    for step in range(1, half):
        pairs = [
            (side * half + b, side * half + (b + step) % half)
            for side in range(2)
            for b in range(half)
        ]
        pieces.append(lax.ppermute(rows, CTX, pairs))
    return pieces


def ring_scatter(pieces, count):
    half = count // 2
    arrived = []
    for step in range(1, half):
        pairs = [
            (side * half + b, side * half + (b - step) % half)
            for side in range(2)
            for b in range(half)
        ]
        arrived.append(lax.ppermute(pieces[step], CTX, pairs))
    return arrived


def add_up(members):
    return sum(member.astype(wide) for member in members).astype(low_type)


def ring_position(z):
    return jnp.where(z == 2, 3, jnp.where(z == 3, 2, z))


SWAP = [(0, 1), (1, 0)]
RING = [(z * 2 + x, after * 2 + x) for z, after in enumerate((1, 3, 0, 2)) for x in range(2)]
ACROSS_X = [(d, d ^ 1) for d in range(8)]


def along_z(rows):
    return lax.ppermute(rows, "dp", RING)


def along_x(rows):
    return lax.ppermute(rows, "dp", ACROSS_X)


def along_y(rows):
    return lax.ppermute(rows, "chip", SWAP)


def on_chip(rows):
    return lax.ppermute(rows, "core", SWAP)


def join(*members):
    return jnp.concatenate(members, axis=0)


def by_z(ring, first, rows, position):
    parts = [member[first : first + rows] for member in ring]
    placed = []
    for spot in (0, 1, 3, 2):
        step = lax.rem(position + 4 - spot, 4)
        chosen = parts[3]
        for index in (2, 1, 0):
            chosen = jnp.where(step == index, parts[index], chosen)
        placed.append(chosen)
    return jnp.stack(placed)


def z_halves(ring, position):
    size = ring[0].shape[0] // 2
    return [by_z(ring, part * size, size, position) for part in range(2)]


def cross(halves):
    return [along_x(halves[0]), along_y(halves[1])]


def cross_other(halves):
    return [along_y(halves[0]), along_x(halves[1])]


def paired(halves, crossed):
    return [jnp.stack([halves[part], crossed[part]]) for part in range(2)]


def swapped(members):
    return [on_chip(member) for member in members]


def linked_forward(
    first, second, chosen, tokens, cotangent, sizes, at, below, count, kept, attention_step, output_step, feed_step
):
    position = at[0]

    def gather(rows):
        whole = lax.all_gather(rows, EVERY, axis=0)
        return whole.reshape(4, 2, 2, 2, *rows.shape)

    v = Bag()
    v.f, v.g, v.h = [first[:128]], [second[:128]], [second[128:256]]
    first_feed, second_reduce = gather(first[128:]), gather(second[256:])

    def advance(ring):
        ring.append(along_z(ring[-1]))

    def mix(near, far):
        return near[0], far[0], near[1], far[1]

    def weights_f():
        return mix(v.f_near, v.f_far) + mix(v.f_near_other, v.f_far_other)

    def weights_g():
        return mix(v.g_near, v.g_far) + mix(v.g_near_other, v.g_far_other)

    def weights_h():
        return mix(v.h_near, v.h_far) + mix(v.h_near_other, v.h_far_other)

    for _ in range(3):
        advance(v.f)
    v.tokens = spread_tokens(tokens, below, count)
    v.chosen = chosen
    v = sync(v)
    v.f_half = z_halves(v.f, position)
    del v.f
    v.f_cross = cross(v.f_half)
    v.factors = lax.all_to_all(v.chosen, LANE, split_axis=0, concat_axis=0, tiled=True)
    del v.chosen
    advance(v.g)
    v = sync(v)
    v.f_near = paired(v.f_half, v.f_cross)
    del v.f_half, v.f_cross
    v.f_far = cross_other(v.f_near)
    v.f_near_other = swapped(v.f_near)
    v.factors_other = on_chip(v.factors)
    advance(v.g)
    advance(v.g)
    v = sync(v)
    v.g_half = z_halves(v.g, position)
    del v.g
    v.g_cross = cross(v.g_half)
    v.f_far_other = swapped(v.f_far)
    v.picked = unpack_factors(at, v.factors, v.factors_other, sizes)
    del v.factors, v.factors_other
    advance(v.h)
    v = sync(v)
    v.g_near = paired(v.g_half, v.g_cross)
    del v.g_half, v.g_cross
    v.g_far = cross_other(v.g_near)
    v.g_near_other = swapped(v.g_near)
    advance(v.h)
    advance(v.h)
    v.current = v.tokens
    del v.tokens
    attention_step(v.current, (PIECES, weights_f()), v.picked[0], 0)
    v.middle = output_step(v.current, (PIECES, weights_f()), v.picked[0], 0)
    del v.current
    v.kept = kept
    v = sync(v)
    kept[:] = v.kept
    v.h_half = z_halves(v.h, position)
    del v.h
    v.h_cross = cross(v.h_half)
    v.g_far_other = swapped(v.g_far)
    v.current = feed_step(v.middle, (GATHERED, (first_feed,)), v.picked[0], 0)
    v.kept = kept
    v = sync(v)
    kept[:] = v.kept
    v.h_near = paired(v.h_half, v.h_cross)
    del v.h_half, v.h_cross
    v.h_far = cross_other(v.h_near)
    v.h_near_other = swapped(v.h_near)
    v.cotangent_other = spread_inside(cotangent, count)
    attention_step(v.current, (PIECES, weights_g()), v.picked[1], 1)
    v.middle = output_step(v.current, (PIECES, weights_g()), v.picked[1], 1)
    del v.current
    v.kept = kept
    v = sync(v)
    kept[:] = v.kept
    v.h_far_other = swapped(v.h_far)
    cotangent_got = spread_across(cotangent, below, count)
    frozen = [
        ((PIECES, weights_f()), (GATHERED, (first_feed,))),
        ((PIECES, weights_g()), (MIXED, (*weights_h(), second_reduce))),
    ]
    current = feed_step(v.middle, frozen[1][1], v.picked[1], 1)
    current, cotangent_got = sync((current, cotangent_got))
    cotangent = joined_tokens(cotangent, cotangent_got, v.cotangent_other, below)
    return current, cotangent, v.picked, frozen


SQUARE = (4, 2, 2, 2, 32, 1024)
TALL = (4, 2, 2, 2, 128, 1024)


def square_unit(form, part):
    return part if form == WHOLE else (part // 2, part % 2 * 32)


def expand_unit(form, part):
    return {WHOLE: part, GATHERED: 32 * part}.get(form, (part // 2, part % 2 * 32))


def fetch(form, at_ref, sources, unit, rows, held, arrived, by_quarter=None):
    spread_z = slice(None) if by_quarter is None else by_quarter
    if not isinstance(unit, tuple):
        if form == WHOLE:
            source = sources[unit].at[spread_z]
        else:
            source = sources[-1].at[(spread_z, *[slice(None)] * 3, pl.ds(unit, rows), slice(None))]
        pltpu.make_async_copy(source, held.at[spread_z], arrived).start()
        return
    part, first = unit
    x, y, core = at_ref[1], at_ref[2], at_ref[3]
    for other in range(2):
        for far in range(2):
            source = sources[other * 4 + part * 2 + far]
            for over in range(2):
                over_x, over_y = (over, far) if part == 0 else (far, over)
                pltpu.make_async_copy(
                    source.at[over, spread_z, pl.ds(first, rows), :],
                    held.at[
                        spread_z,
                        lax.rem(x + over_x, 2),
                        lax.rem(y + over_y, 2),
                        lax.rem(core + other, 2),
                    ],
                    arrived,
                ).start()


def wait_for(held, arrived):
    pltpu.make_async_copy(held, held, arrived).wait()


def square(held):
    return held[...].reshape(1024, 1024)


QKV_TILE, OUTPUT_TILE, FEED_TILE, TURN_TILE, QKV_BACK_TILE = 0, 0, 512, 512, 512
STRIP = 64
QKV_ROWS, OUTPUT_ROWS, QKV_BACK_ROWS, FEED_BACK_ROWS = 256, 256, 256, 256
COLUMNS = 1024


def strips(count, body):
    def step(index, carry):
        body(pl.ds(pl.multiple_of(index * STRIP, STRIP), STRIP))
        return carry

    lax.fori_loop(0, count // STRIP, step, 0, unroll=True)


def normalize_rows(values, gain, shift):
    center = jnp.mean(values, axis=-1, keepdims=True)
    spread = values - center
    scale = lax.rsqrt(jnp.mean(spread * spread, axis=-1, keepdims=True) + epsilon)
    unit = spread * scale
    return unit, scale, unit * gain + shift


def normalize_pull(grad, unit, scale, gain):
    scaled = grad * gain
    first = jnp.mean(scaled, axis=-1, keepdims=True)
    second = jnp.mean(scaled * unit, axis=-1, keepdims=True)
    return scale * (scaled - first - unit * second)


def store_norm(values_ref, gain_ref, shift_ref, normed_ref, unit_ref, scale_ref):
    def norm(rows):
        unit, scale, normed = normalize_rows(values_ref[rows, :].astype(wide), gain_ref[...], shift_ref[...])
        normed_ref[rows, :] = normed.astype(low_type)
        unit_ref[rows, :] = unit.astype(low_type)
        scale_ref[rows, :] = jnp.broadcast_to(scale, (STRIP, 128))

    strips(values_ref.shape[0], norm)


def store_pull(out_ref, grad_ref, inner_ref, unit_ref, scale_ref, gain_ref):
    def pull(rows):
        out_ref[rows, :] = grad_ref[rows, :].astype(wide) + normalize_pull(
            inner_ref[rows, :], unit_ref[rows, :].astype(wide), scale_ref[rows, :1], gain_ref[...]
        )

    strips(out_ref.shape[0], pull)


def row_tiles(count, size):
    return [slice(first, first + size) for first in range(0, count, size)]


def span(part):
    return slice(part * COLUMNS, (part + 1) * COLUMNS)


TILED = [False]


def at_first(body):
    if TILED[0]:
        pl.when(pl.program_id(0) == 0)(body)
    else:
        body()


def at_last(body):
    if TILED[0]:
        pl.when(pl.program_id(0) == pl.num_programs(0) - 1)(body)
    else:
        body()


def await_first(held, arrived):
    at_first(lambda: wait_for(held, arrived))


def gather_sum(total, step_value):
    @at_first
    def _():
        total[...] = step_value

    if TILED[0]:

        @pl.when(pl.program_id(0) > 0)
        def _():
            total[...] = total[...] + step_value


def qkv_kernel(form, at_ref, x_ref, gain_ref, shift_ref, left_ref, right_ref, bias_ref, *refs):
    sources, (normed_ref, unit_ref, scale_ref, rank_ref, *outs) = refs[:-9], refs[-9:-2]
    held, arrived = refs[-2:]

    @at_first
    def _():
        for part in range(3):
            fetch(form, at_ref, sources, square_unit(form, part), 32, held.at[part], arrived.at[part])

    store_norm(x_ref, gain_ref, shift_ref, normed_ref, unit_ref, scale_ref)
    rank_ref[...] = times(normed_ref[...], left_ref[...], ROWS_BY_ROWS).astype(low_type)
    for part, out in enumerate(outs):
        await_first(held.at[part], arrived.at[part])
        for rows in row_tiles(out.shape[0], QKV_ROWS):
            out[rows, :] = (
                times(normed_ref[rows, :], square(held.at[part]))
                + times(rank_ref[rows, :], right_ref[:, span(part)])
                + bias_ref[:, span(part)]
            ).astype(low_type)


def output_kernel(form, at_ref, x_ref, attended_ref, left_ref, right_ref, bias_ref, gain_ref, shift_ref, *refs):
    sources, (low_ref, middle_ref, normed_ref, unit_ref, scale_ref, rank_ref) = refs[:-8], refs[-8:-2]
    held, arrived = refs[-2:]
    at_first(lambda: fetch(form, at_ref, sources, square_unit(form, 3), 32, held, arrived))
    low_ref[...] = attended_ref[...].astype(low_type)
    rank_ref[...] = times(low_ref[...], left_ref[...], ROWS_BY_ROWS).astype(low_type)
    await_first(held, arrived)
    for rows in row_tiles(x_ref.shape[0], OUTPUT_ROWS):
        middle_ref[rows, :] = (
            x_ref[rows, :].astype(wide)
            + times(low_ref[rows, :], square(held))
            + times(rank_ref[rows, :], right_ref[...])
            + bias_ref[...]
        )
    store_norm(middle_ref, gain_ref, shift_ref, normed_ref, unit_ref, scale_ref)


def fetch_feed_part(form, at_ref, sources, part, expand, reduce, arrived, reduce_first):
    jobs = [
        (expand_unit(form, part), 32, expand.at[part], arrived.at[0, part], None),
        ({WHOLE: 4, GATHERED: 128, MIXED: 0}[form], 128, reduce, arrived.at[1, part], part),
    ]
    for unit, rows, held, semaphore, quarter in jobs[::-1] if reduce_first else jobs:
        fetch(form, at_ref, sources, unit, rows, held, semaphore, quarter)


def fetch_feed_forward(form, at_ref, sources, expand, reduce, arrived, reduce_first):
    for part in range(4):
        fetch_feed_part(form, at_ref, sources, part, expand, reduce, arrived, reduce_first)


def feed_forward_kernel(
    form, at_ref, normed_ref, middle_ref, expand_left_ref, expand_right_ref, expand_bias_ref,
    reduce_left_ref, reduce_right_ref, reduce_bias_ref, *refs,
):
    sources, (result_ref, slope_ref, active_ref, rank_expand_ref, rank_reduce_ref) = refs[:-9], refs[-9:-4]
    expand, reduce, rank_sum, arrived = refs[-4:]
    at_first(lambda: fetch_feed_forward(form, at_ref, sources, expand, reduce, arrived, False))
    rank_expand_ref[...] = times(normed_ref[...], expand_left_ref[...], ROWS_BY_ROWS).astype(low_type)
    result_ref[...] = middle_ref[...] + reduce_bias_ref[...]
    rank_sum[...] = jnp.zeros_like(rank_sum)

    def part_step(part, carry):
        columns = pl.ds(pl.multiple_of(part * COLUMNS, COLUMNS), COLUMNS)
        await_first(expand.at[part], arrived.at[0, part])
        await_first(reduce.at[part], arrived.at[1, part])
        value = (
            times(normed_ref[...], square(expand.at[part]))
            + times(rank_expand_ref[...], expand_right_ref[:, columns])
            + expand_bias_ref[:, columns]
        )
        squared = value * value
        bent = jnp.tanh(value * (root_factor + 0.044715 * root_factor * squared))
        half = 0.5 + 0.5 * bent
        slope_ref[:, columns] = (
            half
            + value * (0.5 - 0.5 * bent * bent) * (root_factor + 3 * 0.044715 * root_factor * squared)
        ).astype(low_type)
        active = (value * half).astype(low_type)
        active_ref[:, columns] = active
        result_ref[...] = result_ref[...] + times(active, square(reduce.at[part]))
        rank_sum[...] = rank_sum[...] + times(active, reduce_left_ref[:, columns], ROWS_BY_ROWS)
        return carry

    lax.fori_loop(0, 4, part_step, 0)
    rank_reduce_ref[...] = rank_sum[...].astype(low_type)
    result_ref[...] = result_ref[...] + times(rank_reduce_ref[...], reduce_right_ref[...])


def feed_output_backward_kernel(
    form, output_form, members, at_ref, grad_ref, normed_ref, unit_ref, scale_ref, rank_expand_ref, rank_reduce_ref,
    attended_ref, rank_output_ref, gain_ref, output_left_ref, output_right_ref, expand_left_ref, expand_right_ref,
    reduce_left_ref, reduce_right_ref, slope_ref, active_ref, *refs,
):
    sources, output_sources, outs, scratch = refs[:members], refs[members:-23], refs[-23:-15], refs[-15:]
    middle_ref, out_ref, output_left_g, output_right_g, expand_left_g, expand_right_g, reduce_left_g, reduce_right_g = outs
    (
        expand, reduce, arrived, held, held_arrived, slope, active, side_arrived,
        low_grad, turned, bent, total, turn_sum, low_middle, output_turned,
    ) = scratch
    for part in range(4):
        for which, (source, kept) in enumerate(((slope_ref, slope), (active_ref, active))):
            pltpu.make_async_copy(
                source.at[:, span(part)], kept.at[part], side_arrived.at[which, part]
            ).start()
        fetch_feed_part(form, at_ref, sources, part, expand, reduce, arrived, True)
    fetch(output_form, at_ref, output_sources, square_unit(output_form, 3), 32, held, held_arrived)
    low_grad[...] = grad_ref[...].astype(low_type)
    turned[...] = times(low_grad[...], reduce_right_ref[...], ROWS_BY_ROWS).astype(low_type)
    reduce_right_g[...] = times(rank_reduce_ref[...], low_grad[...], COLS_BY_COLS).astype(low_type)
    total[...] = jnp.zeros_like(total)
    turn_sum[...] = jnp.zeros_like(turn_sum)

    def part_step(part, carry):
        columns = pl.ds(pl.multiple_of(part * COLUMNS, COLUMNS), COLUMNS)
        wait_for(slope.at[part], side_arrived.at[0, part])
        wait_for(active.at[part], side_arrived.at[1, part])
        wait_for(reduce.at[part], arrived.at[1, part])
        wait_for(expand.at[part], arrived.at[0, part])
        for rows in row_tiles(grad_ref.shape[0], FEED_BACK_ROWS):
            grad_active = times(low_grad[rows, :], square(reduce.at[part]), ROWS_BY_ROWS) + times(
                turned[rows, :], reduce_left_ref[:, columns]
            )
            bent[rows, :] = (grad_active * slope[part, rows, :].astype(wide)).astype(low_type)
            total[rows, :] = total[rows, :] + times(bent[rows, :], square(expand.at[part]), ROWS_BY_ROWS)
        turn_sum[...] = turn_sum[...] + times(bent[...], expand_right_ref[:, columns], ROWS_BY_ROWS)
        reduce_left_g[:, columns] = times(turned[...], active[part], COLS_BY_COLS).astype(low_type)
        expand_right_g[:, columns] = times(rank_expand_ref[...], bent[...], COLS_BY_COLS).astype(low_type)
        return carry

    lax.fori_loop(0, 4, part_step, 0)
    turned[...] = turn_sum[...].astype(low_type)
    expand_left_g[...] = times(turned[...], normed_ref[...], COLS_BY_COLS).astype(low_type)
    total[...] = total[...] + times(turned[...], expand_left_ref[...])
    store_pull(middle_ref, grad_ref, total, unit_ref, scale_ref, gain_ref)
    low_middle[...] = middle_ref[...].astype(low_type)
    output_turned[...] = times(low_middle[...], output_right_ref[...], ROWS_BY_ROWS).astype(low_type)
    output_right_g[...] = times(rank_output_ref[...], low_middle[...], COLS_BY_COLS).astype(low_type)
    output_left_g[...] = times(output_turned[...], attended_ref[...], COLS_BY_COLS).astype(low_type)
    wait_for(held, held_arrived)
    out_ref[...] = (
        times(low_middle[...], square(held), ROWS_BY_ROWS) + times(output_turned[...], output_left_ref[...])
    ).astype(low_type)


def qkv_turn_kernel(pieces, form, at_ref, normed_ref, rank_ref, dq_ref, *refs):
    dk_refs, dv_refs, (right_ref, *refs) = refs[:pieces], refs[pieces : 2 * pieces], refs[2 * pieces :]
    dk_ref, dv_ref, turned_ref, left_g, right_g, left_sum, right_sum = refs
    dk_ref[...] = add_up([member[...] for member in dk_refs])
    dv_ref[...] = add_up([member[...] for member in dv_refs])
    grads = (dq_ref, dk_ref, dv_ref)
    turned = sum(
        times(grads[part][...], right_ref[:, span(part)], ROWS_BY_ROWS) for part in range(3)
    ).astype(low_type)
    turned_ref[...] = turned
    gather_sum(left_sum, times(turned, normed_ref[...], COLS_BY_COLS))
    for part in range(3):
        gather_sum(right_sum.at[part], times(rank_ref[...], grads[part][...], COLS_BY_COLS))

    @at_last
    def _():
        left_g[...] = left_sum[...].astype(low_type)
        for part in range(3):
            right_g[:, span(part)] = right_sum[part].astype(low_type)


def qkv_backward_kernel(
    form, at_ref, grad_ref, unit_ref, scale_ref, turned_ref, dq_ref, dk_ref, dv_ref, gain_ref, left_ref, *refs
):
    sources, (out_ref, low_ref), (held, arrived, total) = refs[:-5], refs[-5:-3], refs[-3:]

    @at_first
    def _():
        for part in range(3):
            fetch(form, at_ref, sources, square_unit(form, part), 32, held.at[part], arrived.at[part])

    total[...] = times(turned_ref[...], left_ref[...])
    for part, member in enumerate((dq_ref, dk_ref, dv_ref)):
        await_first(held.at[part], arrived.at[part])
        for rows in row_tiles(out_ref.shape[0], QKV_BACK_ROWS):
            total[rows, :] = total[rows, :] + times(member[rows, :], square(held.at[part]), ROWS_BY_ROWS)
    store_pull(out_ref, grad_ref, total, unit_ref, scale_ref, gain_ref)
    low_ref[...] = out_ref[...].astype(low_type)


def qkv_whole_kernel(
    pieces, form, at_ref, grad_ref, unit_ref, scale_ref, normed_ref, rank_ref, dq_ref, *refs
):
    dk_refs, dv_refs, (gain_ref, left_ref, right_ref, *refs) = refs[:pieces], refs[pieces : 2 * pieces], refs[2 * pieces :]
    sources, (out_ref, left_g, right_g) = refs[:-9], refs[-9:-6]
    held, arrived, turned, total, dk_ref, dv_ref = refs[-6:]
    for part in range(3):
        fetch(form, at_ref, sources, square_unit(form, part), 32, held.at[part], arrived.at[part])
    dk_ref[...] = add_up([member[...] for member in dk_refs])
    dv_ref[...] = add_up([member[...] for member in dv_refs])
    grads = (dq_ref, dk_ref, dv_ref)
    turned[...] = sum(
        times(grads[part][...], right_ref[:, span(part)], ROWS_BY_ROWS) for part in range(3)
    ).astype(low_type)
    for part in range(3):
        right_g[:, span(part)] = times(rank_ref[...], grads[part][...], COLS_BY_COLS).astype(low_type)
    left_g[...] = times(turned[...], normed_ref[...], COLS_BY_COLS).astype(low_type)
    for part, member in enumerate(grads):
        wait_for(held.at[part], arrived.at[part])
        for rows in row_tiles(out_ref.shape[0], QKV_BACK_ROWS):
            value = times(member[rows, :], square(held.at[part]), ROWS_BY_ROWS)
            before = total[rows, :] if part else times(turned[rows, :], left_ref[...])
            total[rows, :] = before + value
    store_pull(out_ref, grad_ref, total, unit_ref, scale_ref, gain_ref)


def frozen_call(kernel, name, at, weights, tile, tiled, fixed, outs, fixed_outs, scratch, cost):
    form, sources = weights
    count = tiled[0].shape[0]
    TILED[0] = tile > 0

    def by_rows(shape):
        if tile == 0:
            return pl.BlockSpec(memory_space=pltpu.VMEM)
        return pl.BlockSpec((tile, shape[1]), lambda step: (step, 0))

    def every(shape):
        if tile == 0:
            return pl.BlockSpec(memory_space=pltpu.VMEM)
        return pl.BlockSpec(shape, lambda step: (0, 0))

    return pl.pallas_call(
        functools.partial(kernel, form),
        grid=(count // tile,) if tile else (),
        out_shape=tuple(jax.ShapeDtypeStruct(shape, kind) for shape, kind in (*outs, *fixed_outs)),
        in_specs=[pl.BlockSpec(memory_space=pltpu.SMEM)]
        + [by_rows(member.shape) for member in tiled]
        + [every(member.shape) for member in fixed]
        + [pl.BlockSpec(memory_space=pl.ANY)] * len(sources),
        out_specs=tuple(by_rows(shape) for shape, _ in outs) + tuple(every(shape) for shape, _ in fixed_outs),
        scratch_shapes=scratch,
        compiler_params=pltpu.CompilerParams(vmem_limit_bytes=60 * 2**20),
        cost_estimate=pl.CostEstimate(flops=cost * MICROSECOND, bytes_accessed=0, transcendentals=0),
        name=name,
    )(at, *tiled, *fixed, *sources)


def row(vector):
    return vector.reshape(1, -1)


DMA = pltpu.SemaphoreType.DMA


PACKED = ((5, 0), (6, 128), (1, 256), (0, 352), (2, 384), (3, 416), (4, 448), (7, 480))


def unpack_kernel(order, at_ref, own_ref, other_ref, *outs):
    layers, groups = own_ref.shape[1], own_ref.shape[0] // 2
    swapped = at_ref[3] == 1
    for layer_index in range(layers):
        for group in range(groups):
            lanes = []
            for chip in range(2):
                own = own_ref[group * 2 + chip, layer_index]
                other = other_ref[group * 2 + chip, layer_index]
                lanes += [jnp.where(swapped, other, own), jnp.where(swapped, own, other)]
            for kind, first in order:
                out = outs[layer_index * len(order) + kind]
                size = out.shape[1] // (4 * groups)
                out[:, group * 4 * size : (group + 1) * 4 * size] = jnp.concatenate(
                    [lane[:, first : first + size] for lane in lanes], axis=1
                )


def unpack_factors(at, own, other, sizes):
    lanes, layers = own.shape[:2]
    local_spec = pl.BlockSpec(memory_space=pltpu.VMEM)
    found = pl.pallas_call(
        functools.partial(unpack_kernel, PACKED),
        out_shape=tuple(
            jax.ShapeDtypeStruct((RANK, size * lanes * 2), low_type) for _ in range(layers) for size in sizes
        ),
        in_specs=[pl.BlockSpec(memory_space=pltpu.SMEM), local_spec, local_spec],
        out_specs=(local_spec,) * (layers * len(sizes)),
        compiler_params=pltpu.CompilerParams(vmem_limit_bytes=32 * 2**20),
        cost_estimate=pl.CostEstimate(flops=4 * MICROSECOND, bytes_accessed=0, transcendentals=0),
        name="unpack_factors",
    )(at, own, other)
    return [found[layer * len(sizes) : (layer + 1) * len(sizes)] for layer in range(layers)]


def pack_kernel(orders, at_ref, *refs):
    members, out_ref = refs[:-1], refs[-1]
    core, base, offset = at_ref[3], 0, 0
    for order in orders:
        for lane_chip in range(out_ref.shape[1]):
            for owner_core in range(2):
                owner = lane_chip * 2 + owner_core
                parts = []
                for index, _ in enumerate(order):
                    member = members[base + index]
                    size = member.shape[1] // (2 * out_ref.shape[1])
                    parts.append(member[:, owner * size : (owner + 1) * size])
                joined = jnp.concatenate(parts, axis=1)
                out_ref[lax.rem(owner_core + core, 2), lane_chip, :, offset : offset + joined.shape[1]] = joined
        base += len(order)
        offset += joined.shape[1]


def pack_gradients(at, groups, lanes):
    members, width = [], 0
    for order, terms in groups:
        members += [terms[kind] for kind, _ in order]
        width += sum(terms[kind].shape[1] for kind, _ in order) // (2 * lanes)
    local_spec = pl.BlockSpec(memory_space=pltpu.VMEM)
    return pl.pallas_call(
        functools.partial(pack_kernel, [order for order, _ in groups]),
        out_shape=jax.ShapeDtypeStruct((2, lanes, RANK, width), low_type),
        in_specs=[pl.BlockSpec(memory_space=pltpu.SMEM)] + [local_spec] * len(members),
        out_specs=local_spec,
        compiler_params=pltpu.CompilerParams(vmem_limit_bytes=32 * 2**20),
        cost_estimate=pl.CostEstimate(flops=4 * MICROSECOND, bytes_accessed=0, transcendentals=0),
        name="pack_gradients",
    )(at, *members)


LOW, WIDE = low_type, wide


def forward_qkv(current, weights, picked, extras, at):
    rows, columns = current.shape
    full_low = ((rows, columns), LOW)
    bias = jnp.concatenate([extras[0][:columns], jnp.zeros((columns,), WIDE), extras[0][columns:]])
    return frozen_call(
        qkv_kernel, "qkv_forward", at, weights, QKV_TILE, (current,),
        (row(extras[4]), row(extras[5]), picked[0], picked[1], row(bias)),
        (full_low, full_low, ((rows, 128), WIDE), ((rows, RANK), LOW), full_low, full_low, full_low), (),
        [pltpu.VMEM((3, *SQUARE), LOW), DMA((3,))], 9,
    )


def forward_output(current, attended, weights, picked, extras, at):
    rows, columns = current.shape
    full, full_low = ((rows, columns), WIDE), ((rows, columns), LOW)
    return frozen_call(
        output_kernel, "output_forward", at, weights, OUTPUT_TILE, (current, attended),
        (picked[2], picked[3], row(extras[1]), row(extras[6]), row(extras[7])),
        (full_low, full, full_low, full_low, ((rows, 128), WIDE), ((rows, RANK), LOW)), (),
        [pltpu.VMEM(SQUARE, LOW), DMA], 8,
    )


def forward_feed(normed, middle, weights, picked, extras, at):
    rows, columns = middle.shape
    tall, ranks = ((rows, picked[5].shape[1]), LOW), ((rows, RANK), LOW)
    return frozen_call(
        feed_forward_kernel, "feed_forward", at, weights, FEED_TILE, (normed, middle),
        (picked[4], picked[5], row(extras[2]), picked[6], picked[7], row(extras[3])),
        (((rows, columns), WIDE), tall, tall, ranks, ranks), (),
        [
            pltpu.VMEM((4, *SQUARE), LOW), pltpu.VMEM(TALL, LOW), pltpu.VMEM((FEED_TILE or rows, RANK), WIDE),
            DMA((2, 4)),
        ], 20,
    )


def like(member):
    return (member.shape, LOW)


def backward_feed_output(grad, kept, weights, output_weights, picked, extras, at):
    rows, columns = grad.shape
    form, sources = weights
    output_form, output_sources = output_weights
    full, full_low, ranks = ((rows, columns), WIDE), ((rows, columns), LOW), ((rows, RANK), LOW)
    tall = ((4, rows, columns), LOW)
    members = (
        grad, kept.normed_two, kept.unit_two, kept.scale_two, kept.rank_expand, kept.rank_reduce,
        kept.attended_low, kept.rank_output, row(extras[6]), *picked[2:],
    )
    local_spec, anywhere = pl.BlockSpec(memory_space=pltpu.VMEM), pl.BlockSpec(memory_space=pl.ANY)
    outs = (full, full_low, *map(like, picked[2:]))
    return pl.pallas_call(
        functools.partial(feed_output_backward_kernel, form, output_form, len(sources)),
        out_shape=tuple(jax.ShapeDtypeStruct(shape, kind) for shape, kind in outs),
        in_specs=[pl.BlockSpec(memory_space=pltpu.SMEM)]
        + [local_spec] * len(members)
        + [anywhere] * (2 + len(sources) + len(output_sources)),
        out_specs=(local_spec,) * len(outs),
        scratch_shapes=[
            pltpu.VMEM((4, *SQUARE), LOW), pltpu.VMEM(TALL, LOW), DMA((2, 4)), pltpu.VMEM(SQUARE, LOW), DMA,
            pltpu.VMEM(*tall), pltpu.VMEM(*tall), DMA((2, 4)), pltpu.VMEM(*full_low), pltpu.VMEM(*ranks),
            pltpu.VMEM(*full_low), pltpu.VMEM(*full), pltpu.VMEM((rows, RANK), WIDE), pltpu.VMEM(*full_low),
            pltpu.VMEM(*ranks),
        ],
        compiler_params=pltpu.CompilerParams(vmem_limit_bytes=60 * 2**20),
        cost_estimate=pl.CostEstimate(flops=25 * MICROSECOND, bytes_accessed=0, transcendentals=0),
        name="feed_output_backward",
    )(at, *members, kept.slope, kept.active, *sources, *output_sources)


def backward_turn(grads, kept, picked, at):
    query_grad, key_grads, value_grads = grads
    full_low = (query_grad.shape, LOW)
    return frozen_call(
        functools.partial(qkv_turn_kernel, len(key_grads)), "qkv_turn", at, (WHOLE, ()), TURN_TILE,
        (kept.normed_one, kept.rank_attend, query_grad, *key_grads, *value_grads), (picked[1],),
        (full_low, full_low, like(kept.rank_attend)), (like(picked[0]), like(picked[1])),
        [pltpu.VMEM(picked[0].shape, WIDE), pltpu.VMEM((3, *picked[0].shape), WIDE)], 3,
    )


def backward_qkv_whole(grad, grads, kept, weights, picked, extras, at):
    rows, columns = grad.shape
    query_grad, key_grads, value_grads = grads
    return frozen_call(
        functools.partial(qkv_whole_kernel, len(key_grads)), "qkv_whole", at, weights, QKV_BACK_TILE,
        (
            grad, kept.unit_one, kept.scale_one, kept.normed_one, kept.rank_attend, query_grad, *key_grads,
            *value_grads,
        ),
        (row(extras[4]), picked[0], picked[1]),
        (((rows, columns), WIDE),), (like(picked[0]), like(picked[1])),
        [
            pltpu.VMEM((3, *SQUARE), LOW), DMA((3,)), pltpu.VMEM((rows, RANK), LOW),
            pltpu.VMEM((rows, columns), WIDE), pltpu.VMEM((rows, columns), LOW), pltpu.VMEM((rows, columns), LOW),
        ], 11,
    )


def backward_qkv(grad, joined, turned, kept, weights, picked, extras, at):
    rows, columns = grad.shape
    return frozen_call(
        qkv_backward_kernel, "qkv_backward", at, weights, QKV_BACK_TILE,
        (grad, kept.unit_one, kept.scale_one, turned, *joined), (row(extras[4]), picked[0]),
        (((rows, columns), WIDE), ((rows, columns), LOW)), (),
        [pltpu.VMEM((3, *SQUARE), LOW), DMA((3,)), pltpu.VMEM((QKV_BACK_TILE or rows, columns), WIDE)], 9,
    )


def combine_kernel(places, ids_ref, *refs):
    count = len(places)
    received, outs, total = refs[:count], refs[count:-1], refs[-1]
    total[...] = jnp.zeros_like(total)
    for source in range(received[0].shape[0]):
        adapter, spot = ids_ref[source], 0
        for member in received:
            width = member.shape[2]
            at = (adapter, slice(None), slice(spot, spot + width))
            total[at] = total[at] + member[source].astype(wide)
            spot += width
    base = 0
    for member, orders in zip(received, places):
        for layer_index, order in orders:
            for kind, _ in order:
                size = outs[kind].shape[3]
                outs[kind][layer_index] = total[:, :, base : base + size]
                base += size


def combine(ids, received, places, sizes):
    local_spec = pl.BlockSpec(memory_space=pltpu.VMEM)
    width = sum(member.shape[2] for member in received)
    return pl.pallas_call(
        functools.partial(combine_kernel, places),
        out_shape=tuple(jax.ShapeDtypeStruct((LAYERS, ADAPTERS, RANK, size), wide) for size in sizes),
        in_specs=[pl.BlockSpec(memory_space=pltpu.SMEM)] + [local_spec] * len(received),
        out_specs=(local_spec,) * len(sizes),
        scratch_shapes=[pltpu.VMEM((ADAPTERS, RANK, width), wide)],
        compiler_params=pltpu.CompilerParams(vmem_limit_bytes=32 * 2**20),
        cost_estimate=pl.CostEstimate(flops=3 * MICROSECOND, bytes_accessed=0, transcendentals=0),
        name="combine",
    )(ids, *received)


class Bag:
    pass


def open_bag(bag):
    names = tuple(sorted(vars(bag)))
    return tuple(getattr(bag, name) for name in names), names


def close_bag(names, members):
    bag = Bag()
    for name, member in zip(names, members):
        setattr(bag, name, member)
    return bag


jax.tree_util.register_pytree_node(Bag, open_bag, close_bag)


def sync(values):
    leaves, shape = jax.tree.flatten(values)
    return jax.tree.unflatten(shape, lax.optimization_barrier(tuple(leaves)))


def local(
    tokens, cotangent, adapter_ids, attend_weight, output_weight, expand_weight, reduce_weight,
    attend_bias, output_bias, expand_bias, reduce_bias, first_gain, first_shift, second_gain, second_shift,
    *adapters,
):
    data_count, chips = lax.axis_size("dp"), lax.axis_size("chip")
    count = chips * lax.axis_size("core")
    half = count // 2
    devices = data_count * count
    data_rank, core = lax.axis_index("dp"), lax.axis_index("core")
    rank = lax.axis_index("chip") * 2 + core
    below = rank < half
    place = jnp.reshape(lax.rem(rank, half), (1,)).astype(jnp.int32)
    columns = tokens.shape[2]
    linked = (data_count, chips, columns) == (8, 2, 1024)

    lane_chip = jnp.arange(data_count * chips, dtype=jnp.int32)
    lane_sequence = (lane_chip // chips) * 2 + (lane_chip % chips) // (chips // 2)
    lane_adapter = jnp.take(adapter_ids, lane_sequence)

    sizes = [member.shape[2] for member in adapters]
    packed = jnp.concatenate([jnp.swapaxes(adapters[kind], 2, 3) for kind, _ in PACKED], axis=3)
    chosen = jnp.moveaxis(jnp.take(packed, lane_adapter, axis=1), 1, 0)

    def shards(layer_index):
        lists = [attend_weight[layer_index], output_weight[layer_index], expand_weight[layer_index]]
        blocks = [
            member[:, first : first + columns]
            for member in lists
            for first in range(0, member.shape[1], columns)
        ]
        return jnp.concatenate(blocks + [reduce_weight[layer_index]], axis=0)

    extras = [
        tuple(
            member[layer_index]
            for member in (
                attend_bias, output_bias, expand_bias, reduce_bias,
                first_gain, first_shift, second_gain, second_shift,
            )
        )
        for layer_index in range(LAYERS)
    ]
    position = ring_position(data_rank // 2)
    at = jnp.stack([position, data_rank % 2, lax.axis_index("chip"), core]).astype(jnp.int32)
    kept = [Bag(), Bag()]

    def attention_step(current, weights, picked, layer_index):
        keep = kept[layer_index]
        (
            keep.normed_one, keep.unit_one, keep.scale_one, keep.rank_attend,
            keep.queries, keys, values,
        ) = forward_qkv(current, weights, picked, extras[layer_index], at)
        keep.keys, keep.values = ring_gather(keys, count), ring_gather(values, count)
        keep.attended, keep.stat = attend_forward(place, keep.queries, keep.keys, keep.values)

    def output_step(current, weights, picked, layer_index):
        keep = kept[layer_index]
        (
            keep.attended_low, middle, keep.normed_two, keep.unit_two, keep.scale_two,
            keep.rank_output,
        ) = forward_output(current, keep.attended, weights, picked, extras[layer_index], at)
        return middle

    def feed_step(middle, weights, picked, layer_index):
        keep = kept[layer_index]
        result, keep.slope, keep.active, keep.rank_expand, keep.rank_reduce = forward_feed(
            keep.normed_two, middle, weights, picked, extras[layer_index], at
        )
        return result

    if linked:
        first, second = shards(0), shards(1)
        current, grad_current, picked, frozen = linked_forward(
            first, second, chosen, tokens, cotangent, sizes, at, below, count, kept,
            attention_step, output_step, feed_step,
        )
    else:
        current = spread_tokens(tokens, below, count)
        grad_current = spread_tokens(cotangent, below, count)
        mine = lax.all_to_all(chosen, LANE, split_axis=0, concat_axis=0, tiled=True)
        theirs = lax.ppermute(mine, "core", SWAP)
        both = jnp.stack(
            [jnp.where(core == 0, mine, theirs), jnp.where(core == 0, theirs, mine)], axis=1
        )
        places, spot = {}, 0
        for kind, _ in PACKED:
            places[kind] = spot
            spot += sizes[kind]
        picked = [
            tuple(
                jnp.transpose(
                    both[:, :, layer_index, :, places[kind] : places[kind] + size], (2, 0, 1, 3)
                ).reshape(RANK, devices * size)
                for kind, size in enumerate(sizes)
            )
            for layer_index in range(LAYERS)
        ]
        frozen = []
        for layer_index in range(LAYERS):
            whole = lax.all_gather(shards(layer_index), EVERY, axis=0)
            size = columns // devices
            squares = [whole[:, part * size : (part + 1) * size, :].reshape(SQUARE) for part in range(8)]
            tall = whole[:, 8 * size :, :].reshape(TALL)
            frozen.append(((WHOLE, tuple(squares[:4])), (WHOLE, (*squares[4:], tall))))
            first_weights, second_weights = frozen[layer_index]
            attention_step(current, first_weights, picked[layer_index], layer_index)
            middle = output_step(current, first_weights, picked[layer_index], layer_index)
            current = feed_step(middle, second_weights, picked[layer_index], layer_index)

    result = current.astype(low_type)
    result_got, result_other = send_across(result, below, count), send_inside(result, count)
    lanes = data_count * chips

    def to_owners(groups):
        if linked:
            both = pack_gradients(at, groups, lanes)
            own, sent = both[0], both[1]
        else:
            both = jnp.concatenate(
                [
                    jnp.transpose(
                        terms[kind].reshape(RANK, lanes, 2, sizes[kind]), (2, 1, 0, 3)
                    )
                    for order, terms in groups
                    for kind, _ in order
                ],
                axis=3,
            )
            own, sent = jnp.where(core == 0, both[0], both[1]), jnp.where(core == 0, both[1], both[0])
        total = add_up([own, lax.ppermute(sent, "core", SWAP)])
        return lax.all_to_all(total, LANE, split_axis=0, concat_axis=0, tiled=True)

    terms = [None] * LAYERS
    for layer_index in reversed(range(LAYERS)):
        keep, extra, factors = kept[layer_index], extras[layer_index], picked[layer_index]
        first_weights, second_weights = frozen[layer_index]
        middle_grad, attended_grad, *some_terms = backward_feed_output(
            grad_current, keep, second_weights, first_weights, factors, extra, at
        )
        if layer_index == LAYERS - 1:
            middle_grad, attended_grad, some_terms, result_got = sync(
                (middle_grad, attended_grad, some_terms, result_got)
            )
        query_grad, key_grads, value_grads = attend_backward(
            place, keep.queries, keep.keys, keep.values, attended_grad, keep.attended, keep.stat
        )
        if layer_index == LAYERS - 1:
            query_grad, key_grads, value_grads, result_other = sync(
                (query_grad, key_grads, value_grads, result_other)
            )
        grads = (
            query_grad,
            [key_grads[0], *ring_scatter(key_grads, count)],
            [value_grads[0], *ring_scatter(value_grads, count)],
        )
        if layer_index > 0:
            grad_current, *attend_terms = backward_qkv_whole(
                middle_grad, grads, keep, first_weights, factors, extra, at
            )
            terms[layer_index] = [*attend_terms, *some_terms]
            continue
        key_grad, value_grad, turned, *attend_terms = backward_turn(grads, keep, factors, at)
        terms[layer_index] = [*attend_terms, *some_terms]
        received = to_owners([(PACKED, terms[1]), (PACKED, terms[0])])
        grad_current, low_grad = backward_qkv(
            middle_grad, (query_grad, key_grad, value_grad), turned, keep, first_weights, factors, extra, at
        )
    got, other = send_across(low_grad, below, count), send_inside(low_grad, count)
    received, got, other = sync((received, got, other))
    moved = collect_tokens(low_grad, got, other, below)
    kept_part = collect_own(grad_current, below)
    received = [received]
    places = (((1, PACKED), (0, PACKED)),)
    if linked:
        results = combine(lane_adapter, received, places, sizes)
    else:
        owner_adapter = (lane_adapter[:, None] == jnp.arange(ADAPTERS)[None, :]).astype(wide)
        found = [[None] * len(sizes) for _ in range(LAYERS)]
        for held, orders in zip(received, places):
            summed = jnp.einsum(
                "sa,srp->arp", owner_adapter, held.astype(wide), precision=lax.Precision.HIGHEST
            )
            spot = 0
            for layer_index, order in orders:
                for kind, _ in order:
                    found[layer_index][kind] = summed[:, :, spot : spot + sizes[kind]]
                    spot += sizes[kind]
        results = [
            jnp.stack([found[layer_index][kind] for layer_index in range(LAYERS)])
            for kind in range(len(sizes))
        ]
    return (
        collect_tokens(result, result_got, result_other, below),
        jnp.where(kept_part[0], kept_part[1], moved.astype(wide)),
        *[jnp.swapaxes(member, 2, 3) for member in results],
    )


def solution(mesh):
    count = mesh.shape["ctx"]
    inner = Mesh(mesh.devices.reshape(mesh.shape["dp"], count // 2, 2), EVERY)
    token_spec, factor_spec = P("dp", CTX, None), P(None, None, EVERY, None)
    in_specs = (
        (token_spec,) * 2 + (P(),) + (P(None, EVERY, None),) * 4 + (P(),) * 8 + (factor_spec,) * 8
    )
    out_specs = (token_spec,) * 2 + (factor_spec,) * 8
    return jax.shard_map(local, mesh=inner, in_specs=in_specs, out_specs=out_specs, check_vma=False)
```

```python
import functools

import jax
import jax.numpy as jnp
from jax import lax
from jax.experimental import pallas as pl
from jax.experimental.pallas import tpu as pltpu
from jax.sharding import Mesh
from jax.sharding import PartitionSpec as P

HEADS = 16
HEAD_DIM = 64
RANK = 16
ADAPTERS = 8
LAYERS = 2

WHOLE, PIECES, GATHERED, MIXED = range(4)
MICROSECOND = 10**8
BLK = 256

epsilon = 1e-05
root_factor = 0.7978845608028654
low_type = jnp.bfloat16
wide = jnp.float32

ROWS_BY_ROWS = (((1,), (1,)), ((), ()))
COLS_BY_COLS = (((0,), (0,)), ((), ()))
PLAIN = (((1,), (0,)), ((), ()))
EVERY = ("dp", "chip", "core")
LANE = ("dp", "chip")
CTX = ("chip", "core")


def times(left_side, right_side, dims=PLAIN):
    return lax.dot_general(left_side, right_side, dims, preferred_element_type=wide)


def block_steps(place, pieces):
    steps = [(0, 0, 0), (0, 1, 0), (0, 1, 1)]
    for piece in range(1, pieces):
        slot = jnp.where(place >= piece, 0, 1)
        steps += [(piece, slot, 0), (piece, 1, slot)]
    return steps


def block_rows(slot):
    return pl.ds(slot * BLK if isinstance(slot, int) else pl.multiple_of(slot * BLK, BLK), BLK)


def stack_heads(rows, mask):
    zero = jnp.zeros_like(rows)
    return jnp.concatenate([jnp.where(mask, rows, zero), jnp.where(mask, zero, rows)], axis=0)


def update_slot(held, slot, change):
    if isinstance(slot, int):
        return [change(member) if which == slot else member for which, member in enumerate(held)]
    return [jnp.where(slot == which, change(member), member) for which, member in enumerate(held)]


def pick_slot(held, slot):
    return held[slot] if isinstance(slot, int) else jnp.where(slot == 0, held[0], held[1])


def attend_forward_kernel(pieces, place_ref, q_ref, *refs):
    k_refs, v_refs = refs[:pieces], refs[pieces : 2 * pieces]
    o_ref, stat_ref, queries, scores, total = refs[2 * pieces :]
    mask = lax.broadcasted_iota(jnp.int32, (BLK, 2 * HEAD_DIM), 1) < HEAD_DIM
    for slot in range(2):
        queries[slot] = stack_heads(q_ref[block_rows(slot), :] * HEAD_DIM**-0.5, mask)
    steps = block_steps(place_ref[0], pieces)
    peaks = [jnp.full((1, 2 * BLK), -1e30, wide)] * 2
    for step, (piece, slot, key_slot) in enumerate(steps):
        block = times(k_refs[piece][block_rows(key_slot), :], queries[slot], ROWS_BY_ROWS)
        scores[step] = block
        top = jnp.max(block, axis=0, keepdims=True)
        peaks = update_slot(peaks, slot, lambda held, top=top: jnp.maximum(held, top))
    total[...] = jnp.zeros_like(total)
    sums = [jnp.zeros((1, 2 * BLK), wide)] * 2
    for step, (piece, slot, key_slot) in enumerate(steps):
        weights = jnp.exp(scores[step] - pick_slot(peaks, slot))
        part = jnp.sum(weights, axis=0, keepdims=True)
        sums = update_slot(sums, slot, lambda held, part=part: held + part)
        weights = weights.astype(low_type)
        turned = v_refs[piece][block_rows(key_slot), :].T
        total[slot] = total[slot] + jnp.concatenate(
            [
                times(turned[:HEAD_DIM], weights[:, :BLK]),
                times(turned[HEAD_DIM:], weights[:, BLK:]),
            ],
            axis=0,
        )
    for slot in range(2):
        share = 1.0 / sums[slot]
        held = total[slot]
        held = jnp.concatenate(
            [held[:HEAD_DIM] * share[:, :BLK], held[HEAD_DIM:] * share[:, BLK:]], axis=0
        )
        o_ref[block_rows(slot), :] = held.T.astype(low_type)
        stat_ref[0, slot : slot + 1, :] = peaks[slot] + jnp.log(sums[slot])


def attend_backward_kernel(pieces, place_ref, q_ref, g_ref, o_ref, stat_ref, *refs):
    k_refs, v_refs = refs[:pieces], refs[pieces : 2 * pieces]
    dq_ref, dk_refs, dv_refs = refs[2 * pieces], refs[2 * pieces + 1 : 3 * pieces + 1], refs[3 * pieces + 1 : 4 * pieces + 1]
    queries, grads, key_sum, value_sum, query_sum, inner = refs[4 * pieces + 1 :]
    mask = lax.broadcasted_iota(jnp.int32, (BLK, 2 * HEAD_DIM), 1) < HEAD_DIM
    for slot in range(2):
        rows = block_rows(slot)
        queries[slot] = stack_heads(q_ref[rows, :] * HEAD_DIM**-0.5, mask)
        grad = g_ref[rows, :]
        grads[slot] = stack_heads(grad, mask)
        both = (grad.astype(wide) * o_ref[rows, :].astype(wide)).T
        inner[slot] = jnp.concatenate(
            [
                jnp.sum(both[:HEAD_DIM], axis=0, keepdims=True),
                jnp.sum(both[HEAD_DIM:], axis=0, keepdims=True),
            ],
            axis=1,
        )
    key_sum[...] = jnp.zeros_like(key_sum)
    value_sum[...] = jnp.zeros_like(value_sum)
    query_sum[...] = jnp.zeros_like(query_sum)
    for piece, slot, key_slot in block_steps(place_ref[0], pieces):
        at = block_rows(key_slot)
        keys, values = k_refs[piece][at, :], v_refs[piece][at, :]
        own, grad = queries[slot], grads[slot]
        probs = jnp.exp(times(keys, own, ROWS_BY_ROWS) - stat_ref[0, pl.ds(slot, 1), :])
        dscores = probs * (times(values, grad, ROWS_BY_ROWS) - inner[slot])
        dscores = dscores.astype(low_type)
        value_sum[piece, at, :] = value_sum[piece, at, :] + times(probs.astype(low_type), grad)
        key_sum[piece, at, :] = key_sum[piece, at, :] + times(dscores, own)
        turned = keys.T
        query_sum[slot] = query_sum[slot] + jnp.concatenate(
            [
                times(turned[:HEAD_DIM], dscores[:, :BLK]),
                times(turned[HEAD_DIM:], dscores[:, BLK:]),
            ],
            axis=0,
        )
    for slot in range(2):
        dq_ref[block_rows(slot), :] = (query_sum[slot].T * HEAD_DIM**-0.5).astype(low_type)
    for piece in range(pieces):
        dk_refs[piece][...] = key_sum[piece].astype(low_type)
        dv_refs[piece][...] = value_sum[piece].astype(low_type)


def attention_specs():
    own = pl.BlockSpec((2 * BLK, 2 * HEAD_DIM), lambda pair, place: (0, pair))
    stats = pl.BlockSpec((1, 2, 2 * BLK), lambda pair, place: (pair, 0, 0))
    return own, stats


def attend_forward(place, queries, keys, values):
    pieces, pairs = len(keys), queries.shape[1] // (2 * HEAD_DIM)
    own, stats = attention_specs()
    return pl.pallas_call(
        functools.partial(attend_forward_kernel, pieces),
        out_shape=(
            jax.ShapeDtypeStruct(queries.shape, low_type),
            jax.ShapeDtypeStruct((pairs, 2, 2 * BLK), wide),
        ),
        grid_spec=pltpu.PrefetchScalarGridSpec(
            num_scalar_prefetch=1,
            grid=(pairs,),
            in_specs=[own] * (1 + 2 * pieces),
            out_specs=[own, stats],
            scratch_shapes=[
                pltpu.VMEM((2, 2 * BLK, 2 * HEAD_DIM), low_type),
                pltpu.VMEM((2 * pieces + 1, BLK, 2 * BLK), wide),
                pltpu.VMEM((2, 2 * HEAD_DIM, BLK), wide),
            ],
        ),
        compiler_params=pltpu.CompilerParams(vmem_limit_bytes=62 * 2**20),
        cost_estimate=pl.CostEstimate(flops=13 * MICROSECOND, bytes_accessed=0, transcendentals=0),
        name="attend_forward",
    )(place, queries, *keys, *values)


def attend_backward(place, queries, keys, values, grads, attended, stat):
    pieces, pairs = len(keys), queries.shape[1] // (2 * HEAD_DIM)
    own, stats = attention_specs()
    query_grad, *others = pl.pallas_call(
        functools.partial(attend_backward_kernel, pieces),
        out_shape=(jax.ShapeDtypeStruct(queries.shape, low_type),) * (1 + 2 * pieces),
        grid_spec=pltpu.PrefetchScalarGridSpec(
            num_scalar_prefetch=1,
            grid=(pairs,),
            in_specs=[own, own, own, stats] + [own] * (2 * pieces),
            out_specs=[own] * (1 + 2 * pieces),
            scratch_shapes=[
                pltpu.VMEM((2, 2 * BLK, 2 * HEAD_DIM), low_type),
                pltpu.VMEM((2, 2 * BLK, 2 * HEAD_DIM), low_type),
                pltpu.VMEM((pieces, 2 * BLK, 2 * HEAD_DIM), wide),
                pltpu.VMEM((pieces, 2 * BLK, 2 * HEAD_DIM), wide),
                pltpu.VMEM((2, 2 * HEAD_DIM, BLK), wide),
                pltpu.VMEM((2, 1, 2 * BLK), wide),
            ],
        ),
        compiler_params=pltpu.CompilerParams(vmem_limit_bytes=62 * 2**20),
        cost_estimate=pl.CostEstimate(flops=21 * MICROSECOND, bytes_accessed=0, transcendentals=0),
        name="attend_backward",
    )(place, queries, grads, attended, stat, *keys, *values)
    return query_grad, others[:pieces], others[pieces:]


def spread_across(pair, below, count):
    half = count // 2
    across = [(b, half + b if b < half else count - 1 - b) for b in range(count)]
    return lax.ppermute(jnp.where(below, pair[1], pair[0]), CTX, across)


def spread_inside(pair, count):
    half = count // 2
    return lax.ppermute(pair[1], CTX, [(b, half + count - 1 - b) for b in range(half, count)])


def joined_tokens(pair, got, other, below):
    return jnp.concatenate(
        [jnp.where(below, pair[0], got), jnp.where(below, got, other)], axis=0
    )


def spread_tokens(pair, below, count):
    return joined_tokens(pair, spread_across(pair, below, count), spread_inside(pair, count), below)


def send_across(rows, below, count):
    half = count // 2
    across = [(half + b if b < half else count - 1 - b, b) for b in range(count)]
    return lax.ppermute(jnp.where(below, rows[BLK:], rows[:BLK]), CTX, across)


def send_inside(rows, count):
    half = count // 2
    inside = [(half + count - 1 - b, b) for b in range(half, count)]
    return lax.ppermute(rows[BLK:], CTX, inside)


def collect_tokens(rows, got, other, below):
    return jnp.stack([jnp.where(below, rows[:BLK], got), jnp.where(below, got, other)])


def collect_own(rows, below):
    mask = jnp.stack([below, jnp.zeros_like(below)])[:, None, None]
    return mask, jnp.stack([rows[:BLK], rows[:BLK]])


def ring_gather(rows, count):
    half = count // 2
    pieces = [rows]
    for step in range(1, half):
        pairs = [
            (side * half + b, side * half + (b + step) % half)
            for side in range(2)
            for b in range(half)
        ]
        pieces.append(lax.ppermute(rows, CTX, pairs))
    return pieces


def ring_scatter(pieces, count):
    half = count // 2
    arrived = []
    for step in range(1, half):
        pairs = [
            (side * half + b, side * half + (b - step) % half)
            for side in range(2)
            for b in range(half)
        ]
        arrived.append(lax.ppermute(pieces[step], CTX, pairs))
    return arrived


def add_up(members):
    return sum(member.astype(wide) for member in members).astype(low_type)


def ring_position(z):
    return jnp.where(z == 2, 3, jnp.where(z == 3, 2, z))


SWAP = [(0, 1), (1, 0)]
RING = [(z * 2 + x, after * 2 + x) for z, after in enumerate((1, 3, 0, 2)) for x in range(2)]
ACROSS_X = [(d, d ^ 1) for d in range(8)]


def along_z(rows):
    return lax.ppermute(rows, "dp", RING)


def along_x(rows):
    return lax.ppermute(rows, "dp", ACROSS_X)


def along_y(rows):
    return lax.ppermute(rows, "chip", SWAP)


def on_chip(rows):
    return lax.ppermute(rows, "core", SWAP)


def join(*members):
    return jnp.concatenate(members, axis=0)


def by_z(ring, first, rows, position):
    parts = [member[first : first + rows] for member in ring]
    placed = []
    for spot in (0, 1, 3, 2):
        step = lax.rem(position + 4 - spot, 4)
        chosen = parts[3]
        for index in (2, 1, 0):
            chosen = jnp.where(step == index, parts[index], chosen)
        placed.append(chosen)
    return jnp.stack(placed)


def z_halves(ring, position):
    size = ring[0].shape[0] // 2
    return [by_z(ring, part * size, size, position) for part in range(2)]


def cross(halves):
    return [along_x(halves[0]), along_y(halves[1])]


def cross_other(halves):
    return [along_y(halves[0]), along_x(halves[1])]


def paired(halves, crossed):
    return [jnp.stack([halves[part], crossed[part]]) for part in range(2)]


def swapped(members):
    return [on_chip(member) for member in members]


def linked_forward(
    first, second, chosen, tokens, cotangent, sizes, at, below, count, kept, attention_step, output_step, feed_step
):
    position = at[0]

    def gather(rows):
        whole = lax.all_gather(rows, EVERY, axis=0)
        return whole.reshape(4, 2, 2, 2, *rows.shape)

    v = Bag()
    v.f, v.g, v.h = [first[:128]], [second[:128]], [second[128:256]]
    first_feed, second_reduce = gather(first[128:]), gather(second[256:])

    def advance(ring):
        ring.append(along_z(ring[-1]))

    def mix(near, far):
        return near[0], far[0], near[1], far[1]

    def weights_f():
        return mix(v.f_near, v.f_far) + mix(v.f_near_other, v.f_far_other)

    def weights_g():
        return mix(v.g_near, v.g_far) + mix(v.g_near_other, v.g_far_other)

    def weights_h():
        return mix(v.h_near, v.h_far) + mix(v.h_near_other, v.h_far_other)

    for _ in range(3):
        advance(v.f)
    v.tokens = spread_tokens(tokens, below, count)
    v.chosen = chosen
    v = sync(v)
    v.f_half = z_halves(v.f, position)
    del v.f
    v.f_cross = cross(v.f_half)
    v.factors = lax.all_to_all(v.chosen, LANE, split_axis=0, concat_axis=0, tiled=True)
    del v.chosen
    advance(v.g)
    v = sync(v)
    v.f_near = paired(v.f_half, v.f_cross)
    del v.f_half, v.f_cross
    v.f_far = cross_other(v.f_near)
    v.f_near_other = swapped(v.f_near)
    v.factors_other = on_chip(v.factors)
    advance(v.g)
    advance(v.g)
    v = sync(v)
    v.g_half = z_halves(v.g, position)
    del v.g
    v.g_cross = cross(v.g_half)
    v.f_far_other = swapped(v.f_far)
    v.picked = unpack_factors(at, v.factors, v.factors_other, sizes)
    del v.factors, v.factors_other
    advance(v.h)
    v = sync(v)
    v.g_near = paired(v.g_half, v.g_cross)
    del v.g_half, v.g_cross
    v.g_far = cross_other(v.g_near)
    v.g_near_other = swapped(v.g_near)
    advance(v.h)
    advance(v.h)
    v.current = v.tokens
    del v.tokens
    attention_step(v.current, (PIECES, weights_f()), v.picked[0], 0)
    v.middle = output_step(v.current, (PIECES, weights_f()), v.picked[0], 0)
    del v.current
    v.kept = kept
    v = sync(v)
    kept[:] = v.kept
    v.h_half = z_halves(v.h, position)
    del v.h
    v.h_cross = cross(v.h_half)
    v.g_far_other = swapped(v.g_far)
    v.current = feed_step(v.middle, (GATHERED, (first_feed,)), v.picked[0], 0)
    v.kept = kept
    v = sync(v)
    kept[:] = v.kept
    v.h_near = paired(v.h_half, v.h_cross)
    del v.h_half, v.h_cross
    v.h_far = cross_other(v.h_near)
    v.h_near_other = swapped(v.h_near)
    v.cotangent_other = spread_inside(cotangent, count)
    attention_step(v.current, (PIECES, weights_g()), v.picked[1], 1)
    v.middle = output_step(v.current, (PIECES, weights_g()), v.picked[1], 1)
    del v.current
    v.kept = kept
    v = sync(v)
    kept[:] = v.kept
    v.h_far_other = swapped(v.h_far)
    cotangent_got = spread_across(cotangent, below, count)
    frozen = [
        ((PIECES, weights_f()), (GATHERED, (first_feed,))),
        ((PIECES, weights_g()), (MIXED, (*weights_h(), second_reduce))),
    ]
    current = feed_step(v.middle, frozen[1][1], v.picked[1], 1)
    current, cotangent_got = sync((current, cotangent_got))
    cotangent = joined_tokens(cotangent, cotangent_got, v.cotangent_other, below)
    return current, cotangent, v.picked, frozen


SQUARE = (4, 2, 2, 2, 32, 1024)
TALL = (4, 2, 2, 2, 128, 1024)


def square_unit(form, part):
    return part if form == WHOLE else (part // 2, part % 2 * 32)


def expand_unit(form, part):
    return {WHOLE: part, GATHERED: 32 * part}.get(form, (part // 2, part % 2 * 32))


def fetch(form, at_ref, sources, unit, rows, held, arrived, by_quarter=None):
    spread_z = slice(None) if by_quarter is None else by_quarter
    if not isinstance(unit, tuple):
        if form == WHOLE:
            source = sources[unit].at[spread_z]
        else:
            source = sources[-1].at[(spread_z, *[slice(None)] * 3, pl.ds(unit, rows), slice(None))]
        pltpu.make_async_copy(source, held.at[spread_z], arrived).start()
        return
    part, first = unit
    x, y, core = at_ref[1], at_ref[2], at_ref[3]
    for other in range(2):
        for far in range(2):
            source = sources[other * 4 + part * 2 + far]
            for over in range(2):
                over_x, over_y = (over, far) if part == 0 else (far, over)
                pltpu.make_async_copy(
                    source.at[over, spread_z, pl.ds(first, rows), :],
                    held.at[
                        spread_z,
                        lax.rem(x + over_x, 2),
                        lax.rem(y + over_y, 2),
                        lax.rem(core + other, 2),
                    ],
                    arrived,
                ).start()


def wait_for(held, arrived):
    pltpu.make_async_copy(held, held, arrived).wait()


def square(held):
    return held[...].reshape(1024, 1024)


QKV_TILE, OUTPUT_TILE, FEED_TILE, TURN_TILE, QKV_BACK_TILE = 0, 0, 512, 512, 512
STRIP = 64
QKV_ROWS, OUTPUT_ROWS, QKV_BACK_ROWS, FEED_BACK_ROWS = 256, 256, 256, 256
COLUMNS = 1024


def strips(count, body):
    def step(index, carry):
        body(pl.ds(pl.multiple_of(index * STRIP, STRIP), STRIP))
        return carry

    lax.fori_loop(0, count // STRIP, step, 0, unroll=True)


def normalize_rows(values, gain, shift):
    center = jnp.mean(values, axis=-1, keepdims=True)
    spread = values - center
    scale = lax.rsqrt(jnp.mean(spread * spread, axis=-1, keepdims=True) + epsilon)
    unit = spread * scale
    return unit, scale, unit * gain + shift


def normalize_pull(grad, unit, scale, gain):
    scaled = grad * gain
    first = jnp.mean(scaled, axis=-1, keepdims=True)
    second = jnp.mean(scaled * unit, axis=-1, keepdims=True)
    return scale * (scaled - first - unit * second)


def store_norm(values_ref, gain_ref, shift_ref, normed_ref, unit_ref, scale_ref):
    def norm(rows):
        unit, scale, normed = normalize_rows(values_ref[rows, :].astype(wide), gain_ref[...], shift_ref[...])
        normed_ref[rows, :] = normed.astype(low_type)
        unit_ref[rows, :] = unit.astype(low_type)
        scale_ref[rows, :] = jnp.broadcast_to(scale, (STRIP, 128))

    strips(values_ref.shape[0], norm)


def store_pull(out_ref, grad_ref, inner_ref, unit_ref, scale_ref, gain_ref):
    def pull(rows):
        out_ref[rows, :] = grad_ref[rows, :].astype(wide) + normalize_pull(
            inner_ref[rows, :], unit_ref[rows, :].astype(wide), scale_ref[rows, :1], gain_ref[...]
        )

    strips(out_ref.shape[0], pull)


def row_tiles(count, size):
    return [slice(first, first + size) for first in range(0, count, size)]


def span(part):
    return slice(part * COLUMNS, (part + 1) * COLUMNS)


TILED = [False]


def at_first(body):
    if TILED[0]:
        pl.when(pl.program_id(0) == 0)(body)
    else:
        body()


def at_last(body):
    if TILED[0]:
        pl.when(pl.program_id(0) == pl.num_programs(0) - 1)(body)
    else:
        body()


def await_first(held, arrived):
    at_first(lambda: wait_for(held, arrived))


def gather_sum(total, step_value):
    @at_first
    def _():
        total[...] = step_value

    if TILED[0]:

        @pl.when(pl.program_id(0) > 0)
        def _():
            total[...] = total[...] + step_value


def qkv_kernel(form, at_ref, x_ref, gain_ref, shift_ref, left_ref, right_ref, bias_ref, *refs):
    sources, (normed_ref, unit_ref, scale_ref, rank_ref, *outs) = refs[:-9], refs[-9:-2]
    held, arrived = refs[-2:]

    @at_first
    def _():
        for part in range(3):
            fetch(form, at_ref, sources, square_unit(form, part), 32, held.at[part], arrived.at[part])

    store_norm(x_ref, gain_ref, shift_ref, normed_ref, unit_ref, scale_ref)
    rank_ref[...] = times(normed_ref[...], left_ref[...], ROWS_BY_ROWS).astype(low_type)
    for part, out in enumerate(outs):
        await_first(held.at[part], arrived.at[part])
        for rows in row_tiles(out.shape[0], QKV_ROWS):
            out[rows, :] = (
                times(normed_ref[rows, :], square(held.at[part]))
                + times(rank_ref[rows, :], right_ref[:, span(part)])
                + bias_ref[:, span(part)]
            ).astype(low_type)


def output_kernel(form, at_ref, x_ref, attended_ref, left_ref, right_ref, bias_ref, gain_ref, shift_ref, *refs):
    sources, (middle_ref, normed_ref, unit_ref, scale_ref, rank_ref) = refs[:-7], refs[-7:-2]
    held, arrived = refs[-2:]
    at_first(lambda: fetch(form, at_ref, sources, square_unit(form, 3), 32, held, arrived))
    rank_ref[...] = times(attended_ref[...], left_ref[...], ROWS_BY_ROWS).astype(low_type)
    await_first(held, arrived)
    for rows in row_tiles(x_ref.shape[0], OUTPUT_ROWS):
        middle_ref[rows, :] = (
            x_ref[rows, :].astype(wide)
            + times(attended_ref[rows, :], square(held))
            + times(rank_ref[rows, :], right_ref[...])
            + bias_ref[...]
        )
    store_norm(middle_ref, gain_ref, shift_ref, normed_ref, unit_ref, scale_ref)


def fetch_feed_part(form, at_ref, sources, part, expand, reduce, arrived, reduce_first):
    jobs = [
        (expand_unit(form, part), 32, expand.at[part], arrived.at[0, part], None),
        ({WHOLE: 4, GATHERED: 128, MIXED: 0}[form], 128, reduce, arrived.at[1, part], part),
    ]
    for unit, rows, held, semaphore, quarter in jobs[::-1] if reduce_first else jobs:
        fetch(form, at_ref, sources, unit, rows, held, semaphore, quarter)


def fetch_feed_forward(form, at_ref, sources, expand, reduce, arrived, reduce_first):
    for part in range(4):
        fetch_feed_part(form, at_ref, sources, part, expand, reduce, arrived, reduce_first)


def feed_forward_kernel(
    form, at_ref, normed_ref, middle_ref, expand_left_ref, expand_right_ref, expand_bias_ref,
    reduce_left_ref, reduce_right_ref, reduce_bias_ref, *refs,
):
    sources, (result_ref, slope_ref, active_ref, rank_expand_ref, rank_reduce_ref) = refs[:-9], refs[-9:-4]
    expand, reduce, rank_sum, arrived = refs[-4:]
    at_first(lambda: fetch_feed_forward(form, at_ref, sources, expand, reduce, arrived, False))
    rank_expand_ref[...] = times(normed_ref[...], expand_left_ref[...], ROWS_BY_ROWS).astype(low_type)
    result_ref[...] = middle_ref[...] + reduce_bias_ref[...]
    rank_sum[...] = jnp.zeros_like(rank_sum)

    def part_step(part, carry):
        columns = pl.ds(pl.multiple_of(part * COLUMNS, COLUMNS), COLUMNS)
        await_first(expand.at[part], arrived.at[0, part])
        await_first(reduce.at[part], arrived.at[1, part])
        value = (
            times(normed_ref[...], square(expand.at[part]))
            + times(rank_expand_ref[...], expand_right_ref[:, columns])
            + expand_bias_ref[:, columns]
        )
        squared = value * value
        bent = jnp.tanh(value * (root_factor + 0.044715 * root_factor * squared))
        half = 0.5 + 0.5 * bent
        slope_ref[:, columns] = (
            half
            + value * (0.5 - 0.5 * bent * bent) * (root_factor + 3 * 0.044715 * root_factor * squared)
        ).astype(low_type)
        active = (value * half).astype(low_type)
        active_ref[:, columns] = active
        result_ref[...] = result_ref[...] + times(active, square(reduce.at[part]))
        rank_sum[...] = rank_sum[...] + times(active, reduce_left_ref[:, columns], ROWS_BY_ROWS)
        return carry

    lax.fori_loop(0, 4, part_step, 0)
    rank_reduce_ref[...] = rank_sum[...].astype(low_type)
    result_ref[...] = result_ref[...] + times(rank_reduce_ref[...], reduce_right_ref[...])


def feed_output_backward_kernel(
    form, output_form, members, at_ref, grad_ref, normed_ref, unit_ref, scale_ref, rank_expand_ref, rank_reduce_ref,
    attended_ref, rank_output_ref, gain_ref, output_left_ref, output_right_ref, expand_left_ref, expand_right_ref,
    reduce_left_ref, reduce_right_ref, slope_ref, active_ref, *refs,
):
    sources, output_sources, outs, scratch = refs[:members], refs[members:-23], refs[-23:-15], refs[-15:]
    middle_ref, out_ref, output_left_g, output_right_g, expand_left_g, expand_right_g, reduce_left_g, reduce_right_g = outs
    (
        expand, reduce, arrived, held, held_arrived, slope, active, side_arrived,
        low_grad, turned, bent, total, turn_sum, low_middle, output_turned,
    ) = scratch
    for part in range(4):
        for which, (source, kept) in enumerate(((slope_ref, slope), (active_ref, active))):
            pltpu.make_async_copy(
                source.at[:, span(part)], kept.at[part], side_arrived.at[which, part]
            ).start()
        fetch_feed_part(form, at_ref, sources, part, expand, reduce, arrived, True)
    fetch(output_form, at_ref, output_sources, square_unit(output_form, 3), 32, held, held_arrived)
    low_grad[...] = grad_ref[...].astype(low_type)
    turned[...] = times(low_grad[...], reduce_right_ref[...], ROWS_BY_ROWS).astype(low_type)
    reduce_right_g[...] = times(rank_reduce_ref[...], low_grad[...], COLS_BY_COLS).astype(low_type)
    total[...] = jnp.zeros_like(total)
    turn_sum[...] = jnp.zeros_like(turn_sum)

    def part_step(part, carry):
        columns = pl.ds(pl.multiple_of(part * COLUMNS, COLUMNS), COLUMNS)
        wait_for(slope.at[part], side_arrived.at[0, part])
        wait_for(active.at[part], side_arrived.at[1, part])
        wait_for(reduce.at[part], arrived.at[1, part])
        wait_for(expand.at[part], arrived.at[0, part])
        for rows in row_tiles(grad_ref.shape[0], FEED_BACK_ROWS):
            grad_active = times(low_grad[rows, :], square(reduce.at[part]), ROWS_BY_ROWS) + times(
                turned[rows, :], reduce_left_ref[:, columns]
            )
            bent[rows, :] = (grad_active * slope[part, rows, :].astype(wide)).astype(low_type)
            total[rows, :] = total[rows, :] + times(bent[rows, :], square(expand.at[part]), ROWS_BY_ROWS)
        turn_sum[...] = turn_sum[...] + times(bent[...], expand_right_ref[:, columns], ROWS_BY_ROWS)
        reduce_left_g[:, columns] = times(turned[...], active[part], COLS_BY_COLS).astype(low_type)
        expand_right_g[:, columns] = times(rank_expand_ref[...], bent[...], COLS_BY_COLS).astype(low_type)
        return carry

    lax.fori_loop(0, 4, part_step, 0)
    turned[...] = turn_sum[...].astype(low_type)
    expand_left_g[...] = times(turned[...], normed_ref[...], COLS_BY_COLS).astype(low_type)
    total[...] = total[...] + times(turned[...], expand_left_ref[...])
    store_pull(middle_ref, grad_ref, total, unit_ref, scale_ref, gain_ref)
    low_middle[...] = middle_ref[...].astype(low_type)
    output_turned[...] = times(low_middle[...], output_right_ref[...], ROWS_BY_ROWS).astype(low_type)
    output_right_g[...] = times(rank_output_ref[...], low_middle[...], COLS_BY_COLS).astype(low_type)
    output_left_g[...] = times(output_turned[...], attended_ref[...], COLS_BY_COLS).astype(low_type)
    wait_for(held, held_arrived)
    out_ref[...] = (
        times(low_middle[...], square(held), ROWS_BY_ROWS) + times(output_turned[...], output_left_ref[...])
    ).astype(low_type)


def qkv_turn_kernel(pieces, form, at_ref, normed_ref, rank_ref, dq_ref, *refs):
    dk_refs, dv_refs, (right_ref, *refs) = refs[:pieces], refs[pieces : 2 * pieces], refs[2 * pieces :]
    dk_ref, dv_ref, turned_ref, left_g, right_g, left_sum, right_sum = refs
    dk_ref[...] = add_up([member[...] for member in dk_refs])
    dv_ref[...] = add_up([member[...] for member in dv_refs])
    grads = (dq_ref, dk_ref, dv_ref)
    turned = sum(
        times(grads[part][...], right_ref[:, span(part)], ROWS_BY_ROWS) for part in range(3)
    ).astype(low_type)
    turned_ref[...] = turned
    gather_sum(left_sum, times(turned, normed_ref[...], COLS_BY_COLS))
    for part in range(3):
        gather_sum(right_sum.at[part], times(rank_ref[...], grads[part][...], COLS_BY_COLS))

    @at_last
    def _():
        left_g[...] = left_sum[...].astype(low_type)
        for part in range(3):
            right_g[:, span(part)] = right_sum[part].astype(low_type)


def qkv_backward_kernel(
    form, at_ref, grad_ref, unit_ref, scale_ref, turned_ref, dq_ref, dk_ref, dv_ref, gain_ref, left_ref, *refs
):
    sources, (out_ref, low_ref), (held, arrived, total) = refs[:-5], refs[-5:-3], refs[-3:]

    @at_first
    def _():
        for part in range(3):
            fetch(form, at_ref, sources, square_unit(form, part), 32, held.at[part], arrived.at[part])

    total[...] = times(turned_ref[...], left_ref[...])
    for part, member in enumerate((dq_ref, dk_ref, dv_ref)):
        await_first(held.at[part], arrived.at[part])
        for rows in row_tiles(out_ref.shape[0], QKV_BACK_ROWS):
            total[rows, :] = total[rows, :] + times(member[rows, :], square(held.at[part]), ROWS_BY_ROWS)
    store_pull(out_ref, grad_ref, total, unit_ref, scale_ref, gain_ref)
    low_ref[...] = out_ref[...].astype(low_type)


def qkv_whole_kernel(
    pieces, form, at_ref, grad_ref, unit_ref, scale_ref, normed_ref, rank_ref, dq_ref, *refs
):
    dk_refs, dv_refs, (gain_ref, left_ref, right_ref, *refs) = refs[:pieces], refs[pieces : 2 * pieces], refs[2 * pieces :]
    sources, (out_ref, left_g, right_g) = refs[:-9], refs[-9:-6]
    held, arrived, turned, total, dk_ref, dv_ref = refs[-6:]
    for part in range(3):
        fetch(form, at_ref, sources, square_unit(form, part), 32, held.at[part], arrived.at[part])
    dk_ref[...] = add_up([member[...] for member in dk_refs])
    dv_ref[...] = add_up([member[...] for member in dv_refs])
    grads = (dq_ref, dk_ref, dv_ref)
    turned[...] = sum(
        times(grads[part][...], right_ref[:, span(part)], ROWS_BY_ROWS) for part in range(3)
    ).astype(low_type)
    for part in range(3):
        right_g[:, span(part)] = times(rank_ref[...], grads[part][...], COLS_BY_COLS).astype(low_type)
    left_g[...] = times(turned[...], normed_ref[...], COLS_BY_COLS).astype(low_type)
    for part, member in enumerate(grads):
        wait_for(held.at[part], arrived.at[part])
        for rows in row_tiles(out_ref.shape[0], QKV_BACK_ROWS):
            value = times(member[rows, :], square(held.at[part]), ROWS_BY_ROWS)
            before = total[rows, :] if part else times(turned[rows, :], left_ref[...])
            total[rows, :] = before + value
    store_pull(out_ref, grad_ref, total, unit_ref, scale_ref, gain_ref)


def frozen_call(kernel, name, at, weights, tile, tiled, fixed, outs, fixed_outs, scratch, cost):
    form, sources = weights
    count = tiled[0].shape[0]
    TILED[0] = tile > 0

    def by_rows(shape):
        if tile == 0:
            return pl.BlockSpec(memory_space=pltpu.VMEM)
        return pl.BlockSpec((tile, shape[1]), lambda step: (step, 0))

    def every(shape):
        if tile == 0:
            return pl.BlockSpec(memory_space=pltpu.VMEM)
        return pl.BlockSpec(shape, lambda step: (0, 0))

    return pl.pallas_call(
        functools.partial(kernel, form),
        grid=(count // tile,) if tile else (),
        out_shape=tuple(jax.ShapeDtypeStruct(shape, kind) for shape, kind in (*outs, *fixed_outs)),
        in_specs=[pl.BlockSpec(memory_space=pltpu.SMEM)]
        + [by_rows(member.shape) for member in tiled]
        + [every(member.shape) for member in fixed]
        + [pl.BlockSpec(memory_space=pl.ANY)] * len(sources),
        out_specs=tuple(by_rows(shape) for shape, _ in outs) + tuple(every(shape) for shape, _ in fixed_outs),
        scratch_shapes=scratch,
        compiler_params=pltpu.CompilerParams(vmem_limit_bytes=60 * 2**20),
        cost_estimate=pl.CostEstimate(flops=cost * MICROSECOND, bytes_accessed=0, transcendentals=0),
        name=name,
    )(at, *tiled, *fixed, *sources)


def row(vector):
    return vector.reshape(1, -1)


DMA = pltpu.SemaphoreType.DMA


PACKED = ((5, 0), (6, 128), (1, 256), (0, 352), (2, 384), (3, 416), (4, 448), (7, 480))


def unpack_kernel(order, at_ref, own_ref, other_ref, *outs):
    layers, groups = own_ref.shape[1], own_ref.shape[0] // 2
    swapped = at_ref[3] == 1
    for layer_index in range(layers):
        for group in range(groups):
            lanes = []
            for chip in range(2):
                own = own_ref[group * 2 + chip, layer_index]
                other = other_ref[group * 2 + chip, layer_index]
                lanes += [jnp.where(swapped, other, own), jnp.where(swapped, own, other)]
            for kind, first in order:
                out = outs[layer_index * len(order) + kind]
                size = out.shape[1] // (4 * groups)
                out[:, group * 4 * size : (group + 1) * 4 * size] = jnp.concatenate(
                    [lane[:, first : first + size] for lane in lanes], axis=1
                )


def unpack_factors(at, own, other, sizes):
    lanes, layers = own.shape[:2]
    local_spec = pl.BlockSpec(memory_space=pltpu.VMEM)
    found = pl.pallas_call(
        functools.partial(unpack_kernel, PACKED),
        out_shape=tuple(
            jax.ShapeDtypeStruct((RANK, size * lanes * 2), low_type) for _ in range(layers) for size in sizes
        ),
        in_specs=[pl.BlockSpec(memory_space=pltpu.SMEM), local_spec, local_spec],
        out_specs=(local_spec,) * (layers * len(sizes)),
        compiler_params=pltpu.CompilerParams(vmem_limit_bytes=32 * 2**20),
        cost_estimate=pl.CostEstimate(flops=4 * MICROSECOND, bytes_accessed=0, transcendentals=0),
        name="unpack_factors",
    )(at, own, other)
    return [found[layer * len(sizes) : (layer + 1) * len(sizes)] for layer in range(layers)]


def pack_kernel(orders, at_ref, *refs):
    members, out_ref = refs[:-1], refs[-1]
    core, base, offset = at_ref[3], 0, 0
    for order in orders:
        for lane_chip in range(out_ref.shape[1]):
            for owner_core in range(2):
                owner = lane_chip * 2 + owner_core
                parts = []
                for index, _ in enumerate(order):
                    member = members[base + index]
                    size = member.shape[1] // (2 * out_ref.shape[1])
                    parts.append(member[:, owner * size : (owner + 1) * size])
                joined = jnp.concatenate(parts, axis=1)
                out_ref[lax.rem(owner_core + core, 2), lane_chip, :, offset : offset + joined.shape[1]] = joined
        base += len(order)
        offset += joined.shape[1]


def pack_gradients(at, groups, lanes):
    members, width = [], 0
    for order, terms in groups:
        members += [terms[kind] for kind, _ in order]
        width += sum(terms[kind].shape[1] for kind, _ in order) // (2 * lanes)
    local_spec = pl.BlockSpec(memory_space=pltpu.VMEM)
    return pl.pallas_call(
        functools.partial(pack_kernel, [order for order, _ in groups]),
        out_shape=jax.ShapeDtypeStruct((2, lanes, RANK, width), low_type),
        in_specs=[pl.BlockSpec(memory_space=pltpu.SMEM)] + [local_spec] * len(members),
        out_specs=local_spec,
        compiler_params=pltpu.CompilerParams(vmem_limit_bytes=32 * 2**20),
        cost_estimate=pl.CostEstimate(flops=4 * MICROSECOND, bytes_accessed=0, transcendentals=0),
        name="pack_gradients",
    )(at, *members)


LOW, WIDE = low_type, wide


def forward_qkv(current, weights, picked, extras, at):
    rows, columns = current.shape
    full_low = ((rows, columns), LOW)
    bias = jnp.concatenate([extras[0][:columns], jnp.zeros((columns,), WIDE), extras[0][columns:]])
    return frozen_call(
        qkv_kernel, "qkv_forward", at, weights, QKV_TILE, (current,),
        (row(extras[4]), row(extras[5]), picked[0], picked[1], row(bias)),
        (full_low, full_low, ((rows, 128), WIDE), ((rows, RANK), LOW), full_low, full_low, full_low), (),
        [pltpu.VMEM((3, *SQUARE), LOW), DMA((3,))], 9,
    )


def forward_output(current, attended, weights, picked, extras, at):
    rows, columns = current.shape
    full, full_low = ((rows, columns), WIDE), ((rows, columns), LOW)
    return frozen_call(
        output_kernel, "output_forward", at, weights, OUTPUT_TILE, (current, attended),
        (picked[2], picked[3], row(extras[1]), row(extras[6]), row(extras[7])),
        (full, full_low, full_low, ((rows, 128), WIDE), ((rows, RANK), LOW)), (),
        [pltpu.VMEM(SQUARE, LOW), DMA], 8,
    )


def forward_feed(normed, middle, weights, picked, extras, at):
    rows, columns = middle.shape
    tall, ranks = ((rows, picked[5].shape[1]), LOW), ((rows, RANK), LOW)
    return frozen_call(
        feed_forward_kernel, "feed_forward", at, weights, FEED_TILE, (normed, middle),
        (picked[4], picked[5], row(extras[2]), picked[6], picked[7], row(extras[3])),
        (((rows, columns), WIDE), tall, tall, ranks, ranks), (),
        [
            pltpu.VMEM((4, *SQUARE), LOW), pltpu.VMEM(TALL, LOW), pltpu.VMEM((FEED_TILE or rows, RANK), WIDE),
            DMA((2, 4)),
        ], 20,
    )


def like(member):
    return (member.shape, LOW)


def backward_feed_output(grad, kept, weights, output_weights, picked, extras, at):
    rows, columns = grad.shape
    form, sources = weights
    output_form, output_sources = output_weights
    full, full_low, ranks = ((rows, columns), WIDE), ((rows, columns), LOW), ((rows, RANK), LOW)
    tall = ((4, rows, columns), LOW)
    members = (
        grad, kept.normed_two, kept.unit_two, kept.scale_two, kept.rank_expand, kept.rank_reduce,
        kept.attended, kept.rank_output, row(extras[6]), *picked[2:],
    )
    local_spec, anywhere = pl.BlockSpec(memory_space=pltpu.VMEM), pl.BlockSpec(memory_space=pl.ANY)
    outs = (full, full_low, *map(like, picked[2:]))
    return pl.pallas_call(
        functools.partial(feed_output_backward_kernel, form, output_form, len(sources)),
        out_shape=tuple(jax.ShapeDtypeStruct(shape, kind) for shape, kind in outs),
        in_specs=[pl.BlockSpec(memory_space=pltpu.SMEM)]
        + [local_spec] * len(members)
        + [anywhere] * (2 + len(sources) + len(output_sources)),
        out_specs=(local_spec,) * len(outs),
        scratch_shapes=[
            pltpu.VMEM((4, *SQUARE), LOW), pltpu.VMEM(TALL, LOW), DMA((2, 4)), pltpu.VMEM(SQUARE, LOW), DMA,
            pltpu.VMEM(*tall), pltpu.VMEM(*tall), DMA((2, 4)), pltpu.VMEM(*full_low), pltpu.VMEM(*ranks),
            pltpu.VMEM(*full_low), pltpu.VMEM(*full), pltpu.VMEM((rows, RANK), WIDE), pltpu.VMEM(*full_low),
            pltpu.VMEM(*ranks),
        ],
        compiler_params=pltpu.CompilerParams(vmem_limit_bytes=60 * 2**20),
        cost_estimate=pl.CostEstimate(flops=25 * MICROSECOND, bytes_accessed=0, transcendentals=0),
        name="feed_output_backward",
    )(at, *members, kept.slope, kept.active, *sources, *output_sources)


def backward_turn(grads, kept, picked, at):
    query_grad, key_grads, value_grads = grads
    full_low = (query_grad.shape, LOW)
    return frozen_call(
        functools.partial(qkv_turn_kernel, len(key_grads)), "qkv_turn", at, (WHOLE, ()), TURN_TILE,
        (kept.normed_one, kept.rank_attend, query_grad, *key_grads, *value_grads), (picked[1],),
        (full_low, full_low, like(kept.rank_attend)), (like(picked[0]), like(picked[1])),
        [pltpu.VMEM(picked[0].shape, WIDE), pltpu.VMEM((3, *picked[0].shape), WIDE)], 3,
    )


def backward_qkv_whole(grad, grads, kept, weights, picked, extras, at):
    rows, columns = grad.shape
    query_grad, key_grads, value_grads = grads
    return frozen_call(
        functools.partial(qkv_whole_kernel, len(key_grads)), "qkv_whole", at, weights, QKV_BACK_TILE,
        (
            grad, kept.unit_one, kept.scale_one, kept.normed_one, kept.rank_attend, query_grad, *key_grads,
            *value_grads,
        ),
        (row(extras[4]), picked[0], picked[1]),
        (((rows, columns), WIDE),), (like(picked[0]), like(picked[1])),
        [
            pltpu.VMEM((3, *SQUARE), LOW), DMA((3,)), pltpu.VMEM((rows, RANK), LOW),
            pltpu.VMEM((rows, columns), WIDE), pltpu.VMEM((rows, columns), LOW), pltpu.VMEM((rows, columns), LOW),
        ], 11,
    )


def backward_qkv(grad, joined, turned, kept, weights, picked, extras, at):
    rows, columns = grad.shape
    return frozen_call(
        qkv_backward_kernel, "qkv_backward", at, weights, QKV_BACK_TILE,
        (grad, kept.unit_one, kept.scale_one, turned, *joined), (row(extras[4]), picked[0]),
        (((rows, columns), WIDE), ((rows, columns), LOW)), (),
        [pltpu.VMEM((3, *SQUARE), LOW), DMA((3,)), pltpu.VMEM((QKV_BACK_TILE or rows, columns), WIDE)], 9,
    )


def combine_kernel(places, ids_ref, *refs):
    count = len(places)
    received, outs, total = refs[:count], refs[count:-1], refs[-1]
    total[...] = jnp.zeros_like(total)
    for source in range(received[0].shape[0]):
        adapter, spot = ids_ref[source], 0
        for member in received:
            width = member.shape[2]
            at = (adapter, slice(None), slice(spot, spot + width))
            total[at] = total[at] + member[source].astype(wide)
            spot += width
    base = 0
    for member, orders in zip(received, places):
        for layer_index, order in orders:
            for kind, _ in order:
                size = outs[kind].shape[3]
                outs[kind][layer_index] = total[:, :, base : base + size]
                base += size


def combine(ids, received, places, sizes):
    local_spec = pl.BlockSpec(memory_space=pltpu.VMEM)
    width = sum(member.shape[2] for member in received)
    return pl.pallas_call(
        functools.partial(combine_kernel, places),
        out_shape=tuple(jax.ShapeDtypeStruct((LAYERS, ADAPTERS, RANK, size), wide) for size in sizes),
        in_specs=[pl.BlockSpec(memory_space=pltpu.SMEM)] + [local_spec] * len(received),
        out_specs=(local_spec,) * len(sizes),
        scratch_shapes=[pltpu.VMEM((ADAPTERS, RANK, width), wide)],
        compiler_params=pltpu.CompilerParams(vmem_limit_bytes=32 * 2**20),
        cost_estimate=pl.CostEstimate(flops=3 * MICROSECOND, bytes_accessed=0, transcendentals=0),
        name="combine",
    )(ids, *received)


class Bag:
    pass


def open_bag(bag):
    names = tuple(sorted(vars(bag)))
    return tuple(getattr(bag, name) for name in names), names


def close_bag(names, members):
    bag = Bag()
    for name, member in zip(names, members):
        setattr(bag, name, member)
    return bag


jax.tree_util.register_pytree_node(Bag, open_bag, close_bag)


def sync(values):
    leaves, shape = jax.tree.flatten(values)
    return jax.tree.unflatten(shape, lax.optimization_barrier(tuple(leaves)))


def local(
    tokens, cotangent, adapter_ids, attend_weight, output_weight, expand_weight, reduce_weight,
    attend_bias, output_bias, expand_bias, reduce_bias, first_gain, first_shift, second_gain, second_shift,
    *adapters,
):
    data_count, chips = lax.axis_size("dp"), lax.axis_size("chip")
    count = chips * lax.axis_size("core")
    half = count // 2
    devices = data_count * count
    data_rank, core = lax.axis_index("dp"), lax.axis_index("core")
    rank = lax.axis_index("chip") * 2 + core
    below = rank < half
    place = jnp.reshape(lax.rem(rank, half), (1,)).astype(jnp.int32)
    columns = tokens.shape[2]
    linked = (data_count, chips, columns) == (8, 2, 1024)

    lane_chip = jnp.arange(data_count * chips, dtype=jnp.int32)
    lane_sequence = (lane_chip // chips) * 2 + (lane_chip % chips) // (chips // 2)
    lane_adapter = jnp.take(adapter_ids, lane_sequence)

    sizes = [member.shape[2] for member in adapters]
    packed = jnp.concatenate([jnp.swapaxes(adapters[kind], 2, 3) for kind, _ in PACKED], axis=3)
    chosen = jnp.moveaxis(jnp.take(packed, lane_adapter, axis=1), 1, 0)

    def shards(layer_index):
        lists = [attend_weight[layer_index], output_weight[layer_index], expand_weight[layer_index]]
        blocks = [
            member[:, first : first + columns]
            for member in lists
            for first in range(0, member.shape[1], columns)
        ]
        return jnp.concatenate(blocks + [reduce_weight[layer_index]], axis=0)

    extras = [
        tuple(
            member[layer_index]
            for member in (
                attend_bias, output_bias, expand_bias, reduce_bias,
                first_gain, first_shift, second_gain, second_shift,
            )
        )
        for layer_index in range(LAYERS)
    ]
    position = ring_position(data_rank // 2)
    at = jnp.stack([position, data_rank % 2, lax.axis_index("chip"), core]).astype(jnp.int32)
    kept = [Bag(), Bag()]

    def attention_step(current, weights, picked, layer_index):
        keep = kept[layer_index]
        (
            keep.normed_one, keep.unit_one, keep.scale_one, keep.rank_attend,
            keep.queries, keys, values,
        ) = forward_qkv(current, weights, picked, extras[layer_index], at)
        keep.keys, keep.values = ring_gather(keys, count), ring_gather(values, count)
        keep.attended, keep.stat = attend_forward(place, keep.queries, keep.keys, keep.values)

    def output_step(current, weights, picked, layer_index):
        keep = kept[layer_index]
        (
            middle, keep.normed_two, keep.unit_two, keep.scale_two,
            keep.rank_output,
        ) = forward_output(current, keep.attended, weights, picked, extras[layer_index], at)
        return middle

    def feed_step(middle, weights, picked, layer_index):
        keep = kept[layer_index]
        result, keep.slope, keep.active, keep.rank_expand, keep.rank_reduce = forward_feed(
            keep.normed_two, middle, weights, picked, extras[layer_index], at
        )
        return result

    if linked:
        first, second = shards(0), shards(1)
        current, grad_current, picked, frozen = linked_forward(
            first, second, chosen, tokens, cotangent, sizes, at, below, count, kept,
            attention_step, output_step, feed_step,
        )
    else:
        current = spread_tokens(tokens, below, count)
        grad_current = spread_tokens(cotangent, below, count)
        mine = lax.all_to_all(chosen, LANE, split_axis=0, concat_axis=0, tiled=True)
        theirs = lax.ppermute(mine, "core", SWAP)
        both = jnp.stack(
            [jnp.where(core == 0, mine, theirs), jnp.where(core == 0, theirs, mine)], axis=1
        )
        places, spot = {}, 0
        for kind, _ in PACKED:
            places[kind] = spot
            spot += sizes[kind]
        picked = [
            tuple(
                jnp.transpose(
                    both[:, :, layer_index, :, places[kind] : places[kind] + size], (2, 0, 1, 3)
                ).reshape(RANK, devices * size)
                for kind, size in enumerate(sizes)
            )
            for layer_index in range(LAYERS)
        ]
        frozen = []
        for layer_index in range(LAYERS):
            whole = lax.all_gather(shards(layer_index), EVERY, axis=0)
            size = columns // devices
            squares = [whole[:, part * size : (part + 1) * size, :].reshape(SQUARE) for part in range(8)]
            tall = whole[:, 8 * size :, :].reshape(TALL)
            frozen.append(((WHOLE, tuple(squares[:4])), (WHOLE, (*squares[4:], tall))))
            first_weights, second_weights = frozen[layer_index]
            attention_step(current, first_weights, picked[layer_index], layer_index)
            middle = output_step(current, first_weights, picked[layer_index], layer_index)
            current = feed_step(middle, second_weights, picked[layer_index], layer_index)

    result = current.astype(low_type)
    result_got, result_other = send_across(result, below, count), send_inside(result, count)
    lanes = data_count * chips

    def to_owners(groups):
        if linked:
            both = pack_gradients(at, groups, lanes)
            own, sent = both[0], both[1]
        else:
            both = jnp.concatenate(
                [
                    jnp.transpose(
                        terms[kind].reshape(RANK, lanes, 2, sizes[kind]), (2, 1, 0, 3)
                    )
                    for order, terms in groups
                    for kind, _ in order
                ],
                axis=3,
            )
            own, sent = jnp.where(core == 0, both[0], both[1]), jnp.where(core == 0, both[1], both[0])
        total = add_up([own, lax.ppermute(sent, "core", SWAP)])
        return lax.all_to_all(total, LANE, split_axis=0, concat_axis=0, tiled=True)

    terms = [None] * LAYERS
    for layer_index in reversed(range(LAYERS)):
        keep, extra, factors = kept[layer_index], extras[layer_index], picked[layer_index]
        first_weights, second_weights = frozen[layer_index]
        middle_grad, attended_grad, *some_terms = backward_feed_output(
            grad_current, keep, second_weights, first_weights, factors, extra, at
        )
        if layer_index == LAYERS - 1:
            middle_grad, attended_grad, some_terms, result_got = sync(
                (middle_grad, attended_grad, some_terms, result_got)
            )
        query_grad, key_grads, value_grads = attend_backward(
            place, keep.queries, keep.keys, keep.values, attended_grad, keep.attended, keep.stat
        )
        if layer_index == LAYERS - 1:
            query_grad, key_grads, value_grads, result_other = sync(
                (query_grad, key_grads, value_grads, result_other)
            )
        grads = (
            query_grad,
            [key_grads[0], *ring_scatter(key_grads, count)],
            [value_grads[0], *ring_scatter(value_grads, count)],
        )
        if layer_index > 0:
            grad_current, *attend_terms = backward_qkv_whole(
                middle_grad, grads, keep, first_weights, factors, extra, at
            )
            terms[layer_index] = [*attend_terms, *some_terms]
            continue
        key_grad, value_grad, turned, *attend_terms = backward_turn(grads, keep, factors, at)
        terms[layer_index] = [*attend_terms, *some_terms]
        received = to_owners([(PACKED, terms[1]), (PACKED, terms[0])])
        grad_current, low_grad = backward_qkv(
            middle_grad, (query_grad, key_grad, value_grad), turned, keep, first_weights, factors, extra, at
        )
    got, other = send_across(low_grad, below, count), send_inside(low_grad, count)
    received, got, other = sync((received, got, other))
    moved = collect_tokens(low_grad, got, other, below)
    kept_part = collect_own(grad_current, below)
    received = [received]
    places = (((1, PACKED), (0, PACKED)),)
    if linked:
        results = combine(lane_adapter, received, places, sizes)
    else:
        owner_adapter = (lane_adapter[:, None] == jnp.arange(ADAPTERS)[None, :]).astype(wide)
        found = [[None] * len(sizes) for _ in range(LAYERS)]
        for held, orders in zip(received, places):
            summed = jnp.einsum(
                "sa,srp->arp", owner_adapter, held.astype(wide), precision=lax.Precision.HIGHEST
            )
            spot = 0
            for layer_index, order in orders:
                for kind, _ in order:
                    found[layer_index][kind] = summed[:, :, spot : spot + sizes[kind]]
                    spot += sizes[kind]
        results = [
            jnp.stack([found[layer_index][kind] for layer_index in range(LAYERS)])
            for kind in range(len(sizes))
        ]
    return (
        collect_tokens(result, result_got, result_other, below),
        jnp.where(kept_part[0], kept_part[1], moved.astype(wide)),
        *[jnp.swapaxes(member, 2, 3) for member in results],
    )


def solution(mesh):
    count = mesh.shape["ctx"]
    inner = Mesh(mesh.devices.reshape(mesh.shape["dp"], count // 2, 2), EVERY)
    token_spec, factor_spec = P("dp", CTX, None), P(None, None, EVERY, None)
    in_specs = (
        (token_spec,) * 2 + (P(),) + (P(None, EVERY, None),) * 4 + (P(),) * 8 + (factor_spec,) * 8
    )
    out_specs = (token_spec,) * 2 + (factor_spec,) * 8
    return jax.shard_map(local, mesh=inner, in_specs=in_specs, out_specs=out_specs, check_vma=False)
```
